32 devices in a mesh: dp: 4 (over y, x), mp: 8 (over z, core).
Axes of the slice: x: 2, y: 2, z: 4, core: 2. Of those that a mesh axis runs over, the one named last changes fastest.
Arguments:
- hidden_policy: bfloat16 [64, 16, 2048], P('dp', None, 'mp'), may hold values from -6 to 6
- hidden_reference: bfloat16 [64, 16, 2048], P('dp', None, 'mp'), may hold values from -6 to 6
- ffn_gain_policy: float32 [2048], replicated, may hold values from 0.1 to 1.9
- ffn_gain_reference: float32 [2048], replicated, may hold values from 0.1 to 1.9
- up_policy: bfloat16 [2048, 4096], P(None, 'mp'), may hold values from -0.125 to 0.125
- up_reference: bfloat16 [2048, 4096], P(None, 'mp'), may hold values from -0.125 to 0.125
- down_policy: bfloat16 [4096, 2048], P('mp'), may hold values from -0.125 to 0.125
- down_reference: bfloat16 [4096, 2048], P('mp'), may hold values from -0.125 to 0.125
- final_gain_policy: float32 [2048], replicated, may hold values from 0.1 to 1.9
- final_gain_reference: float32 [2048], replicated, may hold values from 0.1 to 1.9
- out_policy: bfloat16 [2048, 7168], P('dp', 'mp'), may hold values from -4 to 4
- out_reference: bfloat16 [2048, 7168], P('dp', 'mp'), may hold values from -4 to 4
- move_plan: int32 [64], replicated, may hold values from 0 to 63, as said below
- lengths: int32 [64], P('dp'), may hold values from 1 to 16, 512 in all
- targets: int32 [64, 16], P('dp'), may hold values from 0 to 7167
Outputs:
- token_diff: float32 [64, 16], P('dp')
- seq_diff: float32 [64], P('dp')
The draws below stay inside these ranges and needn't reach their ends.
Inputs may be any that keep to these rules, and one draw needn't show every extreme that they name: `move_plan`: A permutation of the slots; slot // 16 is the owning index of dp, each owning exactly 16 requests; from one index of dp to one owner go either no requests or exactly 4.
All inputs are finite; a program needn't handle non-finite values. No bound on the sum of `lengths` on one device may be relied on, other than what follows from the above.
Results may differ from the reference program's by a relative error of at most 0.0081.
Values may be sent and summed in bfloat16 or wider, within the bound.
No kernel may reach another device: no remote copies, remote signals or barrier semaphores. Data moves between devices by JAX's collectives and lax.ppermute only.
A program may use at most 64 MiB of HBM per device.

```python
import math
import jax
import jax.numpy as jnp
import numpy as np
from jax import lax

D = 2048
FF = 4096
REQ_DEV = 16
SEQ = 16
VOCAB = 7168
REQS = 64
CAP = 4


def shared_patterns(key):
    base = jax.random.fold_in(key, 909)
    first, second = jax.random.split(base, 2)
    signs = jnp.where(jax.random.bernoulli(first, 0.5, (3, D)), 1.0, -1.0).astype(jnp.float32)
    stride = VOCAB // 6
    shifts = jax.random.randint(second, (6,), 0, stride).astype(jnp.int32)
    columns = jnp.arange(6, dtype=jnp.int32) * stride + shifts
    return (signs, columns)


def hidden_matrix(key, salt):
    base = jax.random.fold_in(key, salt)
    values = jax.random.normal(base, (REQS, SEQ, D), jnp.float32)
    signs, columns = shared_patterns(key)
    request_ids = jnp.arange(REQS, dtype=jnp.int32)
    pattern_index = request_ids // 4 % 3
    aligned = signs[pattern_index] * 3.0
    chosen = request_ids % 4 == 0
    first_row = jnp.where(chosen[:, None], aligned, values[:, 0, :])
    values = values.at[:, 0, :].set(first_row)
    return jnp.clip(values, -6.0, 6.0).astype(jnp.bfloat16)


def draw_hidden_policy(key, part):
    return hidden_matrix(key, 111)


def draw_hidden_reference(key, part):
    return hidden_matrix(key, 222)


def output_matrix(key, salt):
    base = jax.random.fold_in(key, salt)
    first = jax.random.fold_in(base, 0)
    values = jax.random.normal(first, (D, VOCAB), jnp.float32) * (3.0 / math.sqrt(D))
    signs, columns = shared_patterns(key)
    strengths = jnp.array([130.0, 128.0, 180.0, 177.5, 240.0, 238.0], jnp.float32)
    for index in range(6):
        column_values = signs[index // 2] * (strengths[index] / D)
        values = values.at[:, columns[index]].set(column_values)
    return jnp.clip(values, -4.0, 4.0).astype(jnp.bfloat16)


def draw_out_policy(key, part):
    return output_matrix(key, 101)


def draw_out_reference(key, part):
    return output_matrix(key, 202)


def draw_move_plan(key, part):
    base = jax.random.fold_in(key, 303)
    first, second, third = jax.random.split(base, 3)
    device_count = REQS // REQ_DEV
    offset_count = REQ_DEV // CAP
    half_way = device_count // 2
    others = jax.random.permutation(first, device_count - 2).astype(jnp.int32)
    others = others + (others >= 1).astype(jnp.int32)
    others = others + (others >= half_way).astype(jnp.int32)
    offsets = jnp.concatenate([jnp.full((1,), half_way, jnp.int32), jnp.ones((1,), jnp.int32), others[:offset_count - 2]])
    orders = jax.vmap(lambda item: jax.random.permutation(item, REQ_DEV))(jax.random.split(second, device_count))
    arrival = jax.random.permutation(third, REQ_DEV)
    group = orders // CAP
    copy_index = orders % CAP
    source = jnp.arange(device_count, dtype=jnp.int32)[:, None]
    owner = (source + offsets[group]) % device_count
    slot = arrival[group * CAP + copy_index]
    return (owner * REQ_DEV + slot).reshape(REQS).astype(jnp.int32)


def set_ends(entries, own_key, least, high):
    longest = entries.shape.index(max(entries.shape))
    spots = []
    for shift in (0, 1):
        where = [jax.random.randint(jax.random.fold_in(own_key, axis), (), 0, length) for axis, length in enumerate(entries.shape)]
        where[longest] = (where[longest] + shift) % entries.shape[longest]
        spots.append(tuple(where))
    return entries.at[spots[0]].set(least).at[spots[1]].set(high)


def raised(drawn, key, source, target, shards_of, factor):
    def block_of(dim):
        return (jnp.arange(drawn.shape[dim]) // (drawn.shape[dim] // shards_of)).reshape((-1,) + (1,) * (drawn.ndim - 1 - dim))

    first = jax.random.permutation(key, shards_of)[block_of(target)]
    other_side = (block_of(target) + shards_of // 2) % shards_of
    return jnp.where((block_of(source) == first) | (block_of(source) == other_side), factor * drawn, drawn)


def shard_levels(stream_key, dims, cuts, low, top_value):
    loudness, own = 1.0, jax.random.fold_in(stream_key, 6)
    for position, shards_of in cuts:
        steps = jnp.exp(jax.random.uniform(jax.random.fold_in(own, position), (shards_of,), jnp.float32, low / len(cuts), top_value / len(cuts)))
        loudness = loudness * jnp.repeat(steps, dims[position] // shards_of).reshape([-1 if axis == position else 1 for axis in range(len(dims))])
    return loudness


def rank_table(number_of, lean):
    weights = [(1 << 20) // math.isqrt(grade ** lean) + 1 for grade in range(1, number_of + 1)]
    deviation = 1 + sum(weights) // (1 << 30)
    return np.cumsum(np.array([max(1, weight // deviation) for weight in weights]))


def skewed_ids(stream_key, dims, count, slope):
    table = rank_table(count, slope)
    pick = jax.random.randint(jax.random.fold_in(stream_key, 1), dims, 0, int(table[count - 1]))
    standing = jnp.searchsorted(jnp.asarray(table, jnp.int32), pick, side="right")
    return jax.random.permutation(jax.random.fold_in(stream_key, 2), count)[standing].astype(jnp.int32)


def split_up(number_of, total, most, skew):
    portions = [(1 << 20) // math.isqrt(rank ** skew) + 1 for rank in range(2, number_of + 1)]
    rest, given = total - most - (number_of - 1), [1] * (number_of - 1)
    while rest > 0:
        candidates = [i for i in range(number_of - 1) if given[i] < most]
        pool, budget = sum([portions[i] for i in candidates]), rest
        for i in candidates:
            extra = min(most - given[i], max(1, budget * portions[i] // pool), rest)
            given[i] = given[i] + extra
            rest = rest - extra
    return np.array([most] + given)


def uneven_parts(key, count, total, reach, slope):
    if count == 2:
        one = jax.random.randint(key, (), max(1, total - reach), min(reach, total - 1) + 1)
        return jnp.stack([one, total - one])
    sizes = jnp.asarray(split_up(count, total, reach, slope), jnp.int32)
    twos = (count - 1) // 2
    source_of, sink = sizes[1:1 + 2 * twos:2], sizes[2:2 + 2 * twos:2]
    slack = jnp.minimum(source_of - 1, reach - sink)
    passed = jax.random.randint(jax.random.fold_in(key, 1), (twos,), 0, 1 << 20) % (slack + 1)
    sizes = sizes.at[1:1 + 2 * twos:2].set(source_of - passed).at[2:2 + 2 * twos:2].set(sink + passed)
    return sizes[jax.random.permutation(jax.random.fold_in(key, 2), count)]


def gaussian(stream_key, shape, width, reach, shards=(), kind=jnp.bfloat16):
    values = width * jax.random.normal(stream_key, shape, jnp.float32)
    if shards:
        values = values * shard_levels(stream_key, shape, shards, -0.22, 0.18)
    return jnp.clip(values, -reach, reach).astype(kind)


def noise_with(own_key, extent, deviation, bound, pieces, heavy, kind=jnp.bfloat16):
    values = deviation * jax.random.normal(own_key, extent, jnp.float32)
    if pieces:
        values = values * shard_levels(own_key, extent, pieces, -0.22, 0.18)
    return jnp.clip(raised(values, jax.random.fold_in(own_key, 3), *heavy), -bound, bound).astype(kind)


def setup_inputs(seed: int = 0) -> dict:
    key_of = jax.random.split(jax.random.key(seed), 16)
    hidden_policy = draw_hidden_policy(jax.random.fold_in(key_of[15], 71), 0)
    hidden_reference = draw_hidden_reference(jax.random.fold_in(key_of[15], 71), 0)
    ffn_gain_policy = jnp.clip(1.0 + 0.18 * jax.random.normal(key_of[2], (D,), jnp.float32), 0.1, 1.9)
    ffn_gain_reference = jnp.clip(1.0 + 0.18 * jax.random.normal(key_of[3], (D,), jnp.float32), 0.1, 1.9)
    up_policy = gaussian(key_of[4], (D, FF), D ** -0.5, 0.125, ((1, 8),))
    up_reference = gaussian(key_of[5], (D, FF), D ** -0.5, 0.125, ((1, 8),))
    down_policy = noise_with(key_of[6], (FF, D), FF ** -0.5, 0.125, ((0, 8),), (0, 1, 8, 2.0))
    down_reference = noise_with(key_of[7], (FF, D), FF ** -0.5, 0.125, ((0, 8),), (0, 1, 8, 2.0))
    final_gain_policy = jnp.clip(1.0 + 0.18 * jax.random.normal(key_of[8], (D,), jnp.float32), 0.1, 1.9)
    final_gain_reference = jnp.clip(1.0 + 0.18 * jax.random.normal(key_of[9], (D,), jnp.float32), 0.1, 1.9)
    out_policy = draw_out_policy(jax.random.fold_in(key_of[15], 71), 0)
    out_reference = draw_out_reference(jax.random.fold_in(key_of[15], 71), 0)
    move_plan = draw_move_plan(jax.random.fold_in(key_of[15], 71), 0)
    lengths = uneven_parts(key_of[13], REQS, REQS * SEQ // 2, SEQ, 2).astype(jnp.int32)
    targets = set_ends(skewed_ids(key_of[14], (REQS, SEQ), VOCAB, 2), jax.random.fold_in(key_of[14], 3), 0, VOCAB - 1).astype(jnp.int32)
    return {"hidden_policy": hidden_policy, "hidden_reference": hidden_reference, "ffn_gain_policy": ffn_gain_policy, "ffn_gain_reference": ffn_gain_reference, "up_policy": up_policy, "up_reference": up_reference, "down_policy": down_policy, "down_reference": down_reference, "final_gain_policy": final_gain_policy, "final_gain_reference": final_gain_reference, "out_policy": out_policy, "out_reference": out_reference, "move_plan": move_plan, "lengths": lengths, "targets": targets}


epsilon = 1e-05

def layer_norm(values, gain):
    center = lax.optimization_barrier(jnp.mean(values, axis=-1, keepdims=True))
    spread = lax.optimization_barrier(jnp.mean(jnp.square(values - center), axis=-1, keepdims=True))
    return (values - center) * lax.rsqrt(spread + epsilon) * gain

def model_logprob(hidden, move_plan, ffn_gain, up_weight, down_weight, final_gain, out_weight, target_flat):
    moved = jnp.zeros_like(hidden).at[move_plan].set(hidden)
    stream_in = moved.reshape(REQS * SEQ, D)
    normed_in = layer_norm(stream_in.astype(jnp.float32), ffn_gain).astype(jnp.bfloat16)
    pre = jnp.dot(normed_in, up_weight, preferred_element_type=jnp.float32)
    hidden_units = jax.nn.gelu(pre).astype(jnp.bfloat16)
    stream = stream_in.astype(jnp.float32) + jnp.dot(hidden_units, down_weight, preferred_element_type=jnp.float32)
    normed_out = layer_norm(stream, final_gain).astype(jnp.bfloat16)
    block = math.gcd(REQS * SEQ, 512)
    blocks = REQS * SEQ // block

    def score(pair):
        rows, wanted = pair
        logits = jnp.dot(rows, out_weight, preferred_element_type=jnp.float32)
        top = lax.optimization_barrier(jnp.max(logits, axis=1, keepdims=True))
        total = top[:, 0] + jnp.log(lax.optimization_barrier(jnp.sum(jnp.exp(logits - top), axis=1)))
        picked = jnp.take_along_axis(logits, wanted[:, None], axis=1)[:, 0]
        return picked - total
    scored = lax.map(score, (normed_out.reshape(blocks, block, D), target_flat.reshape(blocks, block)))
    return scored.reshape(REQS, SEQ)

def reference(hidden_policy, hidden_reference, ffn_gain_policy, ffn_gain_reference, up_policy, up_reference, down_policy, down_reference, final_gain_policy, final_gain_reference, out_policy, out_reference, move_plan, lengths, targets):
    target_flat = targets.reshape(REQS * SEQ).astype(jnp.int32)
    policy_lp = model_logprob(hidden_policy, move_plan, ffn_gain_policy, up_policy, down_policy, final_gain_policy, out_policy, target_flat)
    reference_lp = model_logprob(hidden_reference, move_plan, ffn_gain_reference, up_reference, down_reference, final_gain_reference, out_reference, target_flat)
    live = jnp.arange(SEQ, dtype=jnp.int32)[None, :] < lengths[:, None]
    token_diff = jnp.where(live, policy_lp - reference_lp, jnp.float32(0.0))
    seq_diff = lax.optimization_barrier(jnp.sum(token_diff, axis=1))
    return (token_diff, seq_diff)
```

```python
import functools

import jax
import jax.numpy as jnp
from jax import lax
from jax.experimental import pallas as pl
from jax.experimental.pallas import tpu as pltpu
from jax.sharding import PartitionSpec as P

epsilon = 1e-05
params = pltpu.CompilerParams(vmem_limit_bytes=32 * 1024 * 1024)
vmem = pl.BlockSpec(memory_space=pltpu.VMEM)
smem = pl.BlockSpec(memory_space=pltpu.SMEM)


def call(kernel, out_shape, ops, scratch=()):
    specs = [smem] + [vmem] * (len(ops) - 1)
    return pl.pallas_call(
        kernel,
        out_shape=out_shape,
        in_specs=specs,
        out_specs=jax.tree.map(lambda _: vmem, out_shape),
        scratch_shapes=list(scratch),
        compiler_params=params,
    )(*ops)


def exchange(values, axis, flip):
    count = lax.axis_size(axis)
    return lax.ppermute(values, axis, [(i, i ^ flip) for i in range(count)])


def select_kernel(ids, code, *refs):
    parts, out = refs[:-1], refs[-1]
    rows = out.shape[0]
    me = ids[0]
    wanted = me * rows + lax.broadcasted_iota(jnp.int32, (rows, code.shape[2]), 0)
    total = None
    for k, part in enumerate(parts):
        hot = (code[me ^ k] == wanted).astype(jnp.float32).astype(jnp.bfloat16)
        found = jnp.dot(hot, part[...], preferred_element_type=jnp.float32)
        total = found if total is None else total + found
    out[...] = total.astype(out.dtype)


def normalise(parts, gain, chip, core, store):
    half = len(parts) // 2
    width = parts[0].shape[1] * len(parts)
    values = [part[...].astype(jnp.float32) for part in parts]
    center = sum(jnp.sum(v, axis=1, keepdims=True) for v in values) / width
    values = [v - center for v in values]
    spread = sum(jnp.sum(v * v, axis=1, keepdims=True) for v in values) / width
    scale = lax.rsqrt(spread + epsilon)
    for k, v in enumerate(values):
        place = 2 * (chip ^ (k % half)) + (core if k < half else 1 - core)
        store[place] = (v * scale * gain[place]).astype(jnp.bfloat16)
    return values[0]


def ffn_kernel(half, ids, gain, up, down, *refs):
    parts = refs[: 2 * half]
    keep, send, normed, terms = refs[2 * half :]
    chip, core = ids[1], ids[2]
    base = normalise(parts, gain, chip, core, normed)
    part = base.shape[1]
    pre = None
    for b in range(2 * half):
        piece = jnp.dot(
            normed[b], up[b * part : (b + 1) * part, :], preferred_element_type=jnp.float32
        )
        pre = piece if pre is None else pre + piece
    units = jax.nn.gelu(pre).astype(jnp.bfloat16)
    full = jnp.dot(units, down[...], preferred_element_type=jnp.float32)
    for b in range(2 * half):
        terms[b] = full[:, b * part : (b + 1) * part]
    for k in range(half):
        place = 2 * (chip ^ k)
        kept = terms[place + core]
        keep[k] = kept + base if k == 0 else kept
        send[k] = terms[place + 1 - core].astype(jnp.bfloat16)


def pair_kernel(ids, keep, came, own, *outs):
    own[...] = keep[0] + came[0].astype(jnp.float32)
    for k, out in enumerate(outs):
        out[...] = (keep[k + 1] + came[k + 1].astype(jnp.float32)).astype(jnp.bfloat16)


def score_kernel(half, ids, gain, out_full, wanted, *refs):
    parts = refs[: 2 * half]
    stats, normed = refs[2 * half :]
    chip, core = ids[1], ids[2]
    normalise(parts, gain, chip, core, normed)
    part = parts[0].shape[1]
    logits = None
    for b in range(2 * half):
        piece = jnp.dot(
            normed[b], out_full[b * part : (b + 1) * part, :], preferred_element_type=jnp.float32
        )
        logits = piece if logits is None else logits + piece
    entries = lax.broadcasted_iota(jnp.int32, logits.shape, 1) + ids[3] * logits.shape[1]
    picked = jnp.sum(jnp.where(entries == wanted[...], logits, 0.0), axis=1, keepdims=True)
    top = jnp.max(logits, axis=1, keepdims=True)
    total = jnp.sum(jnp.exp(logits - top), axis=1, keepdims=True)
    lane = lax.broadcasted_iota(jnp.int32, (logits.shape[0], 128), 1)
    table = jnp.where(lane == 0, top, jnp.where(lane == 1, total, picked))
    stats[...] = jnp.transpose(table)[:8]


def gather_pair(own, half):
    same = [own] + [exchange(own, "mp", 2 * k) for k in range(1, half)]
    other = [exchange(v, "mp", 1) for v in same]
    return same + other


def local(
    hidden_policy,
    hidden_reference,
    ffn_gain_policy,
    ffn_gain_reference,
    up_policy,
    up_reference,
    down_policy,
    down_reference,
    final_gain_policy,
    final_gain_reference,
    out_policy,
    out_reference,
    move_plan,
    lengths,
    targets,
):
    dp = lax.axis_size("dp")
    mp = lax.axis_size("mp")
    half = mp // 2
    dp_index = lax.axis_index("dp")
    mp_index = lax.axis_index("mp")
    ids = jnp.stack([dp_index, mp_index // 2, mp_index % 2, mp_index]).astype(jnp.int32)
    reqs, slots, part = hidden_policy.shape
    here = reqs * slots
    rows = here // 2
    hiddens = (hidden_policy.reshape(here, part), hidden_reference.reshape(here, part))
    ffn_gains = (ffn_gain_policy.reshape(mp, 1, part), ffn_gain_reference.reshape(mp, 1, part))
    final_gains = (
        final_gain_policy.reshape(mp, 1, part),
        final_gain_reference.reshape(mp, 1, part),
    )
    ups, downs, outs = (
        (up_policy, up_reference),
        (down_policy, down_reference),
        (out_policy, out_reference),
    )

    facts = jnp.concatenate([lengths, targets.reshape(here)])
    relative = jnp.stack([facts] + [exchange(facts, "dp", k) for k in range(1, dp)])
    order = jnp.arange(dp, dtype=jnp.int32)
    place = (order[:, None] ^ dp_index) == order[None, :]
    facts = jnp.sum(jnp.where(place[:, :, None], relative[None], 0), axis=1)
    all_lengths = facts[:, :reqs].reshape(-1)
    all_targets = facts[:, reqs:].reshape(-1)
    slot_ids = jnp.arange(dp * reqs, dtype=jnp.int32)
    positions = jnp.arange(slots, dtype=jnp.int32)

    def codes(slot):
        start = jnp.sum(jnp.where(slot_ids[None] < slot[:, None], all_lengths[None], 0), axis=1)
        live = jnp.sum(jnp.where(slot_ids[None] == slot[:, None], all_lengths[None], 0), axis=1)
        return jnp.where(
            positions[None] < live[:, None], start[:, None] + positions[None], jnp.int32(-1)
        )

    source_code = codes(move_plan).reshape(dp, 1, here)
    owner_code = codes(slot_ids).reshape(-1)
    my_ranks = dp_index * rows + jnp.arange(rows, dtype=jnp.int32)
    wanted = jnp.sum(
        jnp.where(owner_code[None] == my_ranks[:, None], all_targets[None], 0),
        axis=1,
        keepdims=True,
    )

    block = jax.ShapeDtypeStruct((rows, part), jnp.bfloat16)
    moved = []
    for hidden in hiddens:
        parts = [hidden] + [exchange(hidden, "dp", k) for k in range(1, dp)]
        moved.append(call(select_kernel, block, (ids, source_code, *parts)))
    moved = lax.optimization_barrier((*moved, *outs))
    moved, outs = moved[:2], moved[2:]
    outs = [lax.all_gather(out, "dp", axis=0, tiled=True) for out in outs]

    normed_scratch = pltpu.VMEM((mp, rows, part), jnp.bfloat16)
    streams = []
    for m in range(2):
        parts = gather_pair(moved[m], half)
        keep, send = call(
            functools.partial(ffn_kernel, half),
            (
                jax.ShapeDtypeStruct((half, rows, part), jnp.float32),
                jax.ShapeDtypeStruct((half, rows, part), jnp.bfloat16),
            ),
            (ids, ffn_gains[m], ups[m], downs[m], *parts),
            [normed_scratch, pltpu.VMEM((mp, rows, part), jnp.float32)],
        )
        came = exchange(send, "mp", 1)
        own, *pieces = call(
            pair_kernel,
            (jax.ShapeDtypeStruct((rows, part), jnp.float32),) + (block,) * (half - 1),
            (ids, keep, came),
        )
        for k, piece in enumerate(pieces):
            own = own + exchange(piece, "mp", 2 * (k + 1)).astype(jnp.float32)
        streams.append(own.astype(jnp.bfloat16))

    stats = []
    for m in range(2):
        parts = gather_pair(streams[m], half)
        stats.append(
            call(
                functools.partial(score_kernel, half),
                jax.ShapeDtypeStruct((8, rows), jnp.float32),
                (ids, final_gains[m], outs[m], wanted, *parts),
                [normed_scratch],
            )
        )
    mine = jnp.stack([s[:3] for s in stats])
    mine = jnp.stack([mine] + [exchange(mine, "mp", k) for k in range(1, mp)])
    top = jnp.max(mine[:, :, 0], axis=0)
    total = jnp.sum(mine[:, :, 1] * jnp.exp(mine[:, :, 0] - top[None]), axis=0)
    logprob = jnp.sum(mine[:, :, 2], axis=0) - (top + jnp.log(total))
    diff = logprob[0] - logprob[1]
    relative = jnp.stack([diff] + [exchange(diff, "dp", k) for k in range(1, dp)])
    ranks = (order ^ dp_index)[:, None] * rows + jnp.arange(rows, dtype=jnp.int32)[None]
    my_code = codes(dp_index * reqs + jnp.arange(reqs, dtype=jnp.int32))
    hit = my_code[:, :, None] == ranks.reshape(1, 1, -1)
    token_diff = jnp.sum(jnp.where(hit, relative.reshape(1, 1, -1), 0.0), axis=2)
    return (token_diff, jnp.sum(token_diff, axis=1))


def solution(mesh):
    return jax.shard_map(
        local,
        mesh=mesh,
        in_specs=(
            P("dp", None, "mp"),
            P("dp", None, "mp"),
            P(),
            P(),
            P(None, "mp"),
            P(None, "mp"),
            P("mp", None),
            P("mp", None),
            P(),
            P(),
            P("dp", "mp"),
            P("dp", "mp"),
            P(),
            P("dp"),
            P("dp", None),
        ),
        out_specs=(P("dp", None), P("dp")),
        check_vma=False,
    )
```

```python
import functools

import jax
import jax.numpy as jnp
from jax import lax
from jax.experimental import pallas as pl
from jax.experimental.pallas import tpu as pltpu
from jax.sharding import PartitionSpec as P

epsilon = 1e-05
params = pltpu.CompilerParams(vmem_limit_bytes=24 * 1024 * 1024)
vmem = pl.BlockSpec(memory_space=pltpu.VMEM)
smem = pl.BlockSpec(memory_space=pltpu.SMEM)


def call(kernel, out_shape, ops, scratch=()):
    specs = [smem] + [vmem] * (len(ops) - 1)
    return pl.pallas_call(
        kernel,
        out_shape=out_shape,
        in_specs=specs,
        out_specs=jax.tree.map(lambda _: vmem, out_shape),
        scratch_shapes=list(scratch),
        compiler_params=params,
    )(*ops)


def exchange(values, axis, flip):
    count = lax.axis_size(axis)
    return lax.ppermute(values, axis, [(i, i ^ flip) for i in range(count)])


def select_kernel(ids, code, *refs):
    parts, out = refs[:-1], refs[-1]
    rows = out.shape[1]
    dp = len(parts) // 2
    me = ids[0]
    wanted = me * rows + lax.broadcasted_iota(jnp.int32, (rows, code.shape[2]), 0)
    hots = [
        (code[me ^ k] == wanted).astype(jnp.float32).astype(jnp.bfloat16) for k in range(dp)
    ]
    for m in range(2):
        total = None
        for k in range(dp):
            values = parts[m * dp + k][...]
            values = values.reshape(-1, values.shape[-1])
            found = jnp.dot(hots[k], values, preferred_element_type=jnp.float32)
            total = found if total is None else total + found
        out[m] = total.astype(out.dtype)


def normalise(values, gain, chip, core, store):
    half = len(values) // 2
    width = values[0].shape[1] * len(values)
    values = [v.astype(jnp.float32) for v in values]
    center = sum(jnp.sum(v, axis=1, keepdims=True) for v in values) / width
    values = [v - center for v in values]
    spread = sum(jnp.sum(v * v, axis=1, keepdims=True) for v in values) / width
    scale = lax.rsqrt(spread + epsilon)
    for k, v in enumerate(values):
        place = 2 * (chip ^ (k % half)) + (core if k < half else 1 - core)
        store[place] = (v * scale * gain[place]).astype(jnp.bfloat16)
    return values[0]


def ffn_kernel(half, ids, *refs):
    gains, ups, downs = refs[:2], refs[2:4], refs[4:6]
    parts = refs[6 : 6 + 2 * half]
    keep, send, normed, terms = refs[6 + 2 * half :]
    chip, core = ids[1], ids[2]
    for m in range(2):
        up, down = ups[m], downs[m]
        base = normalise([part[m] for part in parts], gains[m], chip, core, normed.at[m])
        part = base.shape[1]
        pre = None
        for b in range(2 * half):
            piece = jnp.dot(
                normed[m, b], up[b * part : (b + 1) * part, :], preferred_element_type=jnp.float32
            )
            pre = piece if pre is None else pre + piece
        units = jax.nn.gelu(pre).astype(jnp.bfloat16)
        full = jnp.dot(units, down[...], preferred_element_type=jnp.float32)
        for b in range(2 * half):
            terms[m, b] = full[:, b * part : (b + 1) * part]
        for k in range(half):
            place = 2 * (chip ^ k)
            kept = terms[m, place + core]
            keep[k, m] = kept + base if k == 0 else kept
            send[k, m] = terms[m, place + 1 - core].astype(jnp.bfloat16)


def pair_kernel(ids, keep, came, own, *outs):
    own[...] = keep[0] + came[0].astype(jnp.float32)
    for k, out in enumerate(outs):
        out[...] = (keep[k + 1] + came[k + 1].astype(jnp.float32)).astype(jnp.bfloat16)


def score_kernel(half, ids, wanted, *refs):
    gains, refs = refs[:2], refs[2:]
    parts, refs = refs[: 2 * half], refs[2 * half :]
    outs, (stats, normed) = refs[:-2], refs[-2:]
    dp = len(outs) // 2
    me, chip, core = ids[0], ids[1], ids[2]
    lane = lax.broadcasted_iota(jnp.int32, (parts[0].shape[1], 128), 1)
    table = jnp.zeros(lane.shape, jnp.float32)
    ratio = 2 * half // dp
    for m in range(2):
        normalise([part[m] for part in parts], gains[m], chip, core, normed.at[m])
        part = parts[0].shape[2]
        logits = None
        for k in range(dp):
            for b in range(ratio):
                piece = jnp.dot(
                    normed[m, (me ^ k) * ratio + b],
                    outs[m * dp + k][b * part : (b + 1) * part, :],
                    preferred_element_type=jnp.float32,
                )
                logits = piece if logits is None else logits + piece
        entries = lax.broadcasted_iota(jnp.int32, logits.shape, 1) + ids[3] * logits.shape[1]
        picked = jnp.sum(jnp.where(entries == wanted[...], logits, 0.0), axis=1, keepdims=True)
        top = jnp.max(logits, axis=1, keepdims=True)
        total = jnp.sum(jnp.exp(logits - top), axis=1, keepdims=True)
        table = jnp.where(lane == m, top, table)
        table = jnp.where(lane == 2 + m, total, table)
        table = jnp.where(lane == 4 + m, picked, table)
    stats[...] = jnp.transpose(table)[:8]


def merge(ids, mine, came):
    top = jnp.maximum(mine[0:2], came[0:2])
    total = mine[2:4] * jnp.exp(mine[0:2] - top) + came[2:4] * jnp.exp(came[0:2] - top)
    return top, total, mine[4:6] + came[4:6]


def merge_kernel(ids, mine, came, out):
    out[0:2], out[2:4], out[4:6] = merge(ids, mine, came)
    out[6:8] = jnp.zeros((2, out.shape[1]), jnp.float32)


def last_kernel(ids, mine, came, out):
    top, total, picked = merge(ids, mine, came)
    logprob = picked - (top + jnp.log(total))
    out[...] = logprob[0:1] - logprob[1:2]


def local(
    hidden_policy,
    hidden_reference,
    ffn_gain_policy,
    ffn_gain_reference,
    up_policy,
    up_reference,
    down_policy,
    down_reference,
    final_gain_policy,
    final_gain_reference,
    out_policy,
    out_reference,
    move_plan,
    lengths,
    targets,
):
    dp = lax.axis_size("dp")
    mp = lax.axis_size("mp")
    half = mp // 2
    dp_index = lax.axis_index("dp")
    mp_index = lax.axis_index("mp")
    ids = jnp.stack([dp_index, mp_index // 2, mp_index % 2, mp_index]).astype(jnp.int32)
    reqs, slots, part = hidden_policy.shape
    here = reqs * slots
    rows = here // 2
    ffn_gains = (ffn_gain_policy.reshape(mp, 1, part), ffn_gain_reference.reshape(mp, 1, part))
    final_gains = (
        final_gain_policy.reshape(mp, 1, part),
        final_gain_reference.reshape(mp, 1, part),
    )
    bits = [1 << b for b in range(dp.bit_length() - 1)]

    hidden_parts = []
    for hidden in (hidden_policy, hidden_reference):
        hidden_parts += [hidden] + [exchange(hidden, "dp", k) for k in range(1, dp)]
    facts = jnp.concatenate([lengths, targets.reshape(here)])
    relative = jnp.stack([facts] + [exchange(facts, "dp", k) for k in range(1, dp)])
    order = jnp.arange(dp, dtype=jnp.int32)
    place = (order[:, None] ^ dp_index) == order[None, :]
    facts = jnp.sum(jnp.where(place[:, :, None], relative[None], 0), axis=1)
    all_lengths = facts[:, :reqs].reshape(-1)
    all_targets = facts[:, reqs:].reshape(-1)
    slot_ids = jnp.arange(dp * reqs, dtype=jnp.int32)
    positions = jnp.arange(slots, dtype=jnp.int32)

    def codes(slot):
        start = jnp.sum(jnp.where(slot_ids[None] < slot[:, None], all_lengths[None], 0), axis=1)
        live = jnp.sum(jnp.where(slot_ids[None] == slot[:, None], all_lengths[None], 0), axis=1)
        return jnp.where(
            positions[None] < live[:, None], start[:, None] + positions[None], jnp.int32(-1)
        )

    bit_orders = []
    for m in range(2):
        bit_orders.append([bits[(b ^ m) if (b ^ m) < len(bits) else b] for b in range(len(bits))])
    outs = [{0: out_policy}, {0: out_reference}]
    newest = [{0: -1}, {0: -1}]

    def forward(after):
        flat = [outs[m][k] for m in range(2) for k in newest[m]]
        after, *flat = lax.optimization_barrier((after, *flat))
        sent = []
        for m in range(2):
            for k, step in newest[m].items():
                outs[m][k] = flat.pop(0)
                sent += [(m, k, later) for later in range(step + 1, len(bits))]
            newest[m] = {}
        for m, k, step in sorted(sent, key=lambda item: item[2]):
            place = k ^ bit_orders[m][step]
            outs[m][place] = exchange(outs[m][k], "dp", bit_orders[m][step])
            newest[m][place] = step
        return after

    source_code = forward(codes(move_plan).reshape(dp, 1, here))
    moved = call(
        select_kernel,
        jax.ShapeDtypeStruct((2, rows, part), jnp.bfloat16),
        (ids, source_code, *hidden_parts),
    )

    far = sorted(range(1, half), key=lambda k: (k.bit_length() <= 1, k))

    def gather_pair(own):
        same = {0: own}
        for k in far:
            same[k] = exchange(own, "mp", 2 * k)
        same = [same[k] for k in range(half)]
        return same + [exchange(v, "mp", 1) for v in same]

    normed_scratch = pltpu.VMEM((2, mp, rows, part), jnp.bfloat16)
    block = jax.ShapeDtypeStruct((2, rows, part), jnp.bfloat16)
    keep, send = call(
        functools.partial(ffn_kernel, half),
        (
            jax.ShapeDtypeStruct((half, 2, rows, part), jnp.float32),
            jax.ShapeDtypeStruct((half, 2, rows, part), jnp.bfloat16),
        ),
        (
            ids,
            *ffn_gains,
            up_policy,
            up_reference,
            down_policy,
            down_reference,
            *gather_pair(moved),
        ),
        [normed_scratch, pltpu.VMEM((2, mp, rows, part), jnp.float32)],
    )
    came = exchange(send, "mp", 1)
    own, *pieces = call(
        pair_kernel,
        (jax.ShapeDtypeStruct((2, rows, part), jnp.float32),) + (block,) * (half - 1),
        (ids, keep, came),
    )
    arrived = {k: exchange(pieces[k - 1], "mp", 2 * k) for k in far}
    for k in range(1, half):
        own = own + arrived[k].astype(jnp.float32)
    stream = own.astype(jnp.bfloat16)
    for step in range(1, len(bits)):
        stream = forward(stream)

    owner_code = codes(slot_ids).reshape(-1)
    my_ranks = dp_index * rows + jnp.arange(rows, dtype=jnp.int32)
    wanted = jnp.sum(
        jnp.where(owner_code[None] == my_ranks[:, None], all_targets[None], 0),
        axis=1,
        keepdims=True,
    )
    stats = call(
        functools.partial(score_kernel, half),
        jax.ShapeDtypeStruct((8, rows), jnp.float32),
        (
            ids,
            wanted,
            *final_gains,
            *gather_pair(stream),
            *[outs[m][k] for m in range(2) for k in range(dp)],
        ),
        [normed_scratch],
    )
    flips = [1 << b for b in range(mp.bit_length() - 1)]
    for flip in flips[:-1]:
        stats = call(
            merge_kernel,
            jax.ShapeDtypeStruct((8, rows), jnp.float32),
            (ids, stats, exchange(stats, "mp", flip)),
        )
    diff = call(
        last_kernel,
        jax.ShapeDtypeStruct((1, rows), jnp.float32),
        (ids, stats, exchange(stats, "mp", flips[-1])),
    )
    for bit in bits:
        diff = jnp.concatenate([diff, exchange(diff, "dp", bit)])
    ranks = (order ^ dp_index)[:, None] * rows + jnp.arange(rows, dtype=jnp.int32)[None]
    my_code = codes(dp_index * reqs + jnp.arange(reqs, dtype=jnp.int32))
    hit = my_code[:, :, None] == ranks.reshape(1, 1, -1)
    token_diff = jnp.sum(jnp.where(hit, diff.reshape(1, 1, -1), 0.0), axis=2)
    return (token_diff, jnp.sum(token_diff, axis=1))


def solution(mesh):
    return jax.shard_map(
        local,
        mesh=mesh,
        in_specs=(
            P("dp", None, "mp"),
            P("dp", None, "mp"),
            P(),
            P(),
            P(None, "mp"),
            P(None, "mp"),
            P("mp", None),
            P("mp", None),
            P(),
            P(),
            P("dp", "mp"),
            P("dp", "mp"),
            P(),
            P("dp"),
            P("dp", None),
        ),
        out_specs=(P("dp", None), P("dp")),
        check_vma=False,
    )
```

```python
import functools

import jax
import jax.numpy as jnp
from jax import lax
from jax.experimental import pallas as pl
from jax.experimental.pallas import tpu as pltpu
from jax.sharding import PartitionSpec as P

epsilon = 1e-05
params = pltpu.CompilerParams(vmem_limit_bytes=24 * 1024 * 1024)
vmem = pl.BlockSpec(memory_space=pltpu.VMEM)
smem = pl.BlockSpec(memory_space=pltpu.SMEM)
anywhere = pl.BlockSpec(memory_space=pltpu.HBM)


def call(kernel, out_shape, ops, scratch=(), far=()):
    specs = [smem] + [anywhere if i in far else vmem for i in range(1, len(ops))]
    ops = [
        pltpu.with_memory_space_constraint(op, pltpu.HBM) if i in far else op
        for i, op in enumerate(ops)
    ]
    return pl.pallas_call(
        kernel,
        out_shape=out_shape,
        in_specs=specs,
        out_specs=jax.tree.map(lambda _: vmem, out_shape),
        scratch_shapes=list(scratch),
        compiler_params=params,
    )(*ops)


def exchange(values, axis, flip):
    count = lax.axis_size(axis)
    return lax.ppermute(values, axis, [(i, i ^ flip) for i in range(count)])


def fetch(sources, targets, sems):
    copies = [
        pltpu.make_async_copy(source, target, sems.at[i])
        for i, (source, target) in enumerate(zip(sources, targets))
    ]
    for copy in copies:
        copy.start()
    return copies


def select_kernel(dp, ids, code, *refs):
    parts, (out, own, sems) = list(refs[: 2 * dp]), refs[2 * dp :]
    copies = fetch([parts[0], parts[dp]], [own.at[0], own.at[1]], sems)
    rows = out.shape[1]
    me = ids[0]
    wanted = me * rows + lax.broadcasted_iota(jnp.int32, (rows, code.shape[2]), 0)
    hots = [
        (code[me ^ k] == wanted).astype(jnp.float32).astype(jnp.bfloat16) for k in range(dp)
    ]
    for m in range(2):
        copies[m].wait()
        parts[m * dp] = own.at[m]
    for m in range(2):
        total = None
        for k in range(dp):
            values = parts[m * dp + k][...]
            values = values.reshape(-1, values.shape[-1])
            found = jnp.dot(hots[k], values, preferred_element_type=jnp.float32)
            total = found if total is None else total + found
        out[m] = total.astype(out.dtype)


def normalise(values, gain, chip, core, scaled, normed):
    half = len(values) // 2
    part = values[0].shape[1]
    width = part * len(values)
    values = [v.astype(jnp.float32) for v in values]
    center = sum(jnp.sum(v, axis=1, keepdims=True) for v in values) / width
    values = [v - center for v in values]
    spread = sum(jnp.sum(v * v, axis=1, keepdims=True) for v in values) / width
    scale = lax.rsqrt(spread + epsilon)
    for k, v in enumerate(values):
        scaled[2 * (chip ^ (k % half)) + (core if k < half else 1 - core)] = v * scale
    for b in range(2 * half):
        normed[b] = (scaled[b] * gain[:, b * part : (b + 1) * part]).astype(jnp.bfloat16)
    return values[0]


def ffn_kernel(half, ids, *refs):
    parts = refs[6 : 6 + 2 * half]
    keep, send, gains, scaled, normed, up_store, down_store, sems = refs[6 + 2 * half :]
    copies = fetch(
        [refs[0], refs[2], refs[4], refs[1], refs[3], refs[5]],
        [store.at[m] for m in range(2) for store in (gains, up_store, down_store)],
        sems,
    )
    chip, core = ids[1], ids[2]
    for m in range(2):
        copies[3 * m].wait()
        base = normalise([part[m] for part in parts], gains[m], chip, core, scaled, normed)
        part = base.shape[1]
        copies[3 * m + 1].wait()
        pre = None
        for b in range(2 * half):
            piece = jnp.dot(
                normed[b],
                up_store[m, b * part : (b + 1) * part, :],
                preferred_element_type=jnp.float32,
            )
            pre = piece if pre is None else pre + piece
        units = jax.nn.gelu(pre).astype(jnp.bfloat16)
        copies[3 * m + 2].wait()
        full = jnp.dot(units, down_store[m], preferred_element_type=jnp.float32)
        for b in range(2 * half):
            scaled[b] = full[:, b * part : (b + 1) * part]
        for k in range(half):
            place = 2 * (chip ^ k)
            kept = scaled[place + core]
            keep[k, m] = kept + base if k == 0 else kept
            send[k, m] = scaled[place + 1 - core].astype(jnp.bfloat16)


def pair_kernel(ids, keep, came, own, *outs):
    own[...] = keep[0] + came[0].astype(jnp.float32)
    for k, out in enumerate(outs):
        out[...] = (keep[k + 1] + came[k + 1].astype(jnp.float32)).astype(jnp.bfloat16)


def score_kernel(half, ids, wanted, *refs):
    parts = refs[2 : 2 + 2 * half]
    *outs, stats, gains, scaled, normed, out_store, sems = refs[2 + 2 * half :]
    dp = len(outs) // 2
    copies = fetch(
        [refs[0], outs[0], refs[1], outs[dp]],
        [store.at[m] for m in range(2) for store in (gains, out_store)],
        sems,
    )
    me, chip, core = ids[0], ids[1], ids[2]
    lane = lax.broadcasted_iota(jnp.int32, (parts[0].shape[1], 128), 1)
    table = jnp.zeros(lane.shape, jnp.float32)
    ratio = 2 * half // dp
    for m in range(2):
        copies[2 * m].wait()
        normalise([part[m] for part in parts], gains[m], chip, core, scaled, normed)
        part = parts[0].shape[2]
        copies[2 * m + 1].wait()
        outs[m * dp] = out_store.at[m]
        logits = None
        for k in range(dp):
            for b in range(ratio):
                piece = jnp.dot(
                    normed[(me ^ k) * ratio + b],
                    outs[m * dp + k][b * part : (b + 1) * part, :],
                    preferred_element_type=jnp.float32,
                )
                logits = piece if logits is None else logits + piece
        entries = lax.broadcasted_iota(jnp.int32, logits.shape, 1) + ids[3] * logits.shape[1]
        picked = jnp.sum(jnp.where(entries == wanted[...], logits, 0.0), axis=1, keepdims=True)
        top = jnp.max(logits, axis=1, keepdims=True)
        total = jnp.sum(jnp.exp(logits - top), axis=1, keepdims=True)
        table = jnp.where(lane == m, top, table)
        table = jnp.where(lane == 2 + m, total, table)
        table = jnp.where(lane == 4 + m, picked, table)
    stats[...] = jnp.transpose(table)[:8]


def merge(ids, mine, came):
    top = jnp.maximum(mine[0:2], came[0:2])
    total = mine[2:4] * jnp.exp(mine[0:2] - top) + came[2:4] * jnp.exp(came[0:2] - top)
    return top, total, mine[4:6] + came[4:6]


def merge_kernel(ids, mine, came, out):
    out[0:2], out[2:4], out[4:6] = merge(ids, mine, came)
    out[6:8] = jnp.zeros((2, out.shape[1]), jnp.float32)


def last_kernel(ids, mine, came, out):
    top, total, picked = merge(ids, mine, came)
    logprob = picked - (top + jnp.log(total))
    out[...] = logprob[0:1] - logprob[1:2]


def local(
    hidden_policy,
    hidden_reference,
    ffn_gain_policy,
    ffn_gain_reference,
    up_policy,
    up_reference,
    down_policy,
    down_reference,
    final_gain_policy,
    final_gain_reference,
    out_policy,
    out_reference,
    move_plan,
    lengths,
    targets,
):
    dp = lax.axis_size("dp")
    mp = lax.axis_size("mp")
    half = mp // 2
    dp_index = lax.axis_index("dp")
    mp_index = lax.axis_index("mp")
    ids = jnp.stack([dp_index, mp_index // 2, mp_index % 2, mp_index]).astype(jnp.int32)
    reqs, slots, part = hidden_policy.shape
    here = reqs * slots
    rows = here // 2
    ffn_gains = (ffn_gain_policy.reshape(1, -1), ffn_gain_reference.reshape(1, -1))
    final_gains = (final_gain_policy.reshape(1, -1), final_gain_reference.reshape(1, -1))
    bits = [1 << b for b in range(dp.bit_length() - 1)]

    bit_orders = []
    for m in range(2):
        bit_orders.append([bits[(b ^ m) if (b ^ m) < len(bits) else b] for b in range(len(bits))])

    def spread_step(blocks, step, places):
        for m in range(2):
            bit = bit_orders[m][step]
            for k in [k for k in blocks[m] if places(m, k)]:
                blocks[m][k ^ bit] = exchange(blocks[m][k], "dp", bit)

    hiddens = [{0: hidden_policy}, {0: hidden_reference}]
    for step in range(len(bits)):
        spread_step(hiddens, step, lambda m, k: True)
    hidden_parts = [hiddens[m][k] for m in range(2) for k in range(dp)]

    order = jnp.arange(dp, dtype=jnp.int32)
    facts = lax.all_gather(
        jnp.concatenate([lengths[:, None], targets], axis=1), "dp", axis=0, tiled=True
    )
    all_lengths = facts[:, 0]
    all_targets = facts[:, 1:].reshape(-1)
    slot_ids = jnp.arange(dp * reqs, dtype=jnp.int32)
    positions = jnp.arange(slots, dtype=jnp.int32)

    def codes(slot):
        start = jnp.sum(jnp.where(slot_ids[None] < slot[:, None], all_lengths[None], 0), axis=1)
        live = jnp.sum(jnp.where(slot_ids[None] == slot[:, None], all_lengths[None], 0), axis=1)
        return jnp.where(
            positions[None] < live[:, None], start[:, None] + positions[None], jnp.int32(-1)
        )

    source_code = codes(move_plan).reshape(dp, 1, here)
    moved = call(
        functools.partial(select_kernel, dp),
        jax.ShapeDtypeStruct((2, rows, part), jnp.bfloat16),
        (ids, source_code, *hidden_parts),
        [pltpu.VMEM((2,) + hidden_policy.shape, jnp.bfloat16), pltpu.SemaphoreType.DMA((2,))],
        far=(2, 2 + dp),
    )

    outs = [{0: out_policy}, {0: out_reference}]

    def after(first, step, places):
        flat = [(m, k) for m in range(2) for k in outs[m]]
        first, *values = lax.optimization_barrier((first, *[outs[m][k] for m, k in flat]))
        for (m, k), value in zip(flat, values):
            outs[m][k] = value
        spread_step(outs, step, places)
        return first

    moved = after(moved, 0, lambda m, k: True)

    far = sorted(range(1, half), key=lambda k: (k.bit_length() <= 1, k))

    def gather_pair(own):
        same = {0: own}
        for k in far:
            same[k] = exchange(own, "mp", 2 * k)
        same = [same[k] for k in range(half)]
        return same + [exchange(v, "mp", 1) for v in same]

    gain_scratch = pltpu.VMEM((2, 1, part * mp), jnp.float32)
    scaled_scratch = pltpu.VMEM((mp, rows, part), jnp.float32)
    normed_scratch = pltpu.VMEM((mp, rows, part), jnp.bfloat16)
    parts = gather_pair(moved)
    if len(bits) > 1:
        parts[-1] = after(parts[-1], 1, lambda m, k: k == 0)
    block = jax.ShapeDtypeStruct((2, rows, part), jnp.bfloat16)
    keep, send = call(
        functools.partial(ffn_kernel, half),
        (
            jax.ShapeDtypeStruct((half, 2, rows, part), jnp.float32),
            jax.ShapeDtypeStruct((half, 2, rows, part), jnp.bfloat16),
        ),
        (
            ids,
            *ffn_gains,
            up_policy,
            up_reference,
            down_policy,
            down_reference,
            *parts,
        ),
        [
            gain_scratch,
            scaled_scratch,
            normed_scratch,
            pltpu.VMEM((2,) + up_policy.shape, jnp.bfloat16),
            pltpu.VMEM((2,) + down_policy.shape, jnp.bfloat16),
            pltpu.SemaphoreType.DMA((6,)),
        ],
        far=range(1, 7),
    )
    came = exchange(send, "mp", 1)
    own, *pieces = call(
        pair_kernel,
        (jax.ShapeDtypeStruct((2, rows, part), jnp.float32),) + (block,) * (half - 1),
        (ids, keep, came),
    )
    arrived = {k: exchange(pieces[k - 1], "mp", 2 * k) for k in far}
    for k in range(1, half):
        own = own + arrived[k].astype(jnp.float32)
    stream = own.astype(jnp.bfloat16)
    if len(bits) > 1:
        stream = after(stream, 1, lambda m, k: k == bit_orders[m][0])
    for step in range(2, len(bits)):
        stream = after(stream, step, lambda m, k: True)

    owner_code = codes(slot_ids).reshape(-1)
    my_ranks = dp_index * rows + jnp.arange(rows, dtype=jnp.int32)
    wanted = jnp.sum(
        jnp.where(owner_code[None] == my_ranks[:, None], all_targets[None], 0),
        axis=1,
        keepdims=True,
    )
    stats = call(
        functools.partial(score_kernel, half),
        jax.ShapeDtypeStruct((8, rows), jnp.float32),
        (
            ids,
            wanted,
            *final_gains,
            *gather_pair(stream),
            *[outs[m][k] for m in range(2) for k in range(dp)],
        ),
        [
            gain_scratch,
            scaled_scratch,
            normed_scratch,
            pltpu.VMEM((2,) + out_policy.shape, jnp.bfloat16),
            pltpu.SemaphoreType.DMA((4,)),
        ],
        far=(2, 3, 4 + mp, 4 + mp + dp),
    )
    flips = [1 << b for b in range(mp.bit_length() - 1)]
    for flip in flips[:-1]:
        stats = call(
            merge_kernel,
            jax.ShapeDtypeStruct((8, rows), jnp.float32),
            (ids, stats, exchange(stats, "mp", flip)),
        )
    diff = call(
        last_kernel,
        jax.ShapeDtypeStruct((1, rows), jnp.float32),
        (ids, stats, exchange(stats, "mp", flips[-1])),
    )
    for bit in bits:
        diff = jnp.concatenate([diff, exchange(diff, "dp", bit)])
    ranks = (order ^ dp_index)[:, None] * rows + jnp.arange(rows, dtype=jnp.int32)[None]
    my_code = codes(dp_index * reqs + jnp.arange(reqs, dtype=jnp.int32))
    hit = my_code[:, :, None] == ranks.reshape(1, 1, -1)
    token_diff = jnp.sum(jnp.where(hit, diff.reshape(1, 1, -1), 0.0), axis=2)
    return (token_diff, jnp.sum(token_diff, axis=1))


def solution(mesh):
    return jax.shard_map(
        local,
        mesh=mesh,
        in_specs=(
            P("dp", None, "mp"),
            P("dp", None, "mp"),
            P(),
            P(),
            P(None, "mp"),
            P(None, "mp"),
            P("mp", None),
            P("mp", None),
            P(),
            P(),
            P("dp", "mp"),
            P("dp", "mp"),
            P(),
            P("dp"),
            P("dp", None),
        ),
        out_specs=(P("dp", None), P("dp")),
        check_vma=False,
    )
```

```python
import functools

import jax
import jax.numpy as jnp
from jax import lax
from jax.experimental import pallas as pl
from jax.experimental.pallas import tpu as pltpu
from jax.sharding import PartitionSpec as P

epsilon = 1e-05
params = pltpu.CompilerParams(vmem_limit_bytes=24 * 1024 * 1024)
vmem = pl.BlockSpec(memory_space=pltpu.VMEM)
smem = pl.BlockSpec(memory_space=pltpu.SMEM)
anywhere = pl.BlockSpec(memory_space=pltpu.HBM)


def call(kernel, out_shape, ops, scratch=(), far=()):
    specs = [smem] + [anywhere if i in far else vmem for i in range(1, len(ops))]
    ops = [
        pltpu.with_memory_space_constraint(op, pltpu.HBM) if i in far else op
        for i, op in enumerate(ops)
    ]
    return pl.pallas_call(
        kernel,
        out_shape=out_shape,
        in_specs=specs,
        out_specs=jax.tree.map(lambda _: vmem, out_shape),
        scratch_shapes=list(scratch),
        compiler_params=params,
    )(*ops)


def exchange(values, axis, flip):
    count = lax.axis_size(axis)
    return lax.ppermute(values, axis, [(i, i ^ flip) for i in range(count)])


def fetch(sources, targets, sems):
    copies = [
        pltpu.make_async_copy(source, target, sems.at[i])
        for i, (source, target) in enumerate(zip(sources, targets))
    ]
    for copy in copies:
        copy.start()
    return copies


def select_kernel(dp, ids, code, *refs):
    parts, (out, own, sems) = list(refs[: 2 * dp]), refs[2 * dp :]
    copies = fetch([parts[0], parts[dp]], [own.at[0], own.at[1]], sems)
    rows = out.shape[1]
    me = ids[0]
    wanted = me * rows + lax.broadcasted_iota(jnp.int32, (rows, code.shape[2]), 0)
    hots = [
        (code[me ^ k] == wanted).astype(jnp.float32).astype(jnp.bfloat16) for k in range(dp)
    ]
    for m in range(2):
        copies[m].wait()
        parts[m * dp] = own.at[m]
    for m in range(2):
        total = None
        for k in range(dp):
            values = parts[m * dp + k][...]
            values = values.reshape(-1, values.shape[-1])
            found = jnp.dot(hots[k], values, preferred_element_type=jnp.float32)
            total = found if total is None else total + found
        out[m] = total.astype(out.dtype)


def normalise(values, gain, chip, core, scaled, normed):
    half = len(values) // 2
    part = values[0].shape[1]
    width = part * len(values)
    values = [v.astype(jnp.float32) for v in values]
    center = sum(jnp.sum(v, axis=1, keepdims=True) for v in values) / width
    values = [v - center for v in values]
    spread = sum(jnp.sum(v * v, axis=1, keepdims=True) for v in values) / width
    scale = lax.rsqrt(spread + epsilon)
    for k, v in enumerate(values):
        scaled[2 * (chip ^ (k % half)) + (core if k < half else 1 - core)] = v * scale
    for b in range(2 * half):
        normed[b] = (scaled[b] * gain[:, b * part : (b + 1) * part]).astype(jnp.bfloat16)
    return values[0]


def ffn_kernel(half, ids, *refs):
    parts = refs[6 : 6 + 2 * half]
    keep, send, gains, scaled, normed, up_store, down_store, sems = refs[6 + 2 * half :]
    copies = fetch(
        [refs[0], refs[2], refs[4], refs[1], refs[3], refs[5]],
        [store.at[m] for m in range(2) for store in (gains, up_store, down_store)],
        sems,
    )
    chip, core = ids[1], ids[2]
    for m in range(2):
        copies[3 * m].wait()
        base = normalise([part[m] for part in parts], gains[m], chip, core, scaled, normed)
        part = base.shape[1]
        copies[3 * m + 1].wait()
        pre = None
        for b in range(2 * half):
            piece = jnp.dot(
                normed[b],
                up_store[m, b * part : (b + 1) * part, :],
                preferred_element_type=jnp.float32,
            )
            pre = piece if pre is None else pre + piece
        units = jax.nn.gelu(pre).astype(jnp.bfloat16)
        copies[3 * m + 2].wait()
        full = jnp.dot(units, down_store[m], preferred_element_type=jnp.float32)
        for b in range(2 * half):
            scaled[b] = full[:, b * part : (b + 1) * part]
        for k in range(half):
            place = 2 * (chip ^ k)
            kept = scaled[place + core]
            keep[k, m] = kept + base if k == 0 else kept
            send[k, m] = scaled[place + 1 - core].astype(jnp.bfloat16)


def pair_kernel(ids, keep, came, own, *outs):
    own[...] = keep[0] + came[0].astype(jnp.float32)
    for k, out in enumerate(outs):
        out[...] = (keep[k + 1] + came[k + 1].astype(jnp.float32)).astype(jnp.bfloat16)


def score_kernel(half, ids, wanted, *refs):
    parts = refs[2 : 2 + 2 * half]
    *outs, stats, gains, scaled, normed, out_store, sems = refs[2 + 2 * half :]
    dp = len(outs) // 2
    copies = fetch(
        [refs[0], outs[0], refs[1], outs[dp]],
        [store.at[m] for m in range(2) for store in (gains, out_store)],
        sems,
    )
    me, chip, core = ids[0], ids[1], ids[2]
    lane = lax.broadcasted_iota(jnp.int32, (parts[0].shape[1], 128), 1)
    table = jnp.zeros(lane.shape, jnp.float32)
    ratio = 2 * half // dp
    for m in range(2):
        copies[2 * m].wait()
        normalise([part[m] for part in parts], gains[m], chip, core, scaled, normed)
        part = parts[0].shape[2]
        copies[2 * m + 1].wait()
        outs[m * dp] = out_store.at[m]
        logits = None
        for k in range(dp):
            for b in range(ratio):
                piece = jnp.dot(
                    normed[(me ^ k) * ratio + b],
                    outs[m * dp + k][b * part : (b + 1) * part, :],
                    preferred_element_type=jnp.float32,
                )
                logits = piece if logits is None else logits + piece
        entries = lax.broadcasted_iota(jnp.int32, logits.shape, 1) + ids[3] * logits.shape[1]
        picked = jnp.sum(jnp.where(entries == wanted[...], logits, 0.0), axis=1, keepdims=True)
        top = jnp.max(logits, axis=1, keepdims=True)
        total = jnp.sum(jnp.exp(logits - top), axis=1, keepdims=True)
        table = jnp.where(lane == m, top, table)
        table = jnp.where(lane == 2 + m, total, table)
        table = jnp.where(lane == 4 + m, picked, table)
    stats[...] = jnp.transpose(table)[:8]


def last_kernel(dp, mp, ids, every, out):
    for d in range(dp):
        tables = [every[d * mp + j] for j in range(mp)]
        top = functools.reduce(jnp.maximum, [t[0:2] for t in tables])
        total = sum(t[2:4] * jnp.exp(t[0:2] - top) for t in tables)
        logprob = sum(t[4:6] for t in tables) - (top + jnp.log(total))
        out[d : d + 1] = logprob[0:1] - logprob[1:2]


def local(
    hidden_policy,
    hidden_reference,
    ffn_gain_policy,
    ffn_gain_reference,
    up_policy,
    up_reference,
    down_policy,
    down_reference,
    final_gain_policy,
    final_gain_reference,
    out_policy,
    out_reference,
    move_plan,
    lengths,
    targets,
):
    dp = lax.axis_size("dp")
    mp = lax.axis_size("mp")
    half = mp // 2
    dp_index = lax.axis_index("dp")
    mp_index = lax.axis_index("mp")
    ids = jnp.stack([dp_index, mp_index // 2, mp_index % 2, mp_index]).astype(jnp.int32)
    reqs, slots, part = hidden_policy.shape
    here = reqs * slots
    rows = here // 2
    ffn_gains = (ffn_gain_policy.reshape(1, -1), ffn_gain_reference.reshape(1, -1))
    final_gains = (final_gain_policy.reshape(1, -1), final_gain_reference.reshape(1, -1))
    bits = [1 << b for b in range(dp.bit_length() - 1)]

    bit_orders = []
    for m in range(2):
        bit_orders.append([bits[(b ^ m) if (b ^ m) < len(bits) else b] for b in range(len(bits))])

    def spread_step(blocks, step, places):
        for m in range(2):
            bit = bit_orders[m][step]
            for k in [k for k in blocks[m] if places(m, k)]:
                blocks[m][k ^ bit] = exchange(blocks[m][k], "dp", bit)

    hiddens = [{0: hidden_policy}, {0: hidden_reference}]
    outs = [{0: out_policy}, {0: out_reference}]

    def after(first, step, places):
        flat = [(m, k) for m in range(2) for k in outs[m]]
        first, *values = lax.optimization_barrier((first, *[outs[m][k] for m, k in flat]))
        for (m, k), value in zip(flat, values):
            outs[m][k] = value
        spread_step(outs, step, places)
        return first

    for step in range(len(bits)):
        spread_step(hiddens, step, lambda m, k: True)
        if step == 0:
            early = bit_orders[0][0]
            hiddens[0][early] = after(hiddens[0][early], 0, lambda m, k: True)
    hidden_parts = [hiddens[m][k] for m in range(2) for k in range(dp)]

    order = jnp.arange(dp, dtype=jnp.int32)
    facts = jnp.concatenate([lengths[:, None], targets], axis=1)[None]
    for bit in bits:
        facts = jnp.concatenate([facts, exchange(facts, "dp", bit)])
    all_lengths = facts[:, :, 0].reshape(-1)
    all_targets = facts[:, :, 1:].reshape(-1)
    slot_ids = ((order ^ dp_index)[:, None] * reqs + jnp.arange(reqs, dtype=jnp.int32)).reshape(-1)
    positions = jnp.arange(slots, dtype=jnp.int32)

    def codes(slot):
        start = jnp.sum(jnp.where(slot_ids[None] < slot[:, None], all_lengths[None], 0), axis=1)
        live = jnp.sum(jnp.where(slot_ids[None] == slot[:, None], all_lengths[None], 0), axis=1)
        return jnp.where(
            positions[None] < live[:, None], start[:, None] + positions[None], jnp.int32(-1)
        )

    source_code = codes(move_plan).reshape(dp, 1, here)
    moved = call(
        functools.partial(select_kernel, dp),
        jax.ShapeDtypeStruct((2, rows, part), jnp.bfloat16),
        (ids, source_code, *hidden_parts),
        [pltpu.VMEM((2,) + hidden_policy.shape, jnp.bfloat16), pltpu.SemaphoreType.DMA((2,))],
        far=(2, 2 + dp),
    )

    far = sorted(range(1, half), key=lambda k: (k.bit_length() <= 1, k))

    def gather_pair(own):
        same = {0: own}
        for k in far:
            same[k] = exchange(own, "mp", 2 * k)
        same = [same[k] for k in range(half)]
        return same + [exchange(v, "mp", 1) for v in same]

    gain_scratch = pltpu.VMEM((2, 1, part * mp), jnp.float32)
    scaled_scratch = pltpu.VMEM((mp, rows, part), jnp.float32)
    normed_scratch = pltpu.VMEM((mp, rows, part), jnp.bfloat16)
    parts = gather_pair(moved)
    if len(bits) > 1:
        parts[-1] = after(parts[-1], 1, lambda m, k: k == 0)
    block = jax.ShapeDtypeStruct((2, rows, part), jnp.bfloat16)
    keep, send = call(
        functools.partial(ffn_kernel, half),
        (
            jax.ShapeDtypeStruct((half, 2, rows, part), jnp.float32),
            jax.ShapeDtypeStruct((half, 2, rows, part), jnp.bfloat16),
        ),
        (
            ids,
            *ffn_gains,
            up_policy,
            up_reference,
            down_policy,
            down_reference,
            *parts,
        ),
        [
            gain_scratch,
            scaled_scratch,
            normed_scratch,
            pltpu.VMEM((2,) + up_policy.shape, jnp.bfloat16),
            pltpu.VMEM((2,) + down_policy.shape, jnp.bfloat16),
            pltpu.SemaphoreType.DMA((6,)),
        ],
        far=range(1, 7),
    )
    came = exchange(send, "mp", 1)
    own, *pieces = call(
        pair_kernel,
        (jax.ShapeDtypeStruct((2, rows, part), jnp.float32),) + (block,) * (half - 1),
        (ids, keep, came),
    )
    arrived = {k: exchange(pieces[k - 1], "mp", 2 * k) for k in far}
    for k in range(1, half):
        own = own + arrived[k].astype(jnp.float32)
    stream = own.astype(jnp.bfloat16)
    if len(bits) > 1:
        stream = after(stream, 1, lambda m, k: k == bit_orders[m][0])
    for step in range(2, len(bits)):
        stream = after(stream, step, lambda m, k: True)

    owner_code = codes(slot_ids).reshape(-1)
    my_ranks = dp_index * rows + jnp.arange(rows, dtype=jnp.int32)
    wanted = jnp.sum(
        jnp.where(owner_code[None] == my_ranks[:, None], all_targets[None], 0),
        axis=1,
        keepdims=True,
    )
    stats = call(
        functools.partial(score_kernel, half),
        jax.ShapeDtypeStruct((8, rows), jnp.float32),
        (
            ids,
            wanted,
            *final_gains,
            *gather_pair(stream),
            *[outs[m][k] for m in range(2) for k in range(dp)],
        ),
        [
            gain_scratch,
            scaled_scratch,
            normed_scratch,
            pltpu.VMEM((2,) + out_policy.shape, jnp.bfloat16),
            pltpu.SemaphoreType.DMA((4,)),
        ],
        far=(2, 3, 4 + mp, 4 + mp + dp),
    )
    every = lax.all_gather(stats, ("dp", "mp"), axis=0, tiled=False)
    diff = call(
        functools.partial(last_kernel, dp, mp),
        jax.ShapeDtypeStruct((dp, rows), jnp.float32),
        (ids, every),
    )
    ranks = jnp.arange(dp * rows, dtype=jnp.int32)
    my_code = codes(dp_index * reqs + jnp.arange(reqs, dtype=jnp.int32))
    hit = my_code[:, :, None] == ranks[None, None]
    token_diff = jnp.sum(jnp.where(hit, diff.reshape(1, 1, -1), 0.0), axis=2)
    return (token_diff, jnp.sum(token_diff, axis=1))


def solution(mesh):
    return jax.shard_map(
        local,
        mesh=mesh,
        in_specs=(
            P("dp", None, "mp"),
            P("dp", None, "mp"),
            P(),
            P(),
            P(None, "mp"),
            P(None, "mp"),
            P("mp", None),
            P("mp", None),
            P(),
            P(),
            P("dp", "mp"),
            P("dp", "mp"),
            P(),
            P("dp"),
            P("dp", None),
        ),
        out_specs=(P("dp", None), P("dp")),
        check_vma=False,
    )
```

```python
import functools

import jax
import jax.numpy as jnp
from jax import lax
from jax.experimental import pallas as pl
from jax.experimental.pallas import tpu as pltpu
from jax.sharding import PartitionSpec as P

epsilon = 1e-05
vmem = pl.BlockSpec(memory_space=pltpu.VMEM)
smem = pl.BlockSpec(memory_space=pltpu.SMEM)
anywhere = pl.BlockSpec(memory_space=pltpu.HBM)


def call(kernel, out_shape, ops, scratch=(), far=(), mib=4):
    specs = [smem] + [anywhere if i in far else vmem for i in range(1, len(ops))]
    ops = [
        pltpu.with_memory_space_constraint(op, pltpu.HBM) if i in far else op
        for i, op in enumerate(ops)
    ]
    return pl.pallas_call(
        kernel,
        out_shape=out_shape,
        in_specs=specs,
        out_specs=jax.tree.map(lambda _: vmem, out_shape),
        scratch_shapes=list(scratch),
        compiler_params=pltpu.CompilerParams(vmem_limit_bytes=mib * 1024 * 1024),
    )(*ops)


def exchange(values, axis, flip):
    count = lax.axis_size(axis)
    return lax.ppermute(values, axis, [(i, i ^ flip) for i in range(count)])


def fetch(sources, targets, sems):
    copies = [
        pltpu.make_async_copy(source, target, sems.at[i])
        for i, (source, target) in enumerate(zip(sources, targets))
    ]
    for copy in copies:
        copy.start()
    return copies


def pack_kernel(lengths, targets_far, hidden, out, targets, sems):
    reqs = hidden.shape[0]
    copies = fetch([targets_far, hidden], [targets, out.at[pl.ds(0, reqs)]], sems)
    copies[0].wait()
    slots, part = targets.shape[1], hidden.shape[2]
    row = lax.broadcasted_iota(jnp.int32, (slots, part), 0)
    lane = lax.broadcasted_iota(jnp.int32, (slots, part), 1)
    high = lax.shift_right_logical(targets[...], 7)
    low = targets[...] - high * 128
    block = jnp.zeros((reqs, part), jnp.float32)
    for first, values in ((1, high), (1 + slots, low)):
        spot = (lane == row + first).astype(jnp.float32).astype(jnp.bfloat16)
        values = values.astype(jnp.float32).astype(jnp.bfloat16)
        block = block + jnp.dot(values, spot, preferred_element_type=jnp.float32)
    row = lax.broadcasted_iota(jnp.int32, (reqs, part), 0)
    lane = lax.broadcasted_iota(jnp.int32, (reqs, part), 1)
    for r in range(reqs):
        here = jnp.logical_and(row == r, lane == 0)
        block = jnp.where(here, lengths[r].astype(jnp.float32), block)
    out[reqs] = block.astype(jnp.bfloat16)
    copies[1].wait()


def select_kernel(dp, ids, plan, *refs):
    parts, (out, own, sems) = list(refs[: 2 * dp]), refs[2 * dp :]
    (copy,) = fetch([parts[0]], [own], sems)
    parts[0] = own
    rows = out.shape[1]
    reqs, slots, _ = own.shape
    here = reqs * slots
    me = ids[0]
    lengths = [
        parts[dp + k][reqs].astype(jnp.float32)[:, 0:1].astype(jnp.int32) for k in range(dp)
    ]
    lengths = jnp.concatenate(lengths, axis=0)
    row = lax.broadcasted_iota(jnp.int32, (reqs, here), 0)
    slot = jnp.concatenate([row + (me ^ k) * reqs for k in range(dp)], axis=0)
    position = lax.rem(lax.broadcasted_iota(jnp.int32, (1, here), 1), slots)
    wanted = me * rows + lax.broadcasted_iota(jnp.int32, (rows, here), 0)
    hots = []
    for k in range(dp):
        owner = plan[me ^ k]
        start = jnp.sum(jnp.where(slot < owner, lengths, 0), axis=0, keepdims=True)
        live = jnp.sum(jnp.where(slot == owner, lengths, 0), axis=0, keepdims=True)
        code = jnp.where(position < live, start + position, -1)
        hots.append((code == wanted).astype(jnp.float32).astype(jnp.bfloat16))
    copy.wait()
    for m in range(2):
        total = None
        for k in range(dp):
            values = parts[m * dp + k][0:reqs]
            values = values.reshape(-1, values.shape[-1])
            found = jnp.dot(hots[k], values, preferred_element_type=jnp.float32)
            total = found if total is None else total + found
        out[m] = total.astype(out.dtype)


def normalise(values, gain, chip, core, scaled, normed):
    half = len(values) // 2
    part = values[0].shape[1]
    width = part * len(values)
    values = [v.astype(jnp.float32) for v in values]
    center = sum(jnp.sum(v, axis=1, keepdims=True) for v in values) / width
    values = [v - center for v in values]
    spread = sum(jnp.sum(v * v, axis=1, keepdims=True) for v in values) / width
    scale = lax.rsqrt(spread + epsilon)
    for k, v in enumerate(values):
        scaled[2 * (chip ^ (k % half)) + (core if k < half else 1 - core)] = v * scale
    for b in range(2 * half):
        normed[b] = (scaled[b] * gain[:, b * part : (b + 1) * part]).astype(jnp.bfloat16)
    return values[0]


def ffn_kernel(half, ids, *refs):
    parts = refs[6 : 6 + 2 * half]
    keep, send, gains, scaled, normed, up_store, down_store, sems = refs[6 + 2 * half :]
    copies = fetch(
        [refs[0], refs[2], refs[4], refs[1], refs[3], refs[5]],
        [store.at[m] for m in range(2) for store in (gains, up_store, down_store)],
        sems,
    )
    chip, core = ids[1], ids[2]
    for m in range(2):
        copies[3 * m].wait()
        base = normalise([part[m] for part in parts], gains[m], chip, core, scaled, normed)
        part = base.shape[1]
        copies[3 * m + 1].wait()
        pre = None
        for b in range(2 * half):
            piece = jnp.dot(
                normed[b],
                up_store[m, b * part : (b + 1) * part, :],
                preferred_element_type=jnp.float32,
            )
            pre = piece if pre is None else pre + piece
        units = jax.nn.gelu(pre).astype(jnp.bfloat16)
        copies[3 * m + 2].wait()
        full = jnp.dot(units, down_store[m], preferred_element_type=jnp.float32)
        for b in range(2 * half):
            scaled[b] = full[:, b * part : (b + 1) * part]
        for k in range(half):
            place = 2 * (chip ^ k)
            kept = scaled[place + core]
            keep[k, m] = kept + base if k == 0 else kept
            send[k, m] = scaled[place + 1 - core].astype(jnp.bfloat16)


def pair_kernel(ids, keep, came, own, *outs):
    own[...] = keep[0] + came[0].astype(jnp.float32)
    for k, out in enumerate(outs):
        out[...] = (keep[k + 1] + came[k + 1].astype(jnp.float32)).astype(jnp.bfloat16)


def score_kernel(half, ids, wanted, *refs):
    parts = refs[2 : 2 + 2 * half]
    *outs, stats, gains, scaled, normed, out_store, sems = refs[2 + 2 * half :]
    dp = len(outs) // 2
    copies = fetch(
        [refs[0], outs[0], refs[1], outs[dp]],
        [store.at[m] for m in range(2) for store in (gains, out_store)],
        sems,
    )
    me, chip, core = ids[0], ids[1], ids[2]
    lane = lax.broadcasted_iota(jnp.int32, (parts[0].shape[1], 128), 1)
    table = jnp.zeros(lane.shape, jnp.float32)
    ratio = 2 * half // dp
    for m in range(2):
        copies[2 * m].wait()
        normalise([part[m] for part in parts], gains[m], chip, core, scaled, normed)
        part = parts[0].shape[2]
        copies[2 * m + 1].wait()
        outs[m * dp] = out_store.at[m]
        logits = None
        for k in range(dp):
            for b in range(ratio):
                piece = jnp.dot(
                    normed[(me ^ k) * ratio + b],
                    outs[m * dp + k][b * part : (b + 1) * part, :],
                    preferred_element_type=jnp.float32,
                )
                logits = piece if logits is None else logits + piece
        entries = lax.broadcasted_iota(jnp.int32, logits.shape, 1) + ids[3] * logits.shape[1]
        picked = jnp.sum(jnp.where(entries == wanted[...], logits, 0.0), axis=1, keepdims=True)
        top = jnp.max(logits, axis=1, keepdims=True)
        total = jnp.sum(jnp.exp(logits - top), axis=1, keepdims=True)
        table = jnp.where(lane == m, top, table)
        table = jnp.where(lane == 2 + m, total, table)
        table = jnp.where(lane == 4 + m, picked, table)
    stats[...] = jnp.transpose(table)[:8]


def merge(ids, mine, came):
    top = jnp.maximum(mine[0:2], came[0:2])
    total = mine[2:4] * jnp.exp(mine[0:2] - top) + came[2:4] * jnp.exp(came[0:2] - top)
    return top, total, mine[4:6] + came[4:6]


def merge_kernel(ids, mine, came, out):
    out[0:2], out[2:4], out[4:6] = merge(ids, mine, came)
    out[6:8] = jnp.zeros((2, out.shape[1]), jnp.float32)


def last_kernel(ids, mine, came, out):
    top, total, picked = merge(ids, mine, came)
    logprob = picked - (top + jnp.log(total))
    out[...] = logprob[0:1] - logprob[1:2]


def local(
    hidden_policy,
    hidden_reference,
    ffn_gain_policy,
    ffn_gain_reference,
    up_policy,
    up_reference,
    down_policy,
    down_reference,
    final_gain_policy,
    final_gain_reference,
    out_policy,
    out_reference,
    move_plan,
    lengths,
    targets,
):
    dp = lax.axis_size("dp")
    mp = lax.axis_size("mp")
    half = mp // 2
    dp_index = lax.axis_index("dp")
    mp_index = lax.axis_index("mp")
    ids = jnp.stack([dp_index, mp_index // 2, mp_index % 2, mp_index]).astype(jnp.int32)
    reqs, slots, part = hidden_policy.shape
    here = reqs * slots
    rows = here // 2
    ffn_gains = (ffn_gain_policy.reshape(1, -1), ffn_gain_reference.reshape(1, -1))
    final_gains = (final_gain_policy.reshape(1, -1), final_gain_reference.reshape(1, -1))
    bits = [1 << b for b in range(dp.bit_length() - 1)]

    bit_orders = []
    for m in range(2):
        bit_orders.append([bits[(b ^ m) if (b ^ m) < len(bits) else b] for b in range(len(bits))])

    def spread_step(blocks, step, places):
        for m in range(2):
            bit = bit_orders[m][step]
            for k in [k for k in blocks[m] if places(m, k)]:
                blocks[m][k ^ bit] = exchange(blocks[m][k], "dp", bit)

    packed = call(
        pack_kernel,
        jax.ShapeDtypeStruct((reqs + 1, slots, part), jnp.bfloat16),
        (lengths, targets, hidden_reference),
        [pltpu.VMEM(targets.shape, jnp.int32), pltpu.SemaphoreType.DMA((2,))],
        far=(1, 2),
    )
    hiddens = [{0: hidden_policy}, {0: packed}]
    outs = [{0: out_policy}, {0: out_reference}]

    def wait_for(first, places):
        flat = [(m, k) for m in range(2) for k in outs[m] if places(m, k)]
        first, *values = lax.optimization_barrier((first, *[outs[m][k] for m, k in flat]))
        for (m, k), value in zip(flat, values):
            outs[m][k] = value
        return first

    for step in range(len(bits)):
        spread_step(hiddens, step, lambda m, k: True)
    hidden_parts = [hiddens[m][k] for m in range(2) for k in range(dp)]

    order = jnp.arange(dp, dtype=jnp.int32)
    facts = jnp.stack([hiddens[1][k][reqs, :, : 2 * slots + 1] for k in range(dp)])
    facts = facts.astype(jnp.float32).astype(jnp.int32)
    all_lengths = facts[:, :, 0].reshape(-1)
    all_targets = (facts[:, :, 1 : slots + 1] * 128 + facts[:, :, slots + 1 :]).reshape(-1)
    slot_ids = ((order ^ dp_index)[:, None] * reqs + jnp.arange(reqs, dtype=jnp.int32)).reshape(-1)
    positions = jnp.arange(slots, dtype=jnp.int32)

    def codes(slot):
        start = jnp.sum(jnp.where(slot_ids[None] < slot[:, None], all_lengths[None], 0), axis=1)
        live = jnp.sum(jnp.where(slot_ids[None] == slot[:, None], all_lengths[None], 0), axis=1)
        return jnp.where(
            positions[None] < live[:, None], start[:, None] + positions[None], jnp.int32(-1)
        )

    plan = jnp.repeat(move_plan, slots).reshape(dp, 1, here)
    moved = call(
        functools.partial(select_kernel, dp),
        jax.ShapeDtypeStruct((2, rows, part), jnp.bfloat16),
        (ids, plan, *hidden_parts),
        [pltpu.VMEM(hidden_policy.shape, jnp.bfloat16), pltpu.SemaphoreType.DMA((1,))],
        far=(2,),
    )
    moved = wait_for(moved, lambda m, k: True)
    spread_step(outs, 0, lambda m, k: True)

    far = sorted(range(1, half), key=lambda k: (k.bit_length() <= 1, k))

    def gather_pair(own):
        same = {0: own}
        for k in far:
            same[k] = exchange(own, "mp", 2 * k)
        same = [same[k] for k in range(half)]
        return same + [exchange(v, "mp", 1) for v in same]

    gain_scratch = pltpu.VMEM((2, 1, part * mp), jnp.float32)
    scaled_scratch = pltpu.VMEM((mp, rows, part), jnp.float32)
    normed_scratch = pltpu.VMEM((mp, rows, part), jnp.bfloat16)
    parts = gather_pair(moved)
    if len(bits) > 1:
        parts[-1] = wait_for(parts[-1], lambda m, k: k == 0)
        later = [{0: outs[m][0]} for m in range(2)]
        spread_step(later, 1, lambda m, k: True)
    block = jax.ShapeDtypeStruct((2, rows, part), jnp.bfloat16)
    keep, send = call(
        functools.partial(ffn_kernel, half),
        (
            jax.ShapeDtypeStruct((half, 2, rows, part), jnp.float32),
            jax.ShapeDtypeStruct((half, 2, rows, part), jnp.bfloat16),
        ),
        (
            ids,
            *ffn_gains,
            up_policy,
            up_reference,
            down_policy,
            down_reference,
            *parts,
        ),
        [
            gain_scratch,
            scaled_scratch,
            normed_scratch,
            pltpu.VMEM((2,) + up_policy.shape, jnp.bfloat16),
            pltpu.VMEM((2,) + down_policy.shape, jnp.bfloat16),
            pltpu.SemaphoreType.DMA((6,)),
        ],
        far=range(1, 7),
        mib=16,
    )
    came = wait_for(exchange(send, "mp", 1), lambda m, k: k > 0)
    own, *pieces = call(
        pair_kernel,
        (jax.ShapeDtypeStruct((2, rows, part), jnp.float32),) + (block,) * (half - 1),
        (ids, keep, came),
    )
    arrived = {k: exchange(pieces[k - 1], "mp", 2 * k) for k in far}
    for k in range(1, half):
        own = own + arrived[k].astype(jnp.float32)
    stream = own.astype(jnp.bfloat16)
    if len(bits) > 1:
        spread_step(outs, 1, lambda m, k: k == bit_orders[m][0])
        for m in range(2):
            outs[m].update(later[m])
        stream = wait_for(stream, lambda m, k: k != bits[0] + bits[1])
    for step in range(2, len(bits)):
        stream = wait_for(stream, lambda m, k: True)
        spread_step(outs, step, lambda m, k: True)

    owner_code = codes(slot_ids).reshape(-1)
    my_ranks = dp_index * rows + jnp.arange(rows, dtype=jnp.int32)
    wanted = jnp.sum(
        jnp.where(owner_code[None] == my_ranks[:, None], all_targets[None], 0),
        axis=1,
        keepdims=True,
    )
    stats = call(
        functools.partial(score_kernel, half),
        jax.ShapeDtypeStruct((8, rows), jnp.float32),
        (
            ids,
            wanted,
            *final_gains,
            *gather_pair(stream),
            *[outs[m][k] for m in range(2) for k in range(dp)],
        ),
        [
            gain_scratch,
            scaled_scratch,
            normed_scratch,
            pltpu.VMEM((2,) + out_policy.shape, jnp.bfloat16),
            pltpu.SemaphoreType.DMA((4,)),
        ],
        far=(2, 3, 4 + mp, 4 + mp + dp),
        mib=16,
    )
    flips = [1 << b for b in range(mp.bit_length() - 1)]
    for flip in flips[:-1]:
        stats = call(
            merge_kernel,
            jax.ShapeDtypeStruct((8, rows), jnp.float32),
            (ids, stats, exchange(stats, "mp", flip)),
        )
    diff = call(
        last_kernel,
        jax.ShapeDtypeStruct((1, rows), jnp.float32),
        (ids, stats, exchange(stats, "mp", flips[-1])),
    )
    diff = jnp.concatenate([diff] + [exchange(diff, "dp", k) for k in range(1, dp)])
    ranks = ((order ^ dp_index)[:, None] * rows + jnp.arange(rows, dtype=jnp.int32)).reshape(-1)
    my_code = codes(dp_index * reqs + jnp.arange(reqs, dtype=jnp.int32))
    hit = my_code[:, :, None] == ranks[None, None]
    token_diff = jnp.sum(jnp.where(hit, diff.reshape(1, 1, -1), 0.0), axis=2)
    return (token_diff, jnp.sum(token_diff, axis=1))


def solution(mesh):
    return jax.shard_map(
        local,
        mesh=mesh,
        in_specs=(
            P("dp", None, "mp"),
            P("dp", None, "mp"),
            P(),
            P(),
            P(None, "mp"),
            P(None, "mp"),
            P("mp", None),
            P("mp", None),
            P(),
            P(),
            P("dp", "mp"),
            P("dp", "mp"),
            P(),
            P("dp"),
            P("dp", None),
        ),
        out_specs=(P("dp", None), P("dp")),
        check_vma=False,
    )
```

```python
import functools

import jax
import jax.numpy as jnp
from jax import lax
from jax.experimental import pallas as pl
from jax.experimental.pallas import tpu as pltpu
from jax.sharding import PartitionSpec as P

epsilon = 1e-05
vmem = pl.BlockSpec(memory_space=pltpu.VMEM)
smem = pl.BlockSpec(memory_space=pltpu.SMEM)
anywhere = pl.BlockSpec(memory_space=pltpu.HBM)


def call(kernel, out_shape, ops, scratch=(), far=(), mib=4):
    specs = [smem] + [anywhere if i in far else vmem for i in range(1, len(ops))]
    ops = [
        pltpu.with_memory_space_constraint(op, pltpu.HBM) if i in far else op
        for i, op in enumerate(ops)
    ]
    return pl.pallas_call(
        kernel,
        out_shape=out_shape,
        in_specs=specs,
        out_specs=jax.tree.map(lambda _: vmem, out_shape),
        scratch_shapes=list(scratch),
        compiler_params=pltpu.CompilerParams(vmem_limit_bytes=mib * 1024 * 1024),
    )(*ops)


def exchange(values, axis, flip):
    count = lax.axis_size(axis)
    return lax.ppermute(values, axis, [(i, i ^ flip) for i in range(count)])


def fetch(sources, targets, sems):
    copies = [
        pltpu.make_async_copy(source, target, sems.at[i])
        for i, (source, target) in enumerate(zip(sources, targets))
    ]
    for copy in copies:
        copy.start()
    return copies


def pack_kernel(lengths, targets_far, hidden, out, targets, sems):
    reqs = hidden.shape[0]
    copies = fetch([targets_far, hidden], [targets, out.at[pl.ds(0, reqs)]], sems)
    copies[0].wait()
    slots, part = targets.shape[1], hidden.shape[2]
    row = lax.broadcasted_iota(jnp.int32, (slots, part), 0)
    lane = lax.broadcasted_iota(jnp.int32, (slots, part), 1)
    high = lax.shift_right_logical(targets[...], 7)
    low = targets[...] - high * 128
    block = jnp.zeros((reqs, part), jnp.float32)
    for first, values in ((1, high), (1 + slots, low)):
        spot = (lane == row + first).astype(jnp.float32).astype(jnp.bfloat16)
        values = values.astype(jnp.float32).astype(jnp.bfloat16)
        block = block + jnp.dot(values, spot, preferred_element_type=jnp.float32)
    row = lax.broadcasted_iota(jnp.int32, (reqs, part), 0)
    lane = lax.broadcasted_iota(jnp.int32, (reqs, part), 1)
    for r in range(reqs):
        here = jnp.logical_and(row == r, lane == 0)
        block = jnp.where(here, lengths[r].astype(jnp.float32), block)
    out[reqs] = block.astype(jnp.bfloat16)
    copies[1].wait()


def select_kernel(dp, ids, plan, *refs):
    parts, (out, facts, own, sems) = list(refs[: 2 * dp]), refs[2 * dp :]
    (copy,) = fetch([parts[0]], [own], sems)
    parts[0] = own
    rows = out.shape[1]
    reqs, slots, _ = own.shape
    here = reqs * slots
    me = ids[0]
    for k in range(dp):
        facts[k] = parts[dp + k][reqs].astype(jnp.float32)
    lengths = [facts[k][:, 0:1].astype(jnp.int32) for k in range(dp)]
    lengths = jnp.concatenate(lengths, axis=0)
    row = lax.broadcasted_iota(jnp.int32, (reqs, here), 0)
    slot = jnp.concatenate([row + (me ^ k) * reqs for k in range(dp)], axis=0)
    position = lax.rem(lax.broadcasted_iota(jnp.int32, (1, here), 1), slots)
    wanted = me * rows + lax.broadcasted_iota(jnp.int32, (rows, here), 0)
    hots = []
    for k in range(dp):
        owner = plan[me ^ k]
        start = jnp.sum(jnp.where(slot < owner, lengths, 0), axis=0, keepdims=True)
        live = jnp.sum(jnp.where(slot == owner, lengths, 0), axis=0, keepdims=True)
        code = jnp.where(position < live, start + position, -1)
        hots.append((code == wanted).astype(jnp.float32).astype(jnp.bfloat16))
    copy.wait()
    for m in range(2):
        total = None
        for k in range(dp):
            values = parts[m * dp + k][0:reqs]
            values = values.reshape(-1, values.shape[-1])
            found = jnp.dot(hots[k], values, preferred_element_type=jnp.float32)
            total = found if total is None else total + found
        out[m] = total.astype(out.dtype)


def normalise(values, gain, chip, core, scaled, store):
    half = len(values) // 2
    part = values[0].shape[1]
    width = part * len(values)
    values = [v.astype(jnp.float32) for v in values]
    center = sum(jnp.sum(v, axis=1, keepdims=True) for v in values) / width
    values = [v - center for v in values]
    spread = sum(jnp.sum(v * v, axis=1, keepdims=True) for v in values) / width
    scale = lax.rsqrt(spread + epsilon)
    for k, v in enumerate(values):
        scaled[2 * (chip ^ (k % half)) + (core if k < half else 1 - core)] = v * scale
    for b in range(2 * half):
        store(b, (scaled[b] * gain[:, b * part : (b + 1) * part]).astype(jnp.bfloat16))
    return values[0]


def load_kernel(*refs):
    count = (len(refs) - 2) // 2
    for copy in fetch(refs[1 : 1 + count], refs[1 + count : -1], refs[-1]):
        copy.wait()


def ffn_kernel(half, ids, *refs):
    gains_far, ups, downs = refs[:2], refs[2:4], refs[4:6]
    parts = refs[6 : 6 + 2 * half]
    keep, send, gains, scaled, normed, sems = refs[6 + 2 * half :]
    copies = fetch(gains_far, [gains.at[0], gains.at[1]], sems)
    chip, core = ids[1], ids[2]
    part = parts[0].shape[2]

    def store(b, values):
        normed[:, b * part : (b + 1) * part] = values

    for m in range(2):
        copies[m].wait()
        base = normalise([part[m] for part in parts], gains[m], chip, core, scaled, store)
        pre = jnp.dot(normed[...], ups[m][...], preferred_element_type=jnp.float32)
        units = jax.nn.gelu(pre).astype(jnp.bfloat16)
        full = jnp.dot(units, downs[m][...], preferred_element_type=jnp.float32)
        for b in range(2 * half):
            scaled[b] = full[:, b * part : (b + 1) * part]
        for k in range(half):
            place = 2 * (chip ^ k)
            kept = scaled[place + core]
            keep[k, m] = kept + base if k == 0 else kept
            send[k, m] = scaled[place + 1 - core].astype(jnp.bfloat16)


def pair_kernel(ids, keep, came, own, *outs):
    own[...] = keep[0] + came[0].astype(jnp.float32)
    for k, out in enumerate(outs):
        out[...] = (keep[k + 1] + came[k + 1].astype(jnp.float32)).astype(jnp.bfloat16)


def score_kernel(half, ids, wanted, *refs):
    parts = refs[2 : 2 + 2 * half]
    *outs, stats, gains, scaled, normed, out_store, sems = refs[2 + 2 * half :]
    dp = len(outs) // 2
    copies = fetch(
        [refs[0], outs[0], refs[1], outs[dp]],
        [store.at[m] for m in range(2) for store in (gains, out_store)],
        sems,
    )
    me, chip, core = ids[0], ids[1], ids[2]
    lane = lax.broadcasted_iota(jnp.int32, (parts[0].shape[1], 128), 1)
    table = jnp.zeros(lane.shape, jnp.float32)
    ratio = 2 * half // dp
    part = parts[0].shape[2]

    def store(b, values):
        normed[b // ratio, :, b % ratio * part : (b % ratio + 1) * part] = values

    for m in range(2):
        copies[2 * m].wait()
        normalise([part[m] for part in parts], gains[m], chip, core, scaled, store)
        logits = None
        for k in [*range(1, dp), 0]:
            if k == 0:
                copies[2 * m + 1].wait()
                outs[m * dp] = out_store.at[m]
            piece = jnp.dot(
                normed[me ^ k], outs[m * dp + k][...], preferred_element_type=jnp.float32
            )
            logits = piece if logits is None else logits + piece
        entries = lax.broadcasted_iota(jnp.int32, logits.shape, 1) + ids[3] * logits.shape[1]
        picked = jnp.sum(jnp.where(entries == wanted[...], logits, 0.0), axis=1, keepdims=True)
        top = jnp.max(logits, axis=1, keepdims=True)
        total = jnp.sum(jnp.exp(logits - top), axis=1, keepdims=True)
        table = jnp.where(lane == m, top, table)
        table = jnp.where(lane == 2 + m, total, table)
        table = jnp.where(lane == 4 + m, picked, table)
    stats[...] = jnp.transpose(table)[:8]


def merge(tables):
    top = functools.reduce(jnp.maximum, [t[0:2] for t in tables])
    total = sum(t[2:4] * jnp.exp(t[0:2] - top) for t in tables)
    return top, total, sum(t[4:6] for t in tables)


def merge_kernel(ids, *refs):
    out = refs[-1]
    out[0:2], out[2:4], out[4:6] = merge(refs[:-1])
    out[6:8] = jnp.zeros((2, out.shape[1]), jnp.float32)


def last_kernel(ids, *refs):
    out = refs[-1]
    top, total, picked = merge(refs[:-1])
    logprob = picked - (top + jnp.log(total))
    out[...] = logprob[0:1] - logprob[1:2]


def local(
    hidden_policy,
    hidden_reference,
    ffn_gain_policy,
    ffn_gain_reference,
    up_policy,
    up_reference,
    down_policy,
    down_reference,
    final_gain_policy,
    final_gain_reference,
    out_policy,
    out_reference,
    move_plan,
    lengths,
    targets,
):
    dp = lax.axis_size("dp")
    mp = lax.axis_size("mp")
    half = mp // 2
    dp_index = lax.axis_index("dp")
    mp_index = lax.axis_index("mp")
    ids = jnp.stack([dp_index, mp_index // 2, mp_index % 2, mp_index]).astype(jnp.int32)
    reqs, slots, part = hidden_policy.shape
    here = reqs * slots
    rows = here // 2
    ffn_gains = (ffn_gain_policy.reshape(1, -1), ffn_gain_reference.reshape(1, -1))
    final_gains = (final_gain_policy.reshape(1, -1), final_gain_reference.reshape(1, -1))
    bits = [1 << b for b in range(dp.bit_length() - 1)]

    bit_orders = []
    for m in range(2):
        bit_orders.append([bits[(b ^ m) if (b ^ m) < len(bits) else b] for b in range(len(bits))])

    def spread_step(blocks, step, places):
        for m in range(2):
            bit = bit_orders[m][step]
            for k in [k for k in blocks[m] if places(m, k)]:
                blocks[m][k ^ bit] = exchange(blocks[m][k], "dp", bit)

    packed = call(
        pack_kernel,
        jax.ShapeDtypeStruct((reqs + 1, slots, part), jnp.bfloat16),
        (lengths, targets, hidden_reference),
        [pltpu.VMEM(targets.shape, jnp.int32), pltpu.SemaphoreType.DMA((2,))],
        far=(1, 2),
    )
    hiddens = [{0: hidden_policy}, {0: packed}]
    outs = [{0: out_policy}, {0: out_reference}]

    def wait_for(first, places):
        flat = [(m, k) for m in range(2) for k in outs[m] if places(m, k)]
        first, values = lax.optimization_barrier((first, [outs[m][k] for m, k in flat]))
        for (m, k), value in zip(flat, values):
            outs[m][k] = value
        return first

    for m in range(2):
        for k in range(1, dp):
            hiddens[m][k] = exchange(hiddens[m][0], "dp", k)
    hiddens = wait_for(hiddens, lambda m, k: True)
    spread_step(outs, 0, lambda m, k: True)
    hidden_parts = [hiddens[m][k] for m in range(2) for k in range(dp)]

    order = jnp.arange(dp, dtype=jnp.int32)
    plan = jnp.repeat(move_plan, slots).reshape(dp, 1, here)
    moved, facts = call(
        functools.partial(select_kernel, dp),
        (
            jax.ShapeDtypeStruct((2, rows, part), jnp.bfloat16),
            jax.ShapeDtypeStruct((dp, reqs, part), jnp.float32),
        ),
        (ids, plan, *hidden_parts),
        [pltpu.VMEM(hidden_policy.shape, jnp.bfloat16), pltpu.SemaphoreType.DMA((1,))],
        far=(2,),
    )

    facts = facts[:, :, : 2 * slots + 1].astype(jnp.int32)
    all_lengths = facts[:, :, 0].reshape(-1)
    all_targets = (facts[:, :, 1 : slots + 1] * 128 + facts[:, :, slots + 1 :]).reshape(-1)
    slot_ids = ((order ^ dp_index)[:, None] * reqs + jnp.arange(reqs, dtype=jnp.int32)).reshape(-1)
    positions = jnp.arange(slots, dtype=jnp.int32)

    def codes(slot):
        start = jnp.sum(jnp.where(slot_ids[None] < slot[:, None], all_lengths[None], 0), axis=1)
        live = jnp.sum(jnp.where(slot_ids[None] == slot[:, None], all_lengths[None], 0), axis=1)
        return jnp.where(
            positions[None] < live[:, None], start[:, None] + positions[None], jnp.int32(-1)
        )

    far = sorted(range(1, half), key=lambda k: (k.bit_length() <= 1, k))

    def gather_pair(own):
        same = {0: own}
        for k in far:
            same[k] = exchange(own, "mp", 2 * k)
        same = [same[k] for k in range(half)]
        return same + [exchange(v, "mp", 1) for v in same]

    gain_scratch = pltpu.VMEM((2, 1, part * mp), jnp.float32)
    scaled_scratch = pltpu.VMEM((mp, rows, part), jnp.float32)
    parts = gather_pair(moved)
    if len(bits) > 1:
        parts[-1] = wait_for(parts[-1], lambda m, k: True)
        later = [{0: outs[m][0]} for m in range(2)]
        spread_step(later, 1, lambda m, k: True)
    block = jax.ShapeDtypeStruct((2, rows, part), jnp.bfloat16)
    weights = (up_policy, up_reference, down_policy, down_reference)
    weights = call(
        load_kernel,
        tuple(jax.ShapeDtypeStruct(w.shape, w.dtype) for w in weights),
        (ids, *weights),
        [pltpu.SemaphoreType.DMA((4,))],
        far=range(1, 5),
        mib=12,
    )
    keep, send = call(
        functools.partial(ffn_kernel, half),
        (
            jax.ShapeDtypeStruct((half, 2, rows, part), jnp.float32),
            jax.ShapeDtypeStruct((half, 2, rows, part), jnp.bfloat16),
        ),
        (ids, *ffn_gains, *weights, *parts),
        [
            gain_scratch,
            scaled_scratch,
            pltpu.VMEM((rows, part * mp), jnp.bfloat16),
            pltpu.SemaphoreType.DMA((2,)),
        ],
        far=(1, 2),
        mib=16,
    )
    came = exchange(send, "mp", 1)
    own, *pieces = call(
        pair_kernel,
        (jax.ShapeDtypeStruct((2, rows, part), jnp.float32),) + (block,) * (half - 1),
        (ids, keep, came),
    )
    arrived = {k: exchange(pieces[k - 1], "mp", 2 * k) for k in far}
    if len(bits) > 1:
        arrived[far[0]] = wait_for(arrived[far[0]], lambda m, k: k == bit_orders[m][0])
    for k in range(1, half):
        own = own + arrived[k].astype(jnp.float32)
    stream = own.astype(jnp.bfloat16)
    if len(bits) > 1:
        spread_step(outs, 1, lambda m, k: k == bit_orders[m][0])
        for m in range(2):
            outs[m].update(later[m])
        stream = wait_for(stream, lambda m, k: k != bits[0] + bits[1])
    for step in range(2, len(bits)):
        stream = wait_for(stream, lambda m, k: True)
        spread_step(outs, step, lambda m, k: True)

    owner_code = codes(slot_ids).reshape(-1)
    my_ranks = dp_index * rows + jnp.arange(rows, dtype=jnp.int32)
    wanted = jnp.sum(
        jnp.where(owner_code[None] == my_ranks[:, None], all_targets[None], 0),
        axis=1,
        keepdims=True,
    )
    stats = call(
        functools.partial(score_kernel, half),
        jax.ShapeDtypeStruct((8, rows), jnp.float32),
        (
            ids,
            wanted,
            *final_gains,
            *gather_pair(stream),
            *[outs[m][k] for m in range(2) for k in range(dp)],
        ),
        [
            gain_scratch,
            scaled_scratch,
            pltpu.VMEM((dp, rows, part * mp // dp), jnp.bfloat16),
            pltpu.VMEM((2,) + out_policy.shape, jnp.bfloat16),
            pltpu.SemaphoreType.DMA((4,)),
        ],
        far=(2, 3, 4 + mp, 4 + mp + dp),
        mib=16,
    )
    stats = call(
        merge_kernel,
        jax.ShapeDtypeStruct((8, rows), jnp.float32),
        (ids, stats, exchange(stats, "mp", 1)),
    )
    diff = call(
        last_kernel,
        jax.ShapeDtypeStruct((1, rows), jnp.float32),
        (ids, stats, *[exchange(stats, "mp", 2 * k) for k in far]),
    )
    for bit in bits:
        diff = jnp.concatenate([diff, exchange(diff, "dp", bit)])
    ranks = ((order ^ dp_index)[:, None] * rows + jnp.arange(rows, dtype=jnp.int32)).reshape(-1)
    my_code = codes(dp_index * reqs + jnp.arange(reqs, dtype=jnp.int32))
    hit = my_code[:, :, None] == ranks[None, None]
    token_diff = jnp.sum(jnp.where(hit, diff.reshape(1, 1, -1), 0.0), axis=2)
    return (token_diff, jnp.sum(token_diff, axis=1))


def solution(mesh):
    return jax.shard_map(
        local,
        mesh=mesh,
        in_specs=(
            P("dp", None, "mp"),
            P("dp", None, "mp"),
            P(),
            P(),
            P(None, "mp"),
            P(None, "mp"),
            P("mp", None),
            P("mp", None),
            P(),
            P(),
            P("dp", "mp"),
            P("dp", "mp"),
            P(),
            P("dp"),
            P("dp", None),
        ),
        out_specs=(P("dp", None), P("dp")),
        check_vma=False,
    )
```

```python
import functools

import jax
import jax.numpy as jnp
from jax import lax
from jax.experimental import pallas as pl
from jax.experimental.pallas import tpu as pltpu
from jax.sharding import PartitionSpec as P

epsilon = 1e-05
vmem = pl.BlockSpec(memory_space=pltpu.VMEM)
smem = pl.BlockSpec(memory_space=pltpu.SMEM)
anywhere = pl.BlockSpec(memory_space=pltpu.HBM)


def call(kernel, out_shape, ops, scratch=(), far=(), mib=4):
    specs = [smem] + [anywhere if i in far else vmem for i in range(1, len(ops))]
    ops = [
        pltpu.with_memory_space_constraint(op, pltpu.HBM) if i in far else op
        for i, op in enumerate(ops)
    ]
    return pl.pallas_call(
        kernel,
        out_shape=out_shape,
        in_specs=specs,
        out_specs=jax.tree.map(lambda _: vmem, out_shape),
        scratch_shapes=list(scratch),
        compiler_params=pltpu.CompilerParams(vmem_limit_bytes=mib * 1024 * 1024),
    )(*ops)


def exchange(values, axis, flip):
    count = lax.axis_size(axis)
    return lax.ppermute(values, axis, [(i, i ^ flip) for i in range(count)])


def fetch(sources, targets, sems):
    copies = [
        pltpu.make_async_copy(source, target, sems.at[i])
        for i, (source, target) in enumerate(zip(sources, targets))
    ]
    for copy in copies:
        copy.start()
    return copies


def pack_kernel(lengths, targets_far, hidden, out, targets, sems):
    reqs = hidden.shape[0]
    copies = fetch([targets_far, hidden], [targets, out.at[pl.ds(0, reqs)]], sems)
    copies[0].wait()
    slots, part = targets.shape[1], hidden.shape[2]
    row = lax.broadcasted_iota(jnp.int32, (slots, part), 0)
    lane = lax.broadcasted_iota(jnp.int32, (slots, part), 1)
    high = lax.shift_right_logical(targets[...], 7)
    low = targets[...] - high * 128
    block = jnp.zeros((reqs, part), jnp.float32)
    for first, values in ((1, high), (1 + slots, low)):
        spot = (lane == row + first).astype(jnp.float32).astype(jnp.bfloat16)
        values = values.astype(jnp.float32).astype(jnp.bfloat16)
        block = block + jnp.dot(values, spot, preferred_element_type=jnp.float32)
    row = lax.broadcasted_iota(jnp.int32, (reqs, part), 0)
    lane = lax.broadcasted_iota(jnp.int32, (reqs, part), 1)
    for r in range(reqs):
        here = jnp.logical_and(row == r, lane == 0)
        block = jnp.where(here, lengths[r].astype(jnp.float32), block)
    out[reqs] = block.astype(jnp.bfloat16)
    copies[1].wait()


def select_kernel(dp, ids, plan, *refs):
    parts, (out, facts, own, sems) = list(refs[: 2 * dp]), refs[2 * dp :]
    (copy,) = fetch([parts[0]], [own], sems)
    parts[0] = own
    rows = out.shape[1]
    reqs, slots, _ = own.shape
    here = reqs * slots
    me = ids[0]
    for k in range(dp):
        facts[k] = parts[dp + k][reqs].astype(jnp.float32)
    lengths = [facts[k][:, 0:1].astype(jnp.int32) for k in range(dp)]
    lengths = jnp.concatenate(lengths, axis=0)
    row = lax.broadcasted_iota(jnp.int32, (reqs, here), 0)
    slot = jnp.concatenate([row + (me ^ k) * reqs for k in range(dp)], axis=0)
    position = lax.rem(lax.broadcasted_iota(jnp.int32, (1, here), 1), slots)
    wanted = me * rows + lax.broadcasted_iota(jnp.int32, (rows, here), 0)
    hots = []
    for k in range(dp):
        owner = plan[me ^ k]
        start = jnp.sum(jnp.where(slot < owner, lengths, 0), axis=0, keepdims=True)
        live = jnp.sum(jnp.where(slot == owner, lengths, 0), axis=0, keepdims=True)
        code = jnp.where(position < live, start + position, -1)
        hots.append((code == wanted).astype(jnp.float32).astype(jnp.bfloat16))
    copy.wait()
    for m in range(2):
        total = None
        for k in range(dp):
            values = parts[m * dp + k][0:reqs]
            values = values.reshape(-1, values.shape[-1])
            found = jnp.dot(hots[k], values, preferred_element_type=jnp.float32)
            total = found if total is None else total + found
        out[m] = total.astype(out.dtype)


def normalise(values, gain, chip, core, store):
    half = len(values) // 2
    part = values[0].shape[1]
    width = part * len(values)
    values = [v.astype(jnp.float32) for v in values]
    center = sum(jnp.sum(v, axis=1, keepdims=True) for v in values) / width
    values = [v - center for v in values]
    spread = sum(jnp.sum(v * v, axis=1, keepdims=True) for v in values) / width
    scale = lax.rsqrt(spread + epsilon)
    for k, v in enumerate(values):
        place = 2 * (chip ^ (k % half)) + (core if k < half else 1 - core)
        store[place] = (v * scale * gain[place]).astype(jnp.bfloat16)
    return values[0]


def load_kernel(*refs):
    count = (len(refs) - 2) // 2
    for copy in fetch(refs[1 : 1 + count], refs[1 + count : -1], refs[-1]):
        copy.wait()


def blocks_dot(normed, weight, order):
    part = normed.shape[2]
    total = None
    for b, place in enumerate(order):
        rows = weight[b * part : (b + 1) * part, :]
        piece = jnp.dot(normed[place], rows, preferred_element_type=jnp.float32)
        total = piece if total is None else total + piece
    return total


def ffn_kernel(half, ids, *refs):
    gains, ups, downs = refs[:2], refs[2:4], refs[4:6]
    parts = refs[6 : 6 + 2 * half]
    keep, send, normed, terms = refs[6 + 2 * half :]
    chip, core = ids[1], ids[2]
    part = parts[0].shape[2]
    bases = [
        normalise([part[m] for part in parts], gains[m], chip, core, normed.at[m])
        for m in range(2)
    ]
    for m in range(2):
        pre = blocks_dot(normed.at[m], ups[m], range(2 * half))
        units = jax.nn.gelu(pre).astype(jnp.bfloat16)
        full = jnp.dot(units, downs[m][...], preferred_element_type=jnp.float32)
        for b in range(2 * half):
            terms[m, b] = full[:, b * part : (b + 1) * part]
        for k in range(half):
            place = 2 * (chip ^ k)
            kept = terms[m, place + core]
            keep[k, m] = kept + bases[m] if k == 0 else kept
            send[k, m] = terms[m, place + 1 - core].astype(jnp.bfloat16)


def pair_kernel(ids, keep, came, own, *outs):
    own[...] = keep[0] + came[0].astype(jnp.float32)
    for k, out in enumerate(outs):
        out[...] = (keep[k + 1] + came[k + 1].astype(jnp.float32)).astype(jnp.bfloat16)


def score_kernel(half, ids, wanted, *refs):
    gains, parts = refs[:2], refs[2 : 2 + 2 * half]
    *outs, stats, normed, out_store, sems = refs[2 + 2 * half :]
    dp = len(outs) // 2
    copies = fetch([outs[0], outs[dp]], [out_store.at[0], out_store.at[1]], sems)
    me, chip, core = ids[0], ids[1], ids[2]
    lane = lax.broadcasted_iota(jnp.int32, (parts[0].shape[1], 128), 1)
    table = jnp.zeros(lane.shape, jnp.float32)
    ratio = 2 * half // dp
    for m in range(2):
        normalise([part[m] for part in parts], gains[m], chip, core, normed.at[m])
    for m in range(2):
        logits = None
        for k in [*range(1, dp), 0]:
            if k == 0:
                copies[m].wait()
                outs[m * dp] = out_store.at[m]
            order = [(me ^ k) * ratio + b for b in range(ratio)]
            piece = blocks_dot(normed.at[m], outs[m * dp + k], order)
            logits = piece if logits is None else logits + piece
        entries = lax.broadcasted_iota(jnp.int32, logits.shape, 1) + ids[3] * logits.shape[1]
        picked = jnp.sum(jnp.where(entries == wanted[...], logits, 0.0), axis=1, keepdims=True)
        top = jnp.max(logits, axis=1, keepdims=True)
        total = jnp.sum(jnp.exp(logits - top), axis=1, keepdims=True)
        table = jnp.where(lane == m, top, table)
        table = jnp.where(lane == 2 + m, total, table)
        table = jnp.where(lane == 4 + m, picked, table)
    stats[...] = jnp.transpose(table)[:8]


def merge(tables):
    top = functools.reduce(jnp.maximum, [t[0:2] for t in tables])
    total = sum(t[2:4] * jnp.exp(t[0:2] - top) for t in tables)
    return top, total, sum(t[4:6] for t in tables)


def merge_kernel(ids, *refs):
    out = refs[-1]
    out[0:2], out[2:4], out[4:6] = merge(refs[:-1])
    out[6:8] = jnp.zeros((2, out.shape[1]), jnp.float32)


def last_kernel(ids, *refs):
    out = refs[-1]
    top, total, picked = merge(refs[:-1])
    logprob = picked - (top + jnp.log(total))
    out[...] = logprob[0:1] - logprob[1:2]


def local(
    hidden_policy,
    hidden_reference,
    ffn_gain_policy,
    ffn_gain_reference,
    up_policy,
    up_reference,
    down_policy,
    down_reference,
    final_gain_policy,
    final_gain_reference,
    out_policy,
    out_reference,
    move_plan,
    lengths,
    targets,
):
    dp = lax.axis_size("dp")
    mp = lax.axis_size("mp")
    half = mp // 2
    dp_index = lax.axis_index("dp")
    mp_index = lax.axis_index("mp")
    ids = jnp.stack([dp_index, mp_index // 2, mp_index % 2, mp_index]).astype(jnp.int32)
    reqs, slots, part = hidden_policy.shape
    here = reqs * slots
    rows = here // 2
    ffn_gains = (ffn_gain_policy, ffn_gain_reference)
    final_gains = (final_gain_policy, final_gain_reference)
    gains = [gain.reshape(mp, 1, part) for gain in (*ffn_gains, *final_gains)]
    bits = [1 << b for b in range(dp.bit_length() - 1)]

    bit_orders = []
    for m in range(2):
        bit_orders.append([bits[(b ^ m) if (b ^ m) < len(bits) else b] for b in range(len(bits))])

    def spread_step(blocks, step, places):
        for m in range(2):
            bit = bit_orders[m][step]
            for k in [k for k in blocks[m] if places(m, k)]:
                blocks[m][k ^ bit] = exchange(blocks[m][k], "dp", bit)

    packed = call(
        pack_kernel,
        jax.ShapeDtypeStruct((reqs + 1, slots, part), jnp.bfloat16),
        (lengths, targets, hidden_reference),
        [pltpu.VMEM(targets.shape, jnp.int32), pltpu.SemaphoreType.DMA((2,))],
        far=(1, 2),
    )
    hiddens = [{0: hidden_policy}, {0: packed}]
    outs = [{0: out_policy}, {0: out_reference}]

    def wait_for(first, places):
        flat = [(m, k) for m in range(2) for k in outs[m] if places(m, k)]
        first, values = lax.optimization_barrier((first, [outs[m][k] for m, k in flat]))
        for (m, k), value in zip(flat, values):
            outs[m][k] = value
        return first

    for step in range(len(bits)):
        spread_step(hiddens, step, lambda m, k: True)
    hiddens = wait_for(hiddens, lambda m, k: True)
    spread_step(outs, 0, lambda m, k: True)
    hidden_parts = [hiddens[m][k] for m in range(2) for k in range(dp)]

    order = jnp.arange(dp, dtype=jnp.int32)
    plan = jnp.repeat(move_plan, slots).reshape(dp, 1, here)
    moved, facts = call(
        functools.partial(select_kernel, dp),
        (
            jax.ShapeDtypeStruct((2, rows, part), jnp.bfloat16),
            jax.ShapeDtypeStruct((dp, reqs, part), jnp.float32),
        ),
        (ids, plan, *hidden_parts),
        [pltpu.VMEM(hidden_policy.shape, jnp.bfloat16), pltpu.SemaphoreType.DMA((1,))],
        far=(2,),
    )

    facts = facts[:, :, : 2 * slots + 1].astype(jnp.int32)
    all_lengths = facts[:, :, 0].reshape(-1)
    all_targets = (facts[:, :, 1 : slots + 1] * 128 + facts[:, :, slots + 1 :]).reshape(-1)
    slot_ids = ((order ^ dp_index)[:, None] * reqs + jnp.arange(reqs, dtype=jnp.int32)).reshape(-1)
    positions = jnp.arange(slots, dtype=jnp.int32)

    def codes(slot):
        start = jnp.sum(jnp.where(slot_ids[None] < slot[:, None], all_lengths[None], 0), axis=1)
        live = jnp.sum(jnp.where(slot_ids[None] == slot[:, None], all_lengths[None], 0), axis=1)
        return jnp.where(
            positions[None] < live[:, None], start[:, None] + positions[None], jnp.int32(-1)
        )

    far = sorted(range(1, half), key=lambda k: (k.bit_length() <= 1, k))

    def gather_pair(own, loaded=()):
        same = {0: own}
        for k in far:
            same[k] = exchange(own, "mp", 2 * k)
        same[far[0]], loaded = lax.optimization_barrier((same[far[0]], loaded))
        same = [same[k] for k in range(half)]
        return same + [exchange(v, "mp", 1) for v in same], loaded

    weights = (up_policy, up_reference, down_policy, down_reference, *gains)
    moved, weights = lax.optimization_barrier((moved, weights))
    loaded = call(
        load_kernel,
        tuple(jax.ShapeDtypeStruct(w.shape, w.dtype) for w in weights),
        (ids, *weights),
        [pltpu.SemaphoreType.DMA((len(weights),))],
        far=range(1, 1 + len(weights)),
        mib=12,
    )
    parts, loaded = gather_pair(moved, loaded)
    block = jax.ShapeDtypeStruct((2, rows, part), jnp.bfloat16)
    keep, send = call(
        functools.partial(ffn_kernel, half),
        (
            jax.ShapeDtypeStruct((half, 2, rows, part), jnp.float32),
            jax.ShapeDtypeStruct((half, 2, rows, part), jnp.bfloat16),
        ),
        (ids, *loaded[4:6], *loaded[:4], *parts),
        [
            pltpu.VMEM((2, mp, rows, part), jnp.bfloat16),
            pltpu.VMEM((2, mp, rows, part), jnp.float32),
        ],
        mib=14,
    )
    send = wait_for(send, lambda m, k: True)
    if len(bits) > 1:
        later = [{0: outs[m][0]} for m in range(2)]
        spread_step(later, 1, lambda m, k: True)
    came = exchange(send, "mp", 1)
    own, *pieces = call(
        pair_kernel,
        (jax.ShapeDtypeStruct((2, rows, part), jnp.float32),) + (block,) * (half - 1),
        (ids, keep, came),
    )
    arrived = {k: exchange(pieces[k - 1], "mp", 2 * k) for k in far}
    if len(bits) > 1:
        arrived[far[0]] = wait_for(arrived[far[0]], lambda m, k: k == bit_orders[m][0])
    for k in range(1, half):
        own = own + arrived[k].astype(jnp.float32)
    stream = own.astype(jnp.bfloat16)
    if len(bits) > 1:
        spread_step(outs, 1, lambda m, k: k == bit_orders[m][0])
        for m in range(2):
            outs[m].update(later[m])
        stream = wait_for(stream, lambda m, k: k != bits[0] + bits[1])
    for step in range(2, len(bits)):
        stream = wait_for(stream, lambda m, k: True)
        spread_step(outs, step, lambda m, k: True)

    owner_code = codes(slot_ids).reshape(-1)
    my_ranks = dp_index * rows + jnp.arange(rows, dtype=jnp.int32)
    wanted = jnp.sum(
        jnp.where(owner_code[None] == my_ranks[:, None], all_targets[None], 0),
        axis=1,
        keepdims=True,
    )
    stats = call(
        functools.partial(score_kernel, half),
        jax.ShapeDtypeStruct((8, rows), jnp.float32),
        (
            ids,
            wanted,
            *loaded[6:],
            *gather_pair(stream)[0],
            *[outs[m][k] for m in range(2) for k in range(dp)],
        ),
        [
            pltpu.VMEM((2, mp, rows, part), jnp.bfloat16),
            pltpu.VMEM((2,) + out_policy.shape, jnp.bfloat16),
            pltpu.SemaphoreType.DMA((2,)),
        ],
        far=(4 + mp, 4 + mp + dp),
        mib=14,
    )
    stats = call(
        merge_kernel,
        jax.ShapeDtypeStruct((8, rows), jnp.float32),
        (ids, stats, exchange(stats, "mp", 1)),
    )
    diff = call(
        last_kernel,
        jax.ShapeDtypeStruct((1, rows), jnp.float32),
        (ids, stats, *[exchange(stats, "mp", 2 * k) for k in far]),
    )
    diff = jnp.concatenate([diff] + [exchange(diff, "dp", k) for k in range(1, dp)])
    ranks = ((order ^ dp_index)[:, None] * rows + jnp.arange(rows, dtype=jnp.int32)).reshape(-1)
    my_code = codes(dp_index * reqs + jnp.arange(reqs, dtype=jnp.int32))
    hit = my_code[:, :, None] == ranks[None, None]
    token_diff = jnp.sum(jnp.where(hit, diff.reshape(1, 1, -1), 0.0), axis=2)
    return (token_diff, jnp.sum(token_diff, axis=1))


def solution(mesh):
    return jax.shard_map(
        local,
        mesh=mesh,
        in_specs=(
            P("dp", None, "mp"),
            P("dp", None, "mp"),
            P(),
            P(),
            P(None, "mp"),
            P(None, "mp"),
            P("mp", None),
            P("mp", None),
            P(),
            P(),
            P("dp", "mp"),
            P("dp", "mp"),
            P(),
            P("dp"),
            P("dp", None),
        ),
        out_specs=(P("dp", None), P("dp")),
        check_vma=False,
    )
```

```python
import functools

import jax
import jax.numpy as jnp
from jax import lax
from jax.experimental import pallas as pl
from jax.experimental.pallas import tpu as pltpu
from jax.sharding import PartitionSpec as P

epsilon = 1e-05
vmem = pl.BlockSpec(memory_space=pltpu.VMEM)
smem = pl.BlockSpec(memory_space=pltpu.SMEM)
anywhere = pl.BlockSpec(memory_space=pltpu.HBM)


def call(kernel, out_shape, ops, scratch=(), far=(), mib=4):
    specs = [smem] + [anywhere if i in far else vmem for i in range(1, len(ops))]
    ops = [
        pltpu.with_memory_space_constraint(op, pltpu.HBM) if i in far else op
        for i, op in enumerate(ops)
    ]
    return pl.pallas_call(
        kernel,
        out_shape=out_shape,
        in_specs=specs,
        out_specs=jax.tree.map(lambda _: vmem, out_shape),
        scratch_shapes=list(scratch),
        compiler_params=pltpu.CompilerParams(vmem_limit_bytes=mib * 1024 * 1024),
    )(*ops)


def exchange(values, axis, flip):
    count = lax.axis_size(axis)
    return lax.ppermute(values, axis, [(i, i ^ flip) for i in range(count)])


def fetch(sources, targets, sems):
    copies = [
        pltpu.make_async_copy(source, target, sems.at[i])
        for i, (source, target) in enumerate(zip(sources, targets))
    ]
    for copy in copies:
        copy.start()
    return copies


def pack_kernel(lengths, targets_far, hidden, out, targets, sems):
    reqs = hidden.shape[0]
    copies = fetch([targets_far, hidden], [targets, out.at[pl.ds(0, reqs)]], sems)
    copies[0].wait()
    slots, part = targets.shape[1], hidden.shape[2]
    row = lax.broadcasted_iota(jnp.int32, (slots, part), 0)
    lane = lax.broadcasted_iota(jnp.int32, (slots, part), 1)
    high = lax.shift_right_logical(targets[...], 7)
    low = targets[...] - high * 128
    block = jnp.zeros((reqs, part), jnp.float32)
    for first, values in ((1, high), (1 + slots, low)):
        spot = (lane == row + first).astype(jnp.float32).astype(jnp.bfloat16)
        values = values.astype(jnp.float32).astype(jnp.bfloat16)
        block = block + jnp.dot(values, spot, preferred_element_type=jnp.float32)
    row = lax.broadcasted_iota(jnp.int32, (reqs, part), 0)
    lane = lax.broadcasted_iota(jnp.int32, (reqs, part), 1)
    for r in range(reqs):
        here = jnp.logical_and(row == r, lane == 0)
        block = jnp.where(here, lengths[r].astype(jnp.float32), block)
    out[reqs] = block.astype(jnp.bfloat16)
    copies[1].wait()


def select_kernel(dp, ids, plan, *refs):
    parts, (out, facts, own, sems) = list(refs[: 2 * dp]), refs[2 * dp :]
    (copy,) = fetch([parts[0]], [own], sems)
    parts[0] = own
    rows = out.shape[1]
    reqs, slots, _ = own.shape
    here = reqs * slots
    me = ids[0]
    for k in range(dp):
        facts[k] = parts[dp + k][reqs].astype(jnp.float32)
    lengths = [facts[k][:, 0:1].astype(jnp.int32) for k in range(dp)]
    lengths = jnp.concatenate(lengths, axis=0)
    row = lax.broadcasted_iota(jnp.int32, (reqs, here), 0)
    slot = jnp.concatenate([row + (me ^ k) * reqs for k in range(dp)], axis=0)
    position = lax.rem(lax.broadcasted_iota(jnp.int32, (1, here), 1), slots)
    wanted = me * rows + lax.broadcasted_iota(jnp.int32, (rows, here), 0)
    hots = []
    for k in range(dp):
        owner = plan[me ^ k]
        start = jnp.sum(jnp.where(slot < owner, lengths, 0), axis=0, keepdims=True)
        live = jnp.sum(jnp.where(slot == owner, lengths, 0), axis=0, keepdims=True)
        code = jnp.where(position < live, start + position, -1)
        hots.append((code == wanted).astype(jnp.float32).astype(jnp.bfloat16))
    copy.wait()
    for m in range(2):
        total = None
        for k in range(dp):
            values = parts[m * dp + k][0:reqs]
            values = values.reshape(-1, values.shape[-1])
            found = jnp.dot(hots[k], values, preferred_element_type=jnp.float32)
            total = found if total is None else total + found
        out[m] = total.astype(out.dtype)


def normalise(values, gain, chip, core, store, copy):
    half = len(values) // 2
    part = values[0].shape[1]
    width = part * len(values)
    values = [v.astype(jnp.float32) for v in values]
    center = sum(jnp.sum(v, axis=1, keepdims=True) for v in values) / width
    values = [v - center for v in values]
    spread = sum(jnp.sum(v * v, axis=1, keepdims=True) for v in values) / width
    scale = lax.rsqrt(spread + epsilon)
    copy.wait()
    for k, v in enumerate(values):
        place = 2 * (chip ^ (k % half)) + (core if k < half else 1 - core)
        store[place] = (v * scale * gain[place]).astype(jnp.bfloat16)
    return values[0]


def blocks_dot(normed, weight, order):
    part = normed.shape[2]
    total = None
    for b, place in enumerate(order):
        rows = weight[b * part : (b + 1) * part, :]
        piece = jnp.dot(normed[place], rows, preferred_element_type=jnp.float32)
        total = piece if total is None else total + piece
    return total


def ffn_kernel(half, ids, *refs):
    parts = refs[6 : 6 + 2 * half]
    keep, send, gains, ups, downs, normed, terms, sems = refs[6 + 2 * half :]
    copies = fetch(
        refs[:6], [store.at[m] for store in (gains, ups, downs) for m in range(2)], sems
    )
    chip, core = ids[1], ids[2]
    part = parts[0].shape[2]
    bases = [
        normalise([part[m] for part in parts], gains.at[m], chip, core, normed.at[m], copies[m])
        for m in range(2)
    ]
    for m in range(2):
        copies[2 + m].wait()
        pre = blocks_dot(normed.at[m], ups.at[m], range(2 * half))
        units = jax.nn.gelu(pre).astype(jnp.bfloat16)
        copies[4 + m].wait()
        full = jnp.dot(units, downs[m], preferred_element_type=jnp.float32)
        for b in range(2 * half):
            terms[m, b] = full[:, b * part : (b + 1) * part]
        for k in range(half):
            place = 2 * (chip ^ k)
            kept = terms[m, place + core]
            keep[k, m] = kept + bases[m] if k == 0 else kept
            send[k, m] = terms[m, place + 1 - core].astype(jnp.bfloat16)


def pair_kernel(ids, keep, came, own, *outs):
    own[...] = keep[0] + came[0].astype(jnp.float32)
    for k, out in enumerate(outs):
        out[...] = (keep[k + 1] + came[k + 1].astype(jnp.float32)).astype(jnp.bfloat16)


def score_kernel(half, ids, wanted, *refs):
    parts = refs[2 : 2 + 2 * half]
    *outs, stats, gains, normed, out_store, sems = refs[2 + 2 * half :]
    dp = len(outs) // 2
    copies = fetch(
        [refs[0], refs[1], outs[0], outs[dp]],
        [store.at[m] for store in (gains, out_store) for m in range(2)],
        sems,
    )
    me, chip, core = ids[0], ids[1], ids[2]
    lane = lax.broadcasted_iota(jnp.int32, (parts[0].shape[1], 128), 1)
    table = jnp.zeros(lane.shape, jnp.float32)
    ratio = 2 * half // dp
    for m in range(2):
        values = [part[m] for part in parts]
        normalise(values, gains.at[m], chip, core, normed.at[m], copies[m])
    for m in range(2):
        logits = None
        for k in [*range(1, dp), 0]:
            if k == 0:
                copies[2 + m].wait()
                outs[m * dp] = out_store.at[m]
            order = [(me ^ k) * ratio + b for b in range(ratio)]
            piece = blocks_dot(normed.at[m], outs[m * dp + k], order)
            logits = piece if logits is None else logits + piece
        entries = lax.broadcasted_iota(jnp.int32, logits.shape, 1) + ids[3] * logits.shape[1]
        picked = jnp.sum(jnp.where(entries == wanted[...], logits, 0.0), axis=1, keepdims=True)
        top = jnp.max(logits, axis=1, keepdims=True)
        total = jnp.sum(jnp.exp(logits - top), axis=1, keepdims=True)
        table = jnp.where(lane == m, top, table)
        table = jnp.where(lane == 2 + m, total, table)
        table = jnp.where(lane == 4 + m, picked, table)
    stats[...] = jnp.transpose(table)[:8]


def merge(tables):
    top = functools.reduce(jnp.maximum, [t[0:2] for t in tables])
    total = sum(t[2:4] * jnp.exp(t[0:2] - top) for t in tables)
    return top, total, sum(t[4:6] for t in tables)


def merge_kernel(ids, *refs):
    out = refs[-1]
    out[0:2], out[2:4], out[4:6] = merge(refs[:-1])
    out[6:8] = jnp.zeros((2, out.shape[1]), jnp.float32)


def last_kernel(ids, *refs):
    out = refs[-1]
    top, total, picked = merge(refs[:-1])
    logprob = picked - (top + jnp.log(total))
    out[...] = logprob[0:1] - logprob[1:2]


def local(
    hidden_policy,
    hidden_reference,
    ffn_gain_policy,
    ffn_gain_reference,
    up_policy,
    up_reference,
    down_policy,
    down_reference,
    final_gain_policy,
    final_gain_reference,
    out_policy,
    out_reference,
    move_plan,
    lengths,
    targets,
):
    dp = lax.axis_size("dp")
    mp = lax.axis_size("mp")
    half = mp // 2
    dp_index = lax.axis_index("dp")
    mp_index = lax.axis_index("mp")
    ids = jnp.stack([dp_index, mp_index // 2, mp_index % 2, mp_index]).astype(jnp.int32)
    reqs, slots, part = hidden_policy.shape
    here = reqs * slots
    rows = here // 2
    ffn_gains = (ffn_gain_policy, ffn_gain_reference)
    final_gains = (final_gain_policy, final_gain_reference)
    gains = [gain.reshape(mp, 1, part) for gain in (*ffn_gains, *final_gains)]
    bits = [1 << b for b in range(dp.bit_length() - 1)]

    bit_orders = []
    for m in range(2):
        bit_orders.append([bits[(b ^ m) if (b ^ m) < len(bits) else b] for b in range(len(bits))])

    def spread_step(blocks, step, places):
        for m in range(2):
            bit = bit_orders[m][step]
            for k in [k for k in blocks[m] if places(m, k)]:
                blocks[m][k ^ bit] = exchange(blocks[m][k], "dp", bit)

    packed = call(
        pack_kernel,
        jax.ShapeDtypeStruct((reqs + 1, slots, part), jnp.bfloat16),
        (lengths, targets, hidden_reference),
        [pltpu.VMEM(targets.shape, jnp.int32), pltpu.SemaphoreType.DMA((2,))],
        far=(1, 2),
    )
    hiddens = [{0: hidden_policy}, {0: packed}]
    outs = [{0: out_policy}, {0: out_reference}]

    def wait_for(first, places):
        flat = [(m, k) for m in range(2) for k in outs[m] if places(m, k)]
        first, values = lax.optimization_barrier((first, [outs[m][k] for m, k in flat]))
        for (m, k), value in zip(flat, values):
            outs[m][k] = value
        return first

    for step in range(len(bits)):
        spread_step(hiddens, step, lambda m, k: True)
    hiddens = wait_for(hiddens, lambda m, k: True)
    spread_step(outs, 0, lambda m, k: True)
    hidden_parts = [hiddens[m][k] for m in range(2) for k in range(dp)]

    order = jnp.arange(dp, dtype=jnp.int32)
    plan = jnp.repeat(move_plan, slots).reshape(dp, 1, here)
    moved, facts = call(
        functools.partial(select_kernel, dp),
        (
            jax.ShapeDtypeStruct((2, rows, part), jnp.bfloat16),
            jax.ShapeDtypeStruct((dp, reqs, part), jnp.float32),
        ),
        (ids, plan, *hidden_parts),
        [pltpu.VMEM(hidden_policy.shape, jnp.bfloat16), pltpu.SemaphoreType.DMA((1,))],
        far=(2,),
    )

    facts = facts[:, :, : 2 * slots + 1].astype(jnp.int32)
    all_lengths = facts[:, :, 0].reshape(-1)
    all_targets = (facts[:, :, 1 : slots + 1] * 128 + facts[:, :, slots + 1 :]).reshape(-1)
    slot_ids = ((order ^ dp_index)[:, None] * reqs + jnp.arange(reqs, dtype=jnp.int32)).reshape(-1)
    positions = jnp.arange(slots, dtype=jnp.int32)

    def codes(slot):
        start = jnp.sum(jnp.where(slot_ids[None] < slot[:, None], all_lengths[None], 0), axis=1)
        live = jnp.sum(jnp.where(slot_ids[None] == slot[:, None], all_lengths[None], 0), axis=1)
        return jnp.where(
            positions[None] < live[:, None], start[:, None] + positions[None], jnp.int32(-1)
        )

    far = sorted(range(1, half), key=lambda k: (k.bit_length() <= 1, k))

    def gather_pair(own):
        same = {0: own}
        for k in far:
            same[k] = exchange(own, "mp", 2 * k)
        same = [same[k] for k in range(half)]
        return same + [exchange(v, "mp", 1) for v in same]

    parts = gather_pair(moved)
    if len(bits) > 1:
        parts[-1] = wait_for(parts[-1], lambda m, k: k == 0)
        later = [{0: outs[m][0]} for m in range(2)]
        spread_step(later, 1, lambda m, k: True)
    gain_scratch = pltpu.VMEM((2, mp, 1, part), jnp.float32)
    block = jax.ShapeDtypeStruct((2, rows, part), jnp.bfloat16)
    keep, send = call(
        functools.partial(ffn_kernel, half),
        (
            jax.ShapeDtypeStruct((half, 2, rows, part), jnp.float32),
            jax.ShapeDtypeStruct((half, 2, rows, part), jnp.bfloat16),
        ),
        (ids, *gains[:2], up_policy, up_reference, down_policy, down_reference, *parts),
        [
            gain_scratch,
            pltpu.VMEM((2,) + up_policy.shape, jnp.bfloat16),
            pltpu.VMEM((2,) + down_policy.shape, jnp.bfloat16),
            pltpu.VMEM((2, mp, rows, part), jnp.bfloat16),
            pltpu.VMEM((2, mp, rows, part), jnp.float32),
            pltpu.SemaphoreType.DMA((6,)),
        ],
        far=range(1, 7),
        mib=22,
    )
    send = wait_for(send, lambda m, k: k > 0)
    came = exchange(send, "mp", 1)
    own, *pieces = call(
        pair_kernel,
        (jax.ShapeDtypeStruct((2, rows, part), jnp.float32),) + (block,) * (half - 1),
        (ids, keep, came),
    )
    arrived = {k: exchange(pieces[k - 1], "mp", 2 * k) for k in far}
    if len(bits) > 1:
        for m in range(2):
            outs[m].update(later[m])
        arrived[far[0]] = wait_for(arrived[far[0]], lambda m, k: True)
        spread_step(outs, 1, lambda m, k: k == bit_orders[m][0])
    for k in range(1, half):
        own = own + arrived[k].astype(jnp.float32)
    stream = own.astype(jnp.bfloat16)
    for step in range(2, len(bits)):
        stream = wait_for(stream, lambda m, k: True)
        spread_step(outs, step, lambda m, k: True)

    owner_code = codes(slot_ids).reshape(-1)
    my_ranks = dp_index * rows + jnp.arange(rows, dtype=jnp.int32)
    wanted = jnp.sum(
        jnp.where(owner_code[None] == my_ranks[:, None], all_targets[None], 0),
        axis=1,
        keepdims=True,
    )
    stats = call(
        functools.partial(score_kernel, half),
        jax.ShapeDtypeStruct((8, rows), jnp.float32),
        (
            ids,
            wanted,
            *gains[2:],
            *gather_pair(stream),
            *[outs[m][k] for m in range(2) for k in range(dp)],
        ),
        [
            gain_scratch,
            pltpu.VMEM((2, mp, rows, part), jnp.bfloat16),
            pltpu.VMEM((2,) + out_policy.shape, jnp.bfloat16),
            pltpu.SemaphoreType.DMA((4,)),
        ],
        far=(2, 3, 4 + mp, 4 + mp + dp),
        mib=14,
    )
    stats = call(
        merge_kernel,
        jax.ShapeDtypeStruct((8, rows), jnp.float32),
        (ids, stats, exchange(stats, "mp", 1)),
    )
    diff = call(
        last_kernel,
        jax.ShapeDtypeStruct((1, rows), jnp.float32),
        (ids, stats, *[exchange(stats, "mp", 2 * k) for k in far]),
    )
    diff = jnp.concatenate([diff] + [exchange(diff, "dp", k) for k in range(1, dp)])
    ranks = ((order ^ dp_index)[:, None] * rows + jnp.arange(rows, dtype=jnp.int32)).reshape(-1)
    my_code = codes(dp_index * reqs + jnp.arange(reqs, dtype=jnp.int32))
    hit = my_code[:, :, None] == ranks[None, None]
    token_diff = jnp.sum(jnp.where(hit, diff.reshape(1, 1, -1), 0.0), axis=2)
    return (token_diff, jnp.sum(token_diff, axis=1))


def solution(mesh):
    return jax.shard_map(
        local,
        mesh=mesh,
        in_specs=(
            P("dp", None, "mp"),
            P("dp", None, "mp"),
            P(),
            P(),
            P(None, "mp"),
            P(None, "mp"),
            P("mp", None),
            P("mp", None),
            P(),
            P(),
            P("dp", "mp"),
            P("dp", "mp"),
            P(),
            P("dp"),
            P("dp", None),
        ),
        out_specs=(P("dp", None), P("dp")),
        check_vma=False,
    )
```

```python
import functools

import jax
import jax.numpy as jnp
from jax import lax
from jax.experimental import pallas as pl
from jax.experimental.pallas import tpu as pltpu
from jax.sharding import PartitionSpec as P

epsilon = 1e-05
vmem = pl.BlockSpec(memory_space=pltpu.VMEM)
smem = pl.BlockSpec(memory_space=pltpu.SMEM)
anywhere = pl.BlockSpec(memory_space=pltpu.HBM)


def call(kernel, out_shape, ops, scratch=(), far=(), mib=4):
    specs = [anywhere if i in far else vmem if i else smem for i in range(len(ops))]
    ops = [
        pltpu.with_memory_space_constraint(op, pltpu.HBM) if i in far else op
        for i, op in enumerate(ops)
    ]
    return pl.pallas_call(
        kernel,
        out_shape=out_shape,
        in_specs=specs,
        out_specs=jax.tree.map(lambda _: vmem, out_shape),
        scratch_shapes=list(scratch),
        compiler_params=pltpu.CompilerParams(vmem_limit_bytes=mib * 1024 * 1024),
    )(*ops)


def exchange(values, axis, flip):
    count = lax.axis_size(axis)
    return lax.ppermute(values, axis, [(i, i ^ flip) for i in range(count)])


def fetch(sources, targets, sems):
    copies = [
        pltpu.make_async_copy(source, target, sems.at[i])
        for i, (source, target) in enumerate(zip(sources, targets))
    ]
    for copy in copies:
        copy.start()
    return copies


def pack_kernel(lengths_far, targets_far, hidden, out, lengths, targets, sems):
    reqs = hidden.shape[0]
    copies = fetch(
        [lengths_far, targets_far, hidden], [lengths, targets, out.at[pl.ds(0, reqs)]], sems
    )
    copies[1].wait()
    slots, part = targets.shape[1], hidden.shape[2]
    row = lax.broadcasted_iota(jnp.int32, (slots, part), 0)
    lane = lax.broadcasted_iota(jnp.int32, (slots, part), 1)
    high = lax.shift_right_logical(targets[...], 7)
    low = targets[...] - high * 128
    block = jnp.zeros((reqs, part), jnp.float32)
    for first, values in ((1, high), (1 + slots, low)):
        spot = (lane == row + first).astype(jnp.float32).astype(jnp.bfloat16)
        values = values.astype(jnp.float32).astype(jnp.bfloat16)
        block = block + jnp.dot(values, spot, preferred_element_type=jnp.float32)
    row = lax.broadcasted_iota(jnp.int32, (reqs, part), 0)
    lane = lax.broadcasted_iota(jnp.int32, (reqs, part), 1)
    copies[0].wait()
    for r in range(reqs):
        here = jnp.logical_and(row == r, lane == 0)
        block = jnp.where(here, lengths[r].astype(jnp.float32), block)
    out[reqs] = block.astype(jnp.bfloat16)
    copies[2].wait()


def select_kernel(dp, ids, plan_far, *refs):
    parts, (out, facts, own, plan, sems) = list(refs[: 2 * dp]), refs[2 * dp :]
    plan_copy, copy = fetch([plan_far, parts[0]], [plan, own], sems)
    parts[0] = own
    rows = out.shape[1]
    reqs, slots, _ = own.shape
    here = reqs * slots
    me = ids[0]
    for k in range(dp):
        facts[k] = parts[dp + k][reqs].astype(jnp.float32)
    lengths = [facts[k][:, 0:1].astype(jnp.int32) for k in range(dp)]
    lengths = jnp.concatenate(lengths, axis=0)
    row = lax.broadcasted_iota(jnp.int32, (reqs, here), 0)
    slot = jnp.concatenate([row + (me ^ k) * reqs for k in range(dp)], axis=0)
    position = lax.rem(lax.broadcasted_iota(jnp.int32, (1, here), 1), slots)
    wanted = me * rows + lax.broadcasted_iota(jnp.int32, (rows, here), 0)
    request = lax.div(lax.broadcasted_iota(jnp.int32, (1, here), 1), slots)
    hots = []
    plan_copy.wait()
    for k in range(dp):
        owner = jnp.zeros((1, here), jnp.int32)
        for r in range(reqs):
            owner = jnp.where(request == r, plan[(me ^ k) * reqs + r], owner)
        start = jnp.sum(jnp.where(slot < owner, lengths, 0), axis=0, keepdims=True)
        live = jnp.sum(jnp.where(slot == owner, lengths, 0), axis=0, keepdims=True)
        code = jnp.where(position < live, start + position, -1)
        hots.append((code == wanted).astype(jnp.float32).astype(jnp.bfloat16))
    copy.wait()
    for m in range(2):
        total = None
        for k in range(dp):
            values = parts[m * dp + k][0:reqs]
            values = values.reshape(-1, values.shape[-1])
            found = jnp.dot(hots[k], values, preferred_element_type=jnp.float32)
            total = found if total is None else total + found
        out[m] = total.astype(out.dtype)


def normalise(values, gain, chip, core, store, copy):
    half = len(values) // 2
    part = values[0].shape[1]
    width = part * len(values)
    values = [v.astype(jnp.float32) for v in values]
    center = sum(jnp.sum(v, axis=1, keepdims=True) for v in values) / width
    values = [v - center for v in values]
    spread = sum(jnp.sum(v * v, axis=1, keepdims=True) for v in values) / width
    scale = lax.rsqrt(spread + epsilon)
    copy.wait()
    for k, v in enumerate(values):
        place = 2 * (chip ^ (k % half)) + (core if k < half else 1 - core)
        store[place] = (v * scale * gain[place]).astype(jnp.bfloat16)
    return values[0]


def blocks_dot(normed, weight, order):
    part = normed.shape[2]
    total = None
    for b, place in enumerate(order):
        rows = weight[b * part : (b + 1) * part, :]
        piece = jnp.dot(normed[place], rows, preferred_element_type=jnp.float32)
        total = piece if total is None else total + piece
    return total


def ffn_kernel(half, ids, *refs):
    parts = refs[6 : 6 + 2 * half]
    keep, send, gains, ups, downs, normed, terms, sems = refs[6 + 2 * half :]
    copies = fetch(
        refs[:6], [store.at[m] for store in (gains, ups, downs) for m in range(2)], sems
    )
    chip, core = ids[1], ids[2]
    part = parts[0].shape[2]
    bases = [
        normalise([part[m] for part in parts], gains.at[m], chip, core, normed.at[m], copies[m])
        for m in range(2)
    ]
    for m in range(2):
        copies[2 + m].wait()
        pre = blocks_dot(normed.at[m], ups.at[m], range(2 * half))
        units = jax.nn.gelu(pre).astype(jnp.bfloat16)
        copies[4 + m].wait()
        full = jnp.dot(units, downs[m], preferred_element_type=jnp.float32)
        for b in range(2 * half):
            terms[m, b] = full[:, b * part : (b + 1) * part]
        for k in range(half):
            place = 2 * (chip ^ k)
            kept = terms[m, place + core]
            keep[k, m] = kept + bases[m] if k == 0 else kept
            send[k, m] = terms[m, place + 1 - core].astype(jnp.bfloat16)


def pair_kernel(ids, keep, came, own, *outs):
    own[...] = keep[0] + came[0].astype(jnp.float32)
    for k, out in enumerate(outs):
        out[...] = (keep[k + 1] + came[k + 1].astype(jnp.float32)).astype(jnp.bfloat16)


def score_kernel(half, dp, ids, *refs):
    parts = refs[2 : 2 + 2 * half]
    *outs, partial, tail, gains, normed, out_store, sems = refs[2 + 2 * half :]
    here = dp - 1
    copies = fetch(
        [refs[0], refs[1], outs[0], outs[here]],
        [store.at[m] for store in (gains, out_store) for m in range(2)],
        sems,
    )
    me, chip, core = ids[0], ids[1], ids[2]
    ratio = 2 * half // dp
    part = parts[0].shape[2]
    for m in range(2):
        values = [part[m] for part in parts]
        normalise(values, gains.at[m], chip, core, normed.at[m], copies[m])
        for b in range(ratio):
            tail[m, :, b * part : (b + 1) * part] = normed[m, (me ^ here) * ratio + b]
    for m in range(2):
        logits = None
        for k in [*range(1, here), 0]:
            if k == 0:
                copies[2 + m].wait()
                outs[m * here] = out_store.at[m]
            order = [(me ^ k) * ratio + b for b in range(ratio)]
            piece = blocks_dot(normed.at[m], outs[m * here + k], order)
            logits = piece if logits is None else logits + piece
        partial[m] = logits


def finish_kernel(ids, wanted, partial, tail, last_policy, last_reference, stats):
    lane = lax.broadcasted_iota(jnp.int32, (tail.shape[1], 128), 1)
    table = jnp.zeros(lane.shape, jnp.float32)
    for m, last in enumerate((last_policy, last_reference)):
        logits = partial[m] + jnp.dot(tail[m], last[...], preferred_element_type=jnp.float32)
        entries = lax.broadcasted_iota(jnp.int32, logits.shape, 1) + ids[3] * logits.shape[1]
        picked = jnp.sum(jnp.where(entries == wanted[...], logits, 0.0), axis=1, keepdims=True)
        top = jnp.max(logits, axis=1, keepdims=True)
        total = jnp.sum(jnp.exp(logits - top), axis=1, keepdims=True)
        table = jnp.where(lane == m, top, table)
        table = jnp.where(lane == 2 + m, total, table)
        table = jnp.where(lane == 4 + m, picked, table)
    stats[...] = jnp.transpose(table)[:8]


def merge(tables):
    top = functools.reduce(jnp.maximum, [t[0:2] for t in tables])
    total = sum(t[2:4] * jnp.exp(t[0:2] - top) for t in tables)
    return top, total, sum(t[4:6] for t in tables)


def merge_kernel(ids, *refs):
    out = refs[-1]
    out[0:2], out[2:4], out[4:6] = merge(refs[:-1])
    out[6:8] = jnp.zeros((2, out.shape[1]), jnp.float32)


def last_kernel(ids, *refs):
    out = refs[-1]
    top, total, picked = merge(refs[:-1])
    logprob = picked - (top + jnp.log(total))
    out[...] = logprob[0:1] - logprob[1:2]


def local(
    hidden_policy,
    hidden_reference,
    ffn_gain_policy,
    ffn_gain_reference,
    up_policy,
    up_reference,
    down_policy,
    down_reference,
    final_gain_policy,
    final_gain_reference,
    out_policy,
    out_reference,
    move_plan,
    lengths,
    targets,
):
    dp = lax.axis_size("dp")
    mp = lax.axis_size("mp")
    half = mp // 2
    dp_index = lax.axis_index("dp")
    mp_index = lax.axis_index("mp")
    ids = jnp.stack([dp_index, mp_index // 2, mp_index % 2, mp_index]).astype(jnp.int32)
    reqs, slots, part = hidden_policy.shape
    here = reqs * slots
    rows = here // 2
    ffn_gains = (ffn_gain_policy, ffn_gain_reference)
    final_gains = (final_gain_policy, final_gain_reference)
    gains = [gain.reshape(mp, 1, part) for gain in (*ffn_gains, *final_gains)]
    bits = [1 << b for b in range(dp.bit_length() - 1)]

    bit_orders = []
    for m in range(2):
        bit_orders.append([bits[(b ^ m) if (b ^ m) < len(bits) else b] for b in range(len(bits))])

    def spread_step(blocks, step, places):
        for m in range(2):
            bit = bit_orders[m][step]
            for k in [k for k in blocks[m] if places(m, k)]:
                blocks[m][k ^ bit] = exchange(blocks[m][k], "dp", bit)

    packed = call(
        pack_kernel,
        jax.ShapeDtypeStruct((reqs + 1, slots, part), jnp.bfloat16),
        (lengths, targets, hidden_reference),
        [
            pltpu.SMEM(lengths.shape, jnp.int32),
            pltpu.VMEM(targets.shape, jnp.int32),
            pltpu.SemaphoreType.DMA((3,)),
        ],
        far=(0, 1, 2),
    )
    hiddens = [{0: hidden_policy}, {0: packed}]
    outs = [{0: out_policy}, {0: out_reference}]

    def wait_for(first, places):
        flat = [(m, k) for m in range(2) for k in outs[m] if places(m, k)]
        first, values = lax.optimization_barrier((first, [outs[m][k] for m, k in flat]))
        for (m, k), value in zip(flat, values):
            outs[m][k] = value
        return first

    for step in range(len(bits)):
        spread_step(hiddens, step, lambda m, k: True)
    hiddens = wait_for(hiddens, lambda m, k: True)
    spread_step(outs, 0, lambda m, k: True)
    hidden_parts = [hiddens[m][k] for m in range(2) for k in range(dp)]

    order = jnp.arange(dp, dtype=jnp.int32)
    moved, facts = call(
        functools.partial(select_kernel, dp),
        (
            jax.ShapeDtypeStruct((2, rows, part), jnp.bfloat16),
            jax.ShapeDtypeStruct((dp, reqs, part), jnp.float32),
        ),
        (ids, move_plan, *hidden_parts),
        [
            pltpu.VMEM(hidden_policy.shape, jnp.bfloat16),
            pltpu.SMEM(move_plan.shape, jnp.int32),
            pltpu.SemaphoreType.DMA((2,)),
        ],
        far=(1, 2),
    )

    facts = facts[:, :, : 2 * slots + 1].astype(jnp.int32)
    all_lengths = facts[:, :, 0].reshape(-1)
    all_targets = (facts[:, :, 1 : slots + 1] * 128 + facts[:, :, slots + 1 :]).reshape(-1)
    slot_ids = ((order ^ dp_index)[:, None] * reqs + jnp.arange(reqs, dtype=jnp.int32)).reshape(-1)
    positions = jnp.arange(slots, dtype=jnp.int32)

    def codes(slot):
        start = jnp.sum(jnp.where(slot_ids[None] < slot[:, None], all_lengths[None], 0), axis=1)
        live = jnp.sum(jnp.where(slot_ids[None] == slot[:, None], all_lengths[None], 0), axis=1)
        return jnp.where(
            positions[None] < live[:, None], start[:, None] + positions[None], jnp.int32(-1)
        )

    far = sorted(range(1, half), key=lambda k: (k.bit_length() <= 1, k))

    def gather_pair(own):
        same = {0: own}
        for k in far:
            same[k] = exchange(own, "mp", 2 * k)
        same = [same[k] for k in range(half)]
        return same + [exchange(v, "mp", 1) for v in same]

    parts = gather_pair(moved)
    if len(bits) > 1:
        parts[-1] = wait_for(parts[-1], lambda m, k: k == 0)
        later = [{0: outs[m][0]} for m in range(2)]
        spread_step(later, 1, lambda m, k: True)
    gain_scratch = pltpu.VMEM((2, mp, 1, part), jnp.float32)
    block = jax.ShapeDtypeStruct((2, rows, part), jnp.bfloat16)
    keep, send = call(
        functools.partial(ffn_kernel, half),
        (
            jax.ShapeDtypeStruct((half, 2, rows, part), jnp.float32),
            jax.ShapeDtypeStruct((half, 2, rows, part), jnp.bfloat16),
        ),
        (ids, *gains[:2], up_policy, up_reference, down_policy, down_reference, *parts),
        [
            gain_scratch,
            pltpu.VMEM((2,) + up_policy.shape, jnp.bfloat16),
            pltpu.VMEM((2,) + down_policy.shape, jnp.bfloat16),
            pltpu.VMEM((2, mp, rows, part), jnp.bfloat16),
            pltpu.VMEM((2, mp, rows, part), jnp.float32),
            pltpu.SemaphoreType.DMA((6,)),
        ],
        far=range(1, 7),
        mib=22,
    )
    send = wait_for(send, lambda m, k: k > 0)
    came = exchange(send, "mp", 1)
    own, *pieces = call(
        pair_kernel,
        (jax.ShapeDtypeStruct((2, rows, part), jnp.float32),) + (block,) * (half - 1),
        (ids, keep, came),
    )
    arrived = {k: exchange(pieces[k - 1], "mp", 2 * k) for k in far}
    if len(bits) > 1:
        for m in range(2):
            outs[m].update(later[m])
        arrived[far[0]] = wait_for(arrived[far[0]], lambda m, k: True)
        spread_step(outs, 1, lambda m, k: k == bit_orders[m][0])
    for k in range(1, half):
        own = own + arrived[k].astype(jnp.float32)
    stream = own.astype(jnp.bfloat16)
    for step in range(2, len(bits)):
        stream = wait_for(stream, lambda m, k: True)
        spread_step(outs, step, lambda m, k: True)

    owner_code = codes(slot_ids).reshape(-1)
    my_ranks = dp_index * rows + jnp.arange(rows, dtype=jnp.int32)
    wanted = jnp.sum(
        jnp.where(owner_code[None] == my_ranks[:, None], all_targets[None], 0),
        axis=1,
        keepdims=True,
    )
    partial, tail = call(
        functools.partial(score_kernel, half, dp),
        (
            jax.ShapeDtypeStruct((2, rows, out_policy.shape[1]), jnp.float32),
            jax.ShapeDtypeStruct((2, rows, out_policy.shape[0]), jnp.bfloat16),
        ),
        (
            ids,
            *gains[2:],
            *gather_pair(stream),
            *[outs[m][k] for m in range(2) for k in range(dp - 1)],
        ),
        [
            gain_scratch,
            pltpu.VMEM((2, mp, rows, part), jnp.bfloat16),
            pltpu.VMEM((2,) + out_policy.shape, jnp.bfloat16),
            pltpu.SemaphoreType.DMA((4,)),
        ],
        far=(1, 2, 3 + mp, 2 + mp + dp),
        mib=14,
    )
    stats = call(
        finish_kernel,
        jax.ShapeDtypeStruct((8, rows), jnp.float32),
        (ids, wanted, partial, tail, outs[0][dp - 1], outs[1][dp - 1]),
        mib=8,
    )
    stats = call(
        merge_kernel,
        jax.ShapeDtypeStruct((8, rows), jnp.float32),
        (ids, stats, exchange(stats, "mp", 1)),
    )
    diff = call(
        last_kernel,
        jax.ShapeDtypeStruct((1, rows), jnp.float32),
        (ids, stats, *[exchange(stats, "mp", 2 * k) for k in far]),
    )
    diff = jnp.concatenate([diff] + [exchange(diff, "dp", k) for k in range(1, dp)])
    ranks = ((order ^ dp_index)[:, None] * rows + jnp.arange(rows, dtype=jnp.int32)).reshape(-1)
    my_code = codes(dp_index * reqs + jnp.arange(reqs, dtype=jnp.int32))
    hit = my_code[:, :, None] == ranks[None, None]
    token_diff = jnp.sum(jnp.where(hit, diff.reshape(1, 1, -1), 0.0), axis=2)
    return (token_diff, jnp.sum(token_diff, axis=1))


def solution(mesh):
    return jax.shard_map(
        local,
        mesh=mesh,
        in_specs=(
            P("dp", None, "mp"),
            P("dp", None, "mp"),
            P(),
            P(),
            P(None, "mp"),
            P(None, "mp"),
            P("mp", None),
            P("mp", None),
            P(),
            P(),
            P("dp", "mp"),
            P("dp", "mp"),
            P(),
            P("dp"),
            P("dp", None),
        ),
        out_specs=(P("dp", None), P("dp")),
        check_vma=False,
    )
```

```python
import functools

import jax
import jax.numpy as jnp
from jax import lax
from jax.experimental import pallas as pl
from jax.experimental.pallas import tpu as pltpu
from jax.sharding import PartitionSpec as P

epsilon = 1e-05
vmem = pl.BlockSpec(memory_space=pltpu.VMEM)
smem = pl.BlockSpec(memory_space=pltpu.SMEM)
anywhere = pl.BlockSpec(memory_space=pltpu.HBM)


def call(kernel, out_shape, ops, scratch=(), far=(), mib=4):
    specs = [anywhere if i in far else vmem if i else smem for i in range(len(ops))]
    ops = [
        pltpu.with_memory_space_constraint(op, pltpu.HBM) if i in far else op
        for i, op in enumerate(ops)
    ]
    return pl.pallas_call(
        kernel,
        out_shape=out_shape,
        in_specs=specs,
        out_specs=jax.tree.map(lambda _: vmem, out_shape),
        scratch_shapes=list(scratch),
        compiler_params=pltpu.CompilerParams(vmem_limit_bytes=mib * 1024 * 1024),
    )(*ops)


def exchange(values, axis, flip):
    count = lax.axis_size(axis)
    return lax.ppermute(values, axis, [(i, i ^ flip) for i in range(count)])


def fetch(sources, targets, sems):
    copies = [
        pltpu.make_async_copy(source, target, sems.at[i])
        for i, (source, target) in enumerate(zip(sources, targets))
    ]
    for copy in copies:
        copy.start()
    return copies


def pack_kernel(lengths_far, targets_far, hidden, out, lengths, targets, sems):
    reqs = hidden.shape[0]
    copies = fetch(
        [lengths_far, targets_far, hidden], [lengths, targets, out.at[pl.ds(0, reqs)]], sems
    )
    copies[1].wait()
    slots, part = targets.shape[1], hidden.shape[2]
    row = lax.broadcasted_iota(jnp.int32, (slots, part), 0)
    lane = lax.broadcasted_iota(jnp.int32, (slots, part), 1)
    high = lax.shift_right_logical(targets[...], 7)
    low = targets[...] - high * 128
    block = jnp.zeros((reqs, part), jnp.float32)
    for first, values in ((1, high), (1 + slots, low)):
        spot = (lane == row + first).astype(jnp.float32).astype(jnp.bfloat16)
        values = values.astype(jnp.float32).astype(jnp.bfloat16)
        block = block + jnp.dot(values, spot, preferred_element_type=jnp.float32)
    row = lax.broadcasted_iota(jnp.int32, (reqs, part), 0)
    lane = lax.broadcasted_iota(jnp.int32, (reqs, part), 1)
    copies[0].wait()
    for r in range(reqs):
        here = jnp.logical_and(row == r, lane == 0)
        block = jnp.where(here, lengths[r].astype(jnp.float32), block)
    out[reqs] = block.astype(jnp.bfloat16)
    copies[2].wait()


def select_kernel(dp, ids, plan_far, *refs):
    parts, (out, facts, own, plan, sems) = list(refs[: 2 * dp]), refs[2 * dp :]
    plan_copy, copy = fetch([plan_far, parts[0]], [plan, own], sems)
    parts[0] = own
    rows = out.shape[1]
    reqs, slots, _ = own.shape
    here = reqs * slots
    me = ids[0]
    for k in range(dp):
        facts[k] = parts[dp + k][reqs].astype(jnp.float32)
    lengths = [facts[k][:, 0:1].astype(jnp.int32) for k in range(dp)]
    lengths = jnp.concatenate(lengths, axis=0)
    row = lax.broadcasted_iota(jnp.int32, (reqs, here), 0)
    slot = jnp.concatenate([row + (me ^ k) * reqs for k in range(dp)], axis=0)
    position = lax.rem(lax.broadcasted_iota(jnp.int32, (1, here), 1), slots)
    wanted = me * rows + lax.broadcasted_iota(jnp.int32, (rows, here), 0)
    request = lax.div(lax.broadcasted_iota(jnp.int32, (1, here), 1), slots)
    hots = []
    plan_copy.wait()
    for k in range(dp):
        owner = jnp.zeros((1, here), jnp.int32)
        for r in range(reqs):
            owner = jnp.where(request == r, plan[(me ^ k) * reqs + r], owner)
        start = jnp.sum(jnp.where(slot < owner, lengths, 0), axis=0, keepdims=True)
        live = jnp.sum(jnp.where(slot == owner, lengths, 0), axis=0, keepdims=True)
        code = jnp.where(position < live, start + position, -1)
        hots.append((code == wanted).astype(jnp.float32).astype(jnp.bfloat16))
    copy.wait()
    for m in range(2):
        total = None
        for k in range(dp):
            values = parts[m * dp + k][0:reqs]
            values = values.reshape(-1, values.shape[-1])
            found = jnp.dot(hots[k], values, preferred_element_type=jnp.float32)
            total = found if total is None else total + found
        out[m] = total.astype(out.dtype)


def normalise(values, gain, chip, core, store, copy):
    half = len(values) // 2
    part = values[0].shape[1]
    width = part * len(values)
    values = [v.astype(jnp.float32) for v in values]
    center = sum(jnp.sum(v, axis=1, keepdims=True) for v in values) / width
    values = [v - center for v in values]
    spread = sum(jnp.sum(v * v, axis=1, keepdims=True) for v in values) / width
    scale = lax.rsqrt(spread + epsilon)
    copy.wait()
    for k, v in enumerate(values):
        place = 2 * (chip ^ (k % half)) + (core if k < half else 1 - core)
        store[place] = (v * scale * gain[place]).astype(jnp.bfloat16)
    return values[0]


def blocks_dot(normed, weight, order):
    part = normed.shape[2]
    total = None
    for b, place in enumerate(order):
        rows = weight[b * part : (b + 1) * part, :]
        piece = jnp.dot(normed[place], rows, preferred_element_type=jnp.float32)
        total = piece if total is None else total + piece
    return total


def ffn_kernel(half, ids, *refs):
    parts = refs[6 : 6 + 2 * half]
    keep, send, gains, ups, downs, normed, terms, sems = refs[6 + 2 * half :]
    copies = fetch(
        refs[:6], [store.at[m] for store in (gains, ups, downs) for m in range(2)], sems
    )
    chip, core = ids[1], ids[2]
    part = parts[0].shape[2]
    bases = [
        normalise([part[m] for part in parts], gains.at[m], chip, core, normed.at[m], copies[m])
        for m in range(2)
    ]
    for m in range(2):
        copies[2 + m].wait()
        pre = blocks_dot(normed.at[m], ups.at[m], range(2 * half))
        units = jax.nn.gelu(pre).astype(jnp.bfloat16)
        copies[4 + m].wait()
        full = jnp.dot(units, downs[m], preferred_element_type=jnp.float32)
        for b in range(2 * half):
            terms[m, b] = full[:, b * part : (b + 1) * part]
        for k in range(half):
            place = 2 * (chip ^ k)
            kept = terms[m, place + core]
            keep[k, m] = kept + bases[m] if k == 0 else kept
            send[k, m] = terms[m, place + 1 - core].astype(jnp.bfloat16)


def pair_kernel(ids, keep, came, own, *outs):
    own[...] = keep[0] + came[0].astype(jnp.float32)
    for k, out in enumerate(outs):
        out[...] = (keep[k + 1] + came[k + 1].astype(jnp.float32)).astype(jnp.bfloat16)


def score_kernel(half, dp, ids, *refs):
    parts = refs[2 : 2 + 2 * half]
    *outs, partial, tail, gains, normed, out_store, sems = refs[2 + 2 * half :]
    here = dp - 1
    copies = fetch(
        [refs[0], refs[1], outs[0], outs[here]],
        [store.at[m] for store in (gains, out_store) for m in range(2)],
        sems,
    )
    me, chip, core = ids[0], ids[1], ids[2]
    ratio = 2 * half // dp
    part = parts[0].shape[2]
    for m in range(2):
        values = [part[m] for part in parts]
        normalise(values, gains.at[m], chip, core, normed.at[m], copies[m])
        for b in range(ratio):
            tail[m, :, b * part : (b + 1) * part] = normed[m, (me ^ here) * ratio + b]
    for m in range(2):
        logits = None
        for k in [*range(1, here), 0]:
            if k == 0:
                copies[2 + m].wait()
                outs[m * here] = out_store.at[m]
            order = [(me ^ k) * ratio + b for b in range(ratio)]
            piece = blocks_dot(normed.at[m], outs[m * here + k], order)
            logits = piece if logits is None else logits + piece
        partial[m] = logits


def finish_kernel(ids, wanted, partial, tail, last_policy, last_reference, stats):
    lane = lax.broadcasted_iota(jnp.int32, (tail.shape[1], 128), 1)
    table = jnp.zeros(lane.shape, jnp.float32)
    for m, last in enumerate((last_policy, last_reference)):
        logits = partial[m] + jnp.dot(tail[m], last[...], preferred_element_type=jnp.float32)
        entries = lax.broadcasted_iota(jnp.int32, logits.shape, 1) + ids[3] * logits.shape[1]
        picked = jnp.sum(jnp.where(entries == wanted[...], logits, 0.0), axis=1, keepdims=True)
        top = jnp.max(logits, axis=1, keepdims=True)
        total = jnp.sum(jnp.exp(logits - top), axis=1, keepdims=True)
        table = jnp.where(lane == m, top, table)
        table = jnp.where(lane == 2 + m, total, table)
        table = jnp.where(lane == 4 + m, picked, table)
    stats[...] = jnp.transpose(table)[:8]


def merge(tables):
    top = functools.reduce(jnp.maximum, [t[0:2] for t in tables])
    total = sum(t[2:4] * jnp.exp(t[0:2] - top) for t in tables)
    return top, total, sum(t[4:6] for t in tables)


def merge_kernel(ids, *refs):
    out = refs[-1]
    out[0:2], out[2:4], out[4:6] = merge(refs[:-1])
    out[6:8] = jnp.zeros((2, out.shape[1]), jnp.float32)


def last_kernel(ids, *refs):
    out = refs[-1]
    top, total, picked = merge(refs[:-1])
    logprob = picked - (top + jnp.log(total))
    out[...] = logprob[0:1] - logprob[1:2]


def local(
    hidden_policy,
    hidden_reference,
    ffn_gain_policy,
    ffn_gain_reference,
    up_policy,
    up_reference,
    down_policy,
    down_reference,
    final_gain_policy,
    final_gain_reference,
    out_policy,
    out_reference,
    move_plan,
    lengths,
    targets,
):
    dp = lax.axis_size("dp")
    mp = lax.axis_size("mp")
    half = mp // 2
    dp_index = lax.axis_index("dp")
    mp_index = lax.axis_index("mp")
    ids = jnp.stack([dp_index, mp_index // 2, mp_index % 2, mp_index]).astype(jnp.int32)
    reqs, slots, part = hidden_policy.shape
    here = reqs * slots
    rows = here // 2
    ffn_gains = (ffn_gain_policy, ffn_gain_reference)
    final_gains = (final_gain_policy, final_gain_reference)
    gains = [gain.reshape(mp, 1, part) for gain in (*ffn_gains, *final_gains)]
    bits = [1 << b for b in range(dp.bit_length() - 1)]

    bit_orders = []
    for m in range(2):
        bit_orders.append([bits[(b ^ m) if (b ^ m) < len(bits) else b] for b in range(len(bits))])

    def spread_step(blocks, step, places):
        for m in range(2):
            bit = bit_orders[m][step]
            for k in [k for k in blocks[m] if places(m, k)]:
                blocks[m][k ^ bit] = exchange(blocks[m][k], "dp", bit)

    packed = call(
        pack_kernel,
        jax.ShapeDtypeStruct((reqs + 1, slots, part), jnp.bfloat16),
        (lengths, targets, hidden_reference),
        [
            pltpu.SMEM(lengths.shape, jnp.int32),
            pltpu.VMEM(targets.shape, jnp.int32),
            pltpu.SemaphoreType.DMA((3,)),
        ],
        far=(0, 1, 2),
    )
    hiddens = [{0: hidden_policy}, {0: packed}]
    outs = [{0: out_policy}, {0: out_reference}]

    def wait_for(first, places):
        flat = [(m, k) for m in range(2) for k in outs[m] if places(m, k)]
        first, values = lax.optimization_barrier((first, [outs[m][k] for m, k in flat]))
        for (m, k), value in zip(flat, values):
            outs[m][k] = value
        return first

    for step in range(len(bits)):
        spread_step(hiddens, step, lambda m, k: k == 0)
        if step:
            blocks, place = hiddens[0], bit_orders[0][step]
            passed = [k for k in blocks if 0 < k and not k & place]
            values = [blocks[k] for k in passed]
            blocks[place], values = lax.optimization_barrier((blocks[place], values))
            blocks.update(zip(passed, values))
        spread_step(hiddens, step, lambda m, k: 0 < k and not k & bit_orders[m][step])
    hiddens = wait_for(hiddens, lambda m, k: True)
    spread_step(outs, 0, lambda m, k: True)
    hidden_parts = [hiddens[m][k] for m in range(2) for k in range(dp)]

    order = jnp.arange(dp, dtype=jnp.int32)
    moved, facts = call(
        functools.partial(select_kernel, dp),
        (
            jax.ShapeDtypeStruct((2, rows, part), jnp.bfloat16),
            jax.ShapeDtypeStruct((dp, reqs, part), jnp.float32),
        ),
        (ids, move_plan, *hidden_parts),
        [
            pltpu.VMEM(hidden_policy.shape, jnp.bfloat16),
            pltpu.SMEM(move_plan.shape, jnp.int32),
            pltpu.SemaphoreType.DMA((2,)),
        ],
        far=(1, 2),
    )

    facts = facts[:, :, : 2 * slots + 1].astype(jnp.int32)
    all_lengths = facts[:, :, 0].reshape(-1)
    all_targets = (facts[:, :, 1 : slots + 1] * 128 + facts[:, :, slots + 1 :]).reshape(-1)
    slot_ids = ((order ^ dp_index)[:, None] * reqs + jnp.arange(reqs, dtype=jnp.int32)).reshape(-1)
    positions = jnp.arange(slots, dtype=jnp.int32)

    def codes(slot):
        start = jnp.sum(jnp.where(slot_ids[None] < slot[:, None], all_lengths[None], 0), axis=1)
        live = jnp.sum(jnp.where(slot_ids[None] == slot[:, None], all_lengths[None], 0), axis=1)
        return jnp.where(
            positions[None] < live[:, None], start[:, None] + positions[None], jnp.int32(-1)
        )

    far = sorted(range(1, half), key=lambda k: (k.bit_length() <= 1, k))

    def gather_pair(own):
        same = {0: own}
        for k in far:
            same[k] = exchange(own, "mp", 2 * k)
        same = [same[k] for k in range(half)]
        return same + [exchange(v, "mp", 1) for v in same]

    parts = gather_pair(moved)
    if len(bits) > 1:
        parts[-1] = wait_for(parts[-1], lambda m, k: k == 0)
        later = [{0: outs[m][0]} for m in range(2)]
        spread_step(later, 1, lambda m, k: True)
    gain_scratch = pltpu.VMEM((2, mp, 1, part), jnp.float32)
    block = jax.ShapeDtypeStruct((2, rows, part), jnp.bfloat16)
    keep, send = call(
        functools.partial(ffn_kernel, half),
        (
            jax.ShapeDtypeStruct((half, 2, rows, part), jnp.float32),
            jax.ShapeDtypeStruct((half, 2, rows, part), jnp.bfloat16),
        ),
        (ids, *gains[:2], up_policy, up_reference, down_policy, down_reference, *parts),
        [
            gain_scratch,
            pltpu.VMEM((2,) + up_policy.shape, jnp.bfloat16),
            pltpu.VMEM((2,) + down_policy.shape, jnp.bfloat16),
            pltpu.VMEM((2, mp, rows, part), jnp.bfloat16),
            pltpu.VMEM((2, mp, rows, part), jnp.float32),
            pltpu.SemaphoreType.DMA((6,)),
        ],
        far=range(1, 7),
        mib=22,
    )
    send = wait_for(send, lambda m, k: k > 0)
    came = exchange(send, "mp", 1)
    own, *pieces = call(
        pair_kernel,
        (jax.ShapeDtypeStruct((2, rows, part), jnp.float32),) + (block,) * (half - 1),
        (ids, keep, came),
    )
    arrived = {k: exchange(pieces[k - 1], "mp", 2 * k) for k in far}
    if len(bits) > 1:
        for m in range(2):
            outs[m].update(later[m])
        arrived[far[0]] = wait_for(arrived[far[0]], lambda m, k: True)
        spread_step(outs, 1, lambda m, k: k == bit_orders[m][0])
    for k in range(1, half):
        own = own + arrived[k].astype(jnp.float32)
    stream = own.astype(jnp.bfloat16)
    for step in range(2, len(bits)):
        stream = wait_for(stream, lambda m, k: True)
        spread_step(outs, step, lambda m, k: True)

    owner_code = codes(slot_ids).reshape(-1)
    my_ranks = dp_index * rows + jnp.arange(rows, dtype=jnp.int32)
    wanted = jnp.sum(
        jnp.where(owner_code[None] == my_ranks[:, None], all_targets[None], 0),
        axis=1,
        keepdims=True,
    )
    partial, tail = call(
        functools.partial(score_kernel, half, dp),
        (
            jax.ShapeDtypeStruct((2, rows, out_policy.shape[1]), jnp.float32),
            jax.ShapeDtypeStruct((2, rows, out_policy.shape[0]), jnp.bfloat16),
        ),
        (
            ids,
            *gains[2:],
            *gather_pair(stream),
            *[outs[m][k] for m in range(2) for k in range(dp - 1)],
        ),
        [
            gain_scratch,
            pltpu.VMEM((2, mp, rows, part), jnp.bfloat16),
            pltpu.VMEM((2,) + out_policy.shape, jnp.bfloat16),
            pltpu.SemaphoreType.DMA((4,)),
        ],
        far=(1, 2, 3 + mp, 2 + mp + dp),
        mib=14,
    )
    stats = call(
        finish_kernel,
        jax.ShapeDtypeStruct((8, rows), jnp.float32),
        (ids, wanted, partial, tail, outs[0][dp - 1], outs[1][dp - 1]),
        mib=8,
    )
    stats = call(
        merge_kernel,
        jax.ShapeDtypeStruct((8, rows), jnp.float32),
        (ids, stats, exchange(stats, "mp", 1)),
    )
    diff = call(
        last_kernel,
        jax.ShapeDtypeStruct((1, rows), jnp.float32),
        (ids, stats, *[exchange(stats, "mp", 2 * k) for k in far]),
    )
    diff = jnp.concatenate([diff] + [exchange(diff, "dp", k) for k in range(1, dp)])
    ranks = ((order ^ dp_index)[:, None] * rows + jnp.arange(rows, dtype=jnp.int32)).reshape(-1)
    my_code = codes(dp_index * reqs + jnp.arange(reqs, dtype=jnp.int32))
    hit = my_code[:, :, None] == ranks[None, None]
    token_diff = jnp.sum(jnp.where(hit, diff.reshape(1, 1, -1), 0.0), axis=2)
    return (token_diff, jnp.sum(token_diff, axis=1))


def solution(mesh):
    return jax.shard_map(
        local,
        mesh=mesh,
        in_specs=(
            P("dp", None, "mp"),
            P("dp", None, "mp"),
            P(),
            P(),
            P(None, "mp"),
            P(None, "mp"),
            P("mp", None),
            P("mp", None),
            P(),
            P(),
            P("dp", "mp"),
            P("dp", "mp"),
            P(),
            P("dp"),
            P("dp", None),
        ),
        out_specs=(P("dp", None), P("dp")),
        check_vma=False,
    )
```

```python
import functools

import jax
import jax.numpy as jnp
from jax import lax
from jax.experimental import pallas as pl
from jax.experimental.pallas import tpu as pltpu
from jax.sharding import PartitionSpec as P

epsilon = 1e-05
vmem = pl.BlockSpec(memory_space=pltpu.VMEM)
smem = pl.BlockSpec(memory_space=pltpu.SMEM)
anywhere = pl.BlockSpec(memory_space=pltpu.HBM)


def call(kernel, out_shape, ops, scratch=(), far=(), mib=4, cost=None):
    specs = [anywhere if i in far else vmem if i else smem for i in range(len(ops))]
    ops = [
        pltpu.with_memory_space_constraint(op, pltpu.HBM) if i in far else op
        for i, op in enumerate(ops)
    ]
    return pl.pallas_call(
        kernel,
        out_shape=out_shape,
        in_specs=specs,
        out_specs=jax.tree.map(lambda _: vmem, out_shape),
        scratch_shapes=list(scratch),
        cost_estimate=cost and pl.CostEstimate(flops=cost, bytes_accessed=0, transcendentals=0),
        compiler_params=pltpu.CompilerParams(vmem_limit_bytes=mib * 1024 * 1024),
    )(*ops)


def exchange(values, axis, flip):
    count = lax.axis_size(axis)
    return lax.ppermute(values, axis, [(i, i ^ flip) for i in range(count)])


def fetch(sources, targets, sems):
    copies = [
        pltpu.make_async_copy(source, target, sems.at[i])
        for i, (source, target) in enumerate(zip(sources, targets))
    ]
    for copy in copies:
        copy.start()
    return copies


def pack_kernel(lengths_far, targets_far, hidden, out, lengths, targets, sems):
    reqs = hidden.shape[0]
    copies = fetch(
        [lengths_far, targets_far, hidden], [lengths, targets, out.at[pl.ds(0, reqs)]], sems
    )
    copies[1].wait()
    slots, part = targets.shape[1], hidden.shape[2]
    row = lax.broadcasted_iota(jnp.int32, (slots, part), 0)
    lane = lax.broadcasted_iota(jnp.int32, (slots, part), 1)
    high = lax.shift_right_logical(targets[...], 7)
    low = targets[...] - high * 128
    block = jnp.zeros((reqs, part), jnp.float32)
    for first, values in ((1, high), (1 + slots, low)):
        spot = (lane == row + first).astype(jnp.float32).astype(jnp.bfloat16)
        values = values.astype(jnp.float32).astype(jnp.bfloat16)
        block = block + jnp.dot(values, spot, preferred_element_type=jnp.float32)
    row = lax.broadcasted_iota(jnp.int32, (reqs, part), 0)
    lane = lax.broadcasted_iota(jnp.int32, (reqs, part), 1)
    copies[0].wait()
    for r in range(reqs):
        here = jnp.logical_and(row == r, lane == 0)
        block = jnp.where(here, lengths[r].astype(jnp.float32), block)
    out[reqs] = block.astype(jnp.bfloat16)
    copies[2].wait()


def select_kernel(dp, ids, plan_far, *refs):
    parts, (out, facts, own, plan, sems) = list(refs[: 2 * dp]), refs[2 * dp :]
    plan_copy, copy = fetch([plan_far, parts[0]], [plan, own], sems)
    parts[0] = own
    rows = out.shape[1]
    reqs, slots, _ = own.shape
    here = reqs * slots
    me = ids[0]
    for k in range(dp):
        facts[k] = parts[dp + k][reqs].astype(jnp.float32)
    lengths = [facts[k][:, 0:1].astype(jnp.int32) for k in range(dp)]
    lengths = jnp.concatenate(lengths, axis=0)
    row = lax.broadcasted_iota(jnp.int32, (reqs, here), 0)
    slot = jnp.concatenate([row + (me ^ k) * reqs for k in range(dp)], axis=0)
    position = lax.rem(lax.broadcasted_iota(jnp.int32, (1, here), 1), slots)
    wanted = me * rows + lax.broadcasted_iota(jnp.int32, (rows, here), 0)
    request = lax.div(lax.broadcasted_iota(jnp.int32, (1, here), 1), slots)
    hots = []
    plan_copy.wait()
    for k in range(dp):
        owner = jnp.zeros((1, here), jnp.int32)
        for r in range(reqs):
            owner = jnp.where(request == r, plan[(me ^ k) * reqs + r], owner)
        start = jnp.sum(jnp.where(slot < owner, lengths, 0), axis=0, keepdims=True)
        live = jnp.sum(jnp.where(slot == owner, lengths, 0), axis=0, keepdims=True)
        code = jnp.where(position < live, start + position, -1)
        hots.append((code == wanted).astype(jnp.float32).astype(jnp.bfloat16))
    copy.wait()
    for m in range(2):
        total = None
        for k in range(dp):
            values = parts[m * dp + k][0:reqs]
            values = values.reshape(-1, values.shape[-1])
            found = jnp.dot(hots[k], values, preferred_element_type=jnp.float32)
            total = found if total is None else total + found
        out[m] = total.astype(out.dtype)


def normalise(values, gain, chip, core, store, copy):
    half = len(values) // 2
    part = values[0].shape[1]
    width = part * len(values)
    values = [v.astype(jnp.float32) for v in values]
    center = sum(jnp.sum(v, axis=1, keepdims=True) for v in values) / width
    values = [v - center for v in values]
    spread = sum(jnp.sum(v * v, axis=1, keepdims=True) for v in values) / width
    scale = lax.rsqrt(spread + epsilon)
    copy.wait()
    for k, v in enumerate(values):
        place = 2 * (chip ^ (k % half)) + (core if k < half else 1 - core)
        store[place] = (v * scale * gain[place]).astype(jnp.bfloat16)
    return values[0]


def blocks_dot(normed, weight, order):
    part = normed.shape[2]
    total = None
    for b, place in enumerate(order):
        rows = weight[b * part : (b + 1) * part, :]
        piece = jnp.dot(normed[place], rows, preferred_element_type=jnp.float32)
        total = piece if total is None else total + piece
    return total


def ffn_kernel(half, ids, *refs):
    parts = refs[6 : 6 + 2 * half]
    keep, send, gains, ups, downs, normed, terms, sems = refs[6 + 2 * half :]
    copies = fetch(
        refs[:6], [store.at[m] for store in (gains, ups, downs) for m in range(2)], sems
    )
    chip, core = ids[1], ids[2]
    part = parts[0].shape[2]
    bases = [
        normalise([part[m] for part in parts], gains.at[m], chip, core, normed.at[m], copies[m])
        for m in range(2)
    ]
    for m in range(2):
        copies[2 + m].wait()
        pre = blocks_dot(normed.at[m], ups.at[m], range(2 * half))
        units = jax.nn.gelu(pre).astype(jnp.bfloat16)
        copies[4 + m].wait()
        full = jnp.dot(units, downs[m], preferred_element_type=jnp.float32)
        for b in range(2 * half):
            terms[m, b] = full[:, b * part : (b + 1) * part]
        for k in range(half):
            place = 2 * (chip ^ k)
            kept = terms[m, place + core]
            keep[k, m] = kept + bases[m] if k == 0 else kept
            send[k, m] = terms[m, place + 1 - core].astype(jnp.bfloat16)


def pair_kernel(ids, keep, came, own, *outs):
    own[...] = keep[0] + came[0].astype(jnp.float32)
    for k, out in enumerate(outs):
        out[...] = (keep[k + 1] + came[k + 1].astype(jnp.float32)).astype(jnp.bfloat16)


def score_kernel(half, dp, ids, *refs):
    parts = refs[2 : 2 + 2 * half]
    *outs, partial, tail, gains, normed, out_store, sems = refs[2 + 2 * half :]
    here = dp - 1
    copies = fetch(
        [refs[0], refs[1], outs[0], outs[here]],
        [store.at[m] for store in (gains, out_store) for m in range(2)],
        sems,
    )
    me, chip, core = ids[0], ids[1], ids[2]
    ratio = 2 * half // dp
    part = parts[0].shape[2]
    for m in range(2):
        values = [part[m] for part in parts]
        normalise(values, gains.at[m], chip, core, normed.at[m], copies[m])
        for b in range(ratio):
            tail[m, :, b * part : (b + 1) * part] = normed[m, (me ^ here) * ratio + b]
    for m in range(2):
        logits = None
        for k in [*range(1, here), 0]:
            if k == 0:
                copies[2 + m].wait()
                outs[m * here] = out_store.at[m]
            order = [(me ^ k) * ratio + b for b in range(ratio)]
            piece = blocks_dot(normed.at[m], outs[m * here + k], order)
            logits = piece if logits is None else logits + piece
        partial[m] = logits


def finish_kernel(ids, wanted, partial, tail, last_policy, last_reference, stats):
    lane = lax.broadcasted_iota(jnp.int32, (tail.shape[1], 128), 1)
    table = jnp.zeros(lane.shape, jnp.float32)
    for m, last in enumerate((last_policy, last_reference)):
        logits = partial[m] + jnp.dot(tail[m], last[...], preferred_element_type=jnp.float32)
        entries = lax.broadcasted_iota(jnp.int32, logits.shape, 1) + ids[3] * logits.shape[1]
        picked = jnp.sum(jnp.where(entries == wanted[...], logits, 0.0), axis=1, keepdims=True)
        top = jnp.max(logits, axis=1, keepdims=True)
        total = jnp.sum(jnp.exp(logits - top), axis=1, keepdims=True)
        table = jnp.where(lane == m, top, table)
        table = jnp.where(lane == 2 + m, total, table)
        table = jnp.where(lane == 4 + m, picked, table)
    stats[...] = jnp.transpose(table)[:8]


def merge(tables):
    top = functools.reduce(jnp.maximum, [t[0:2] for t in tables])
    total = sum(t[2:4] * jnp.exp(t[0:2] - top) for t in tables)
    return top, total, sum(t[4:6] for t in tables)


def merge_kernel(ids, *refs):
    out = refs[-1]
    out[0:2], out[2:4], out[4:6] = merge(refs[:-1])
    out[6:8] = jnp.zeros((2, out.shape[1]), jnp.float32)


def last_kernel(ids, *refs):
    out = refs[-1]
    top, total, picked = merge(refs[:-1])
    logprob = picked - (top + jnp.log(total))
    out[...] = logprob[0:1] - logprob[1:2]


def local(
    hidden_policy,
    hidden_reference,
    ffn_gain_policy,
    ffn_gain_reference,
    up_policy,
    up_reference,
    down_policy,
    down_reference,
    final_gain_policy,
    final_gain_reference,
    out_policy,
    out_reference,
    move_plan,
    lengths,
    targets,
):
    dp = lax.axis_size("dp")
    mp = lax.axis_size("mp")
    half = mp // 2
    dp_index = lax.axis_index("dp")
    mp_index = lax.axis_index("mp")
    ids = jnp.stack([dp_index, mp_index // 2, mp_index % 2, mp_index]).astype(jnp.int32)
    reqs, slots, part = hidden_policy.shape
    here = reqs * slots
    rows = here // 2
    ffn_gains = (ffn_gain_policy, ffn_gain_reference)
    final_gains = (final_gain_policy, final_gain_reference)
    gains = [gain.reshape(mp, 1, part) for gain in (*ffn_gains, *final_gains)]
    bits = [1 << b for b in range(dp.bit_length() - 1)]

    bit_orders = []
    for m in range(2):
        bit_orders.append([bits[(b ^ m) if (b ^ m) < len(bits) else b] for b in range(len(bits))])

    def spread_step(blocks, step, places):
        for m in range(2):
            bit = bit_orders[m][step]
            for k in [k for k in blocks[m] if places(m, k)]:
                blocks[m][k ^ bit] = exchange(blocks[m][k], "dp", bit)

    packed = call(
        pack_kernel,
        jax.ShapeDtypeStruct((reqs + 1, slots, part), jnp.bfloat16),
        (lengths, targets, hidden_reference),
        [
            pltpu.SMEM(lengths.shape, jnp.int32),
            pltpu.VMEM(targets.shape, jnp.int32),
            pltpu.SemaphoreType.DMA((3,)),
        ],
        far=(0, 1, 2),
    )
    hiddens = [{0: hidden_policy}, {0: packed}]
    outs = [{0: out_policy}, {0: out_reference}]

    def wait_for(first, places):
        flat = [(m, k) for m in range(2) for k in outs[m] if places(m, k)]
        first, values = lax.optimization_barrier((first, [outs[m][k] for m, k in flat]))
        for (m, k), value in zip(flat, values):
            outs[m][k] = value
        return first

    for step in range(len(bits)):
        spread_step(hiddens, step, lambda m, k: k == 0)
        if step:
            blocks, place = hiddens[0], bit_orders[0][step]
            passed = [k for k in blocks if 0 < k and not k & place]
            values = [blocks[k] for k in passed]
            blocks[place], values = lax.optimization_barrier((blocks[place], values))
            blocks.update(zip(passed, values))
        spread_step(hiddens, step, lambda m, k: 0 < k and not k & bit_orders[m][step])
    early = [(m, b) for m in range(2) for b in bits]
    values = wait_for([hiddens[m][b] for m, b in early], lambda m, k: True)
    for (m, b), value in zip(early, values):
        hiddens[m][b] = value
    spread_step(outs, 0, lambda m, k: True)
    hidden_parts = [hiddens[m][k] for m in range(2) for k in range(dp)]

    order = jnp.arange(dp, dtype=jnp.int32)
    moved, facts = call(
        functools.partial(select_kernel, dp),
        (
            jax.ShapeDtypeStruct((2, rows, part), jnp.bfloat16),
            jax.ShapeDtypeStruct((dp, reqs, part), jnp.float32),
        ),
        (ids, move_plan, *hidden_parts),
        [
            pltpu.VMEM(hidden_policy.shape, jnp.bfloat16),
            pltpu.SMEM(move_plan.shape, jnp.int32),
            pltpu.SemaphoreType.DMA((2,)),
        ],
        far=(1, 2),
        cost=10000000000,
    )

    facts = facts[:, :, : 2 * slots + 1].astype(jnp.int32)
    all_lengths = facts[:, :, 0].reshape(-1)
    all_targets = (facts[:, :, 1 : slots + 1] * 128 + facts[:, :, slots + 1 :]).reshape(-1)
    slot_ids = ((order ^ dp_index)[:, None] * reqs + jnp.arange(reqs, dtype=jnp.int32)).reshape(-1)
    positions = jnp.arange(slots, dtype=jnp.int32)

    def codes(slot):
        start = jnp.sum(jnp.where(slot_ids[None] < slot[:, None], all_lengths[None], 0), axis=1)
        live = jnp.sum(jnp.where(slot_ids[None] == slot[:, None], all_lengths[None], 0), axis=1)
        return jnp.where(
            positions[None] < live[:, None], start[:, None] + positions[None], jnp.int32(-1)
        )

    far = sorted(range(1, half), key=lambda k: (k.bit_length() <= 1, k))

    def gather_pair(own):
        same = {0: own}
        for k in far:
            same[k] = exchange(own, "mp", 2 * k)
        same = [same[k] for k in range(half)]
        return same + [exchange(v, "mp", 1) for v in same]

    parts = gather_pair(moved)
    if len(bits) > 1:
        parts[-1] = wait_for(parts[-1], lambda m, k: k == 0)
        later = [{0: outs[m][0]} for m in range(2)]
        spread_step(later, 1, lambda m, k: True)
    gain_scratch = pltpu.VMEM((2, mp, 1, part), jnp.float32)
    block = jax.ShapeDtypeStruct((2, rows, part), jnp.bfloat16)
    keep, send = call(
        functools.partial(ffn_kernel, half),
        (
            jax.ShapeDtypeStruct((half, 2, rows, part), jnp.float32),
            jax.ShapeDtypeStruct((half, 2, rows, part), jnp.bfloat16),
        ),
        (ids, *gains[:2], up_policy, up_reference, down_policy, down_reference, *parts),
        [
            gain_scratch,
            pltpu.VMEM((2,) + up_policy.shape, jnp.bfloat16),
            pltpu.VMEM((2,) + down_policy.shape, jnp.bfloat16),
            pltpu.VMEM((2, mp, rows, part), jnp.bfloat16),
            pltpu.VMEM((2, mp, rows, part), jnp.float32),
            pltpu.SemaphoreType.DMA((6,)),
        ],
        far=range(1, 7),
        mib=22,
    )
    send = wait_for(send, lambda m, k: k > 0)
    came = exchange(send, "mp", 1)
    own, *pieces = call(
        pair_kernel,
        (jax.ShapeDtypeStruct((2, rows, part), jnp.float32),) + (block,) * (half - 1),
        (ids, keep, came),
    )
    arrived = {k: exchange(pieces[k - 1], "mp", 2 * k) for k in far}
    if len(bits) > 1:
        for m in range(2):
            outs[m].update(later[m])
        arrived[far[0]] = wait_for(arrived[far[0]], lambda m, k: True)
        spread_step(outs, 1, lambda m, k: k == bit_orders[m][0])
    for k in range(1, half):
        own = own + arrived[k].astype(jnp.float32)
    stream = own.astype(jnp.bfloat16)
    for step in range(2, len(bits)):
        stream = wait_for(stream, lambda m, k: True)
        spread_step(outs, step, lambda m, k: True)

    owner_code = codes(slot_ids).reshape(-1)
    my_ranks = dp_index * rows + jnp.arange(rows, dtype=jnp.int32)
    wanted = jnp.sum(
        jnp.where(owner_code[None] == my_ranks[:, None], all_targets[None], 0),
        axis=1,
        keepdims=True,
    )
    partial, tail = call(
        functools.partial(score_kernel, half, dp),
        (
            jax.ShapeDtypeStruct((2, rows, out_policy.shape[1]), jnp.float32),
            jax.ShapeDtypeStruct((2, rows, out_policy.shape[0]), jnp.bfloat16),
        ),
        (
            ids,
            *gains[2:],
            *gather_pair(stream),
            *[outs[m][k] for m in range(2) for k in range(dp - 1)],
        ),
        [
            gain_scratch,
            pltpu.VMEM((2, mp, rows, part), jnp.bfloat16),
            pltpu.VMEM((2,) + out_policy.shape, jnp.bfloat16),
            pltpu.SemaphoreType.DMA((4,)),
        ],
        far=(1, 2, 3 + mp, 2 + mp + dp),
        mib=14,
    )
    stats = call(
        finish_kernel,
        jax.ShapeDtypeStruct((8, rows), jnp.float32),
        (ids, wanted, partial, tail, outs[0][dp - 1], outs[1][dp - 1]),
        mib=8,
    )
    stats = call(
        merge_kernel,
        jax.ShapeDtypeStruct((8, rows), jnp.float32),
        (ids, stats, exchange(stats, "mp", 1)),
    )
    diff = call(
        last_kernel,
        jax.ShapeDtypeStruct((1, rows), jnp.float32),
        (ids, stats, *[exchange(stats, "mp", 2 * k) for k in far]),
    )
    diff = jnp.concatenate([diff] + [exchange(diff, "dp", k) for k in range(1, dp)])
    ranks = ((order ^ dp_index)[:, None] * rows + jnp.arange(rows, dtype=jnp.int32)).reshape(-1)
    my_code = codes(dp_index * reqs + jnp.arange(reqs, dtype=jnp.int32))
    hit = my_code[:, :, None] == ranks[None, None]
    token_diff = jnp.sum(jnp.where(hit, diff.reshape(1, 1, -1), 0.0), axis=2)
    return (token_diff, jnp.sum(token_diff, axis=1))


def solution(mesh):
    return jax.shard_map(
        local,
        mesh=mesh,
        in_specs=(
            P("dp", None, "mp"),
            P("dp", None, "mp"),
            P(),
            P(),
            P(None, "mp"),
            P(None, "mp"),
            P("mp", None),
            P("mp", None),
            P(),
            P(),
            P("dp", "mp"),
            P("dp", "mp"),
            P(),
            P("dp"),
            P("dp", None),
        ),
        out_specs=(P("dp", None), P("dp")),
        check_vma=False,
    )
```

```python
import functools

import jax
import jax.numpy as jnp
from jax import lax
from jax.experimental import pallas as pl
from jax.experimental.pallas import tpu as pltpu
from jax.sharding import PartitionSpec as P

epsilon = 1e-05
vmem = pl.BlockSpec(memory_space=pltpu.VMEM)
smem = pl.BlockSpec(memory_space=pltpu.SMEM)
anywhere = pl.BlockSpec(memory_space=pltpu.HBM)


def call(kernel, out_shape, ops, scratch=(), far=(), mib=4, cost=None):
    specs = [anywhere if i in far else vmem if i else smem for i in range(len(ops))]
    ops = [
        pltpu.with_memory_space_constraint(op, pltpu.HBM) if i in far else op
        for i, op in enumerate(ops)
    ]
    return pl.pallas_call(
        kernel,
        out_shape=out_shape,
        in_specs=specs,
        out_specs=jax.tree.map(lambda _: vmem, out_shape),
        scratch_shapes=list(scratch),
        cost_estimate=cost and pl.CostEstimate(flops=cost, bytes_accessed=0, transcendentals=0),
        compiler_params=pltpu.CompilerParams(vmem_limit_bytes=mib * 1024 * 1024),
    )(*ops)


def exchange(values, axis, flip):
    count = lax.axis_size(axis)
    return lax.ppermute(values, axis, [(i, i ^ flip) for i in range(count)])


def fetch(sources, targets, sems):
    copies = [
        pltpu.make_async_copy(source, target, sems.at[i])
        for i, (source, target) in enumerate(zip(sources, targets))
    ]
    for copy in copies:
        copy.start()
    return copies


def pack_kernel(lengths_far, targets_far, hidden, out, lengths, targets, sems):
    reqs = hidden.shape[0]
    copies = fetch(
        [lengths_far, targets_far, hidden], [lengths, targets, out.at[pl.ds(0, reqs)]], sems
    )
    copies[1].wait()
    slots, part = targets.shape[1], hidden.shape[2]
    row = lax.broadcasted_iota(jnp.int32, (slots, part), 0)
    lane = lax.broadcasted_iota(jnp.int32, (slots, part), 1)
    high = lax.shift_right_logical(targets[...], 7)
    low = targets[...] - high * 128
    block = jnp.zeros((reqs, part), jnp.float32)
    for first, values in ((1, high), (1 + slots, low)):
        spot = (lane == row + first).astype(jnp.float32).astype(jnp.bfloat16)
        values = values.astype(jnp.float32).astype(jnp.bfloat16)
        block = block + jnp.dot(values, spot, preferred_element_type=jnp.float32)
    row = lax.broadcasted_iota(jnp.int32, (reqs, part), 0)
    lane = lax.broadcasted_iota(jnp.int32, (reqs, part), 1)
    copies[0].wait()
    for r in range(reqs):
        here = jnp.logical_and(row == r, lane == 0)
        block = jnp.where(here, lengths[r].astype(jnp.float32), block)
    out[reqs] = block.astype(jnp.bfloat16)
    copies[2].wait()


def select_kernel(dp, ids, plan_far, *refs):
    parts, (out, facts, own, plan, sems) = list(refs[: 2 * dp]), refs[2 * dp :]
    plan_copy, copy = fetch([plan_far, parts[0]], [plan, own], sems)
    parts[0] = own
    rows = out.shape[1]
    reqs, slots, _ = own.shape
    here = reqs * slots
    me = ids[0]
    for k in range(dp):
        facts[k] = parts[dp + k][reqs].astype(jnp.float32)
    lengths = [facts[k][:, 0:1].astype(jnp.int32) for k in range(dp)]
    lengths = jnp.concatenate(lengths, axis=0)
    row = lax.broadcasted_iota(jnp.int32, (reqs, here), 0)
    slot = jnp.concatenate([row + (me ^ k) * reqs for k in range(dp)], axis=0)
    position = lax.rem(lax.broadcasted_iota(jnp.int32, (1, here), 1), slots)
    wanted = me * rows + lax.broadcasted_iota(jnp.int32, (rows, here), 0)
    request = lax.div(lax.broadcasted_iota(jnp.int32, (1, here), 1), slots)
    hots = []
    plan_copy.wait()
    for k in range(dp):
        owner = jnp.zeros((1, here), jnp.int32)
        for r in range(reqs):
            owner = jnp.where(request == r, plan[(me ^ k) * reqs + r], owner)
        start = jnp.sum(jnp.where(slot < owner, lengths, 0), axis=0, keepdims=True)
        live = jnp.sum(jnp.where(slot == owner, lengths, 0), axis=0, keepdims=True)
        code = jnp.where(position < live, start + position, -1)
        hots.append((code == wanted).astype(jnp.float32).astype(jnp.bfloat16))
    copy.wait()
    for m in range(2):
        total = None
        for k in range(dp):
            values = parts[m * dp + k][0:reqs]
            values = values.reshape(-1, values.shape[-1])
            found = jnp.dot(hots[k], values, preferred_element_type=jnp.float32)
            total = found if total is None else total + found
        out[m] = total.astype(out.dtype)


def normalise(values, gain, chip, core, store, copy):
    half = len(values) // 2
    part = values[0].shape[1]
    width = part * len(values)
    values = [v.astype(jnp.float32) for v in values]
    center = sum(jnp.sum(v, axis=1, keepdims=True) for v in values) / width
    values = [v - center for v in values]
    spread = sum(jnp.sum(v * v, axis=1, keepdims=True) for v in values) / width
    scale = lax.rsqrt(spread + epsilon)
    copy.wait()
    for k, v in enumerate(values):
        place = 2 * (chip ^ (k % half)) + (core if k < half else 1 - core)
        store[place] = (v * scale * gain[place]).astype(jnp.bfloat16)
    return values[0]


def blocks_dot(normed, weight, order):
    part = normed.shape[2]
    total = None
    for b, place in enumerate(order):
        rows = weight[b * part : (b + 1) * part, :]
        piece = jnp.dot(normed[place], rows, preferred_element_type=jnp.float32)
        total = piece if total is None else total + piece
    return total


def ffn_kernel(half, ids, *refs):
    parts = refs[6 : 6 + 2 * half]
    keep, send, gains, ups, downs, normed, terms, sems = refs[6 + 2 * half :]
    copies = fetch(
        refs[:6], [store.at[m] for store in (gains, ups, downs) for m in range(2)], sems
    )
    chip, core = ids[1], ids[2]
    part = parts[0].shape[2]
    bases = [
        normalise([part[m] for part in parts], gains.at[m], chip, core, normed.at[m], copies[m])
        for m in range(2)
    ]
    for m in range(2):
        copies[2 + m].wait()
        pre = blocks_dot(normed.at[m], ups.at[m], range(2 * half))
        units = jax.nn.gelu(pre).astype(jnp.bfloat16)
        copies[4 + m].wait()
        full = jnp.dot(units, downs[m], preferred_element_type=jnp.float32)
        for b in range(2 * half):
            terms[m, b] = full[:, b * part : (b + 1) * part]
        for k in range(half):
            place = 2 * (chip ^ k)
            kept = terms[m, place + core]
            keep[k, m] = kept + bases[m] if k == 0 else kept
            send[k, m] = terms[m, place + 1 - core].astype(jnp.bfloat16)


def pair_kernel(ids, keep, came, own, *outs):
    own[...] = keep[0] + came[0].astype(jnp.float32)
    for k, out in enumerate(outs):
        out[...] = (keep[k + 1] + came[k + 1].astype(jnp.float32)).astype(jnp.bfloat16)


def score_kernel(half, dp, ids, *refs):
    parts = refs[2 : 2 + 2 * half]
    *outs, partial, tail, gains, normed, out_store, sems = refs[2 + 2 * half :]
    here = dp - 1
    copies = fetch(
        [refs[0], refs[1], outs[0], outs[here]],
        [store.at[m] for store in (gains, out_store) for m in range(2)],
        sems,
    )
    me, chip, core = ids[0], ids[1], ids[2]
    ratio = 2 * half // dp
    part = parts[0].shape[2]
    for m in range(2):
        values = [part[m] for part in parts]
        normalise(values, gains.at[m], chip, core, normed.at[m], copies[m])
        for b in range(ratio):
            tail[m, :, b * part : (b + 1) * part] = normed[m, (me ^ here) * ratio + b]
    for m in range(2):
        logits = None
        for k in [*range(1, here), 0]:
            if k == 0:
                copies[2 + m].wait()
                outs[m * here] = out_store.at[m]
            order = [(me ^ k) * ratio + b for b in range(ratio)]
            piece = blocks_dot(normed.at[m], outs[m * here + k], order)
            logits = piece if logits is None else logits + piece
        partial[m] = logits


def finish_kernel(ids, wanted, partial, tail, last_policy, last_reference, stats):
    lane = lax.broadcasted_iota(jnp.int32, (tail.shape[1], 128), 1)
    table = jnp.zeros(lane.shape, jnp.float32)
    for m, last in enumerate((last_policy, last_reference)):
        logits = partial[m] + jnp.dot(tail[m], last[...], preferred_element_type=jnp.float32)
        entries = lax.broadcasted_iota(jnp.int32, logits.shape, 1) + ids[3] * logits.shape[1]
        picked = jnp.sum(jnp.where(entries == wanted[...], logits, 0.0), axis=1, keepdims=True)
        top = jnp.max(logits, axis=1, keepdims=True)
        total = jnp.sum(jnp.exp(logits - top), axis=1, keepdims=True)
        table = jnp.where(lane == m, top, table)
        table = jnp.where(lane == 2 + m, total, table)
        table = jnp.where(lane == 4 + m, picked, table)
    rows = jnp.transpose(table)[:8]
    for j in range(stats.shape[0]):
        stats[j] = rows


def last_kernel(ids, every, out):
    tables = [every[j] for j in range(every.shape[0])]
    top = functools.reduce(jnp.maximum, [t[0:2] for t in tables])
    total = sum(t[2:4] * jnp.exp(t[0:2] - top) for t in tables)
    logprob = sum(t[4:6] for t in tables) - (top + jnp.log(total))
    for k in range(out.shape[0]):
        out[k] = logprob[0:1] - logprob[1:2]


def local(
    hidden_policy,
    hidden_reference,
    ffn_gain_policy,
    ffn_gain_reference,
    up_policy,
    up_reference,
    down_policy,
    down_reference,
    final_gain_policy,
    final_gain_reference,
    out_policy,
    out_reference,
    move_plan,
    lengths,
    targets,
):
    dp = lax.axis_size("dp")
    mp = lax.axis_size("mp")
    half = mp // 2
    dp_index = lax.axis_index("dp")
    mp_index = lax.axis_index("mp")
    ids = jnp.stack([dp_index, mp_index // 2, mp_index % 2, mp_index]).astype(jnp.int32)
    reqs, slots, part = hidden_policy.shape
    here = reqs * slots
    rows = here // 2
    ffn_gains = (ffn_gain_policy, ffn_gain_reference)
    final_gains = (final_gain_policy, final_gain_reference)
    gains = [gain.reshape(mp, 1, part) for gain in (*ffn_gains, *final_gains)]
    bits = [1 << b for b in range(dp.bit_length() - 1)]

    bit_orders = []
    for m in range(2):
        bit_orders.append([bits[(b ^ m) if (b ^ m) < len(bits) else b] for b in range(len(bits))])

    def spread_step(blocks, step, places):
        for m in range(2):
            bit = bit_orders[m][step]
            for k in [k for k in blocks[m] if places(m, k)]:
                blocks[m][k ^ bit] = exchange(blocks[m][k], "dp", bit)

    packed = call(
        pack_kernel,
        jax.ShapeDtypeStruct((reqs + 1, slots, part), jnp.bfloat16),
        (lengths, targets, hidden_reference),
        [
            pltpu.SMEM(lengths.shape, jnp.int32),
            pltpu.VMEM(targets.shape, jnp.int32),
            pltpu.SemaphoreType.DMA((3,)),
        ],
        far=(0, 1, 2),
    )
    hiddens = [{0: hidden_policy}, {0: packed}]
    outs = [{0: out_policy}, {0: out_reference}]

    def wait_for(first, places):
        flat = [(m, k) for m in range(2) for k in outs[m] if places(m, k)]
        first, values = lax.optimization_barrier((first, [outs[m][k] for m, k in flat]))
        for (m, k), value in zip(flat, values):
            outs[m][k] = value
        return first

    for step in range(len(bits)):
        spread_step(hiddens, step, lambda m, k: k == 0)
        if step:
            blocks, place = hiddens[0], bit_orders[0][step]
            passed = [k for k in blocks if 0 < k and not k & place]
            values = [blocks[k] for k in passed]
            blocks[place], values = lax.optimization_barrier((blocks[place], values))
            blocks.update(zip(passed, values))
        spread_step(hiddens, step, lambda m, k: 0 < k and not k & bit_orders[m][step])
    early = [(m, b) for m in range(2) for b in bits]
    values = wait_for([hiddens[m][b] for m, b in early], lambda m, k: True)
    for (m, b), value in zip(early, values):
        hiddens[m][b] = value
    spread_step(outs, 0, lambda m, k: True)
    hidden_parts = [hiddens[m][k] for m in range(2) for k in range(dp)]

    order = jnp.arange(dp, dtype=jnp.int32)
    moved, facts = call(
        functools.partial(select_kernel, dp),
        (
            jax.ShapeDtypeStruct((2, rows, part), jnp.bfloat16),
            jax.ShapeDtypeStruct((dp, reqs, part), jnp.float32),
        ),
        (ids, move_plan, *hidden_parts),
        [
            pltpu.VMEM(hidden_policy.shape, jnp.bfloat16),
            pltpu.SMEM(move_plan.shape, jnp.int32),
            pltpu.SemaphoreType.DMA((2,)),
        ],
        far=(1, 2),
        cost=10000000000,
    )

    facts = facts[:, :, : 2 * slots + 1].astype(jnp.int32)
    all_lengths = facts[:, :, 0].reshape(-1)
    all_targets = (facts[:, :, 1 : slots + 1] * 128 + facts[:, :, slots + 1 :]).reshape(-1)
    slot_ids = ((order ^ dp_index)[:, None] * reqs + jnp.arange(reqs, dtype=jnp.int32)).reshape(-1)
    positions = jnp.arange(slots, dtype=jnp.int32)

    def codes(slot):
        start = jnp.sum(jnp.where(slot_ids[None] < slot[:, None], all_lengths[None], 0), axis=1)
        live = jnp.sum(jnp.where(slot_ids[None] == slot[:, None], all_lengths[None], 0), axis=1)
        return jnp.where(
            positions[None] < live[:, None], start[:, None] + positions[None], jnp.int32(-1)
        )

    far = sorted(range(1, half), key=lambda k: (k.bit_length() <= 1, k))

    def gather_pair(own):
        same = {0: own}
        for k in far:
            same[k] = exchange(own, "mp", 2 * k)
        same = [same[k] for k in range(half)]
        return same + [exchange(v, "mp", 1) for v in same]

    parts = gather_pair(moved)
    if len(bits) > 1:
        parts[-1] = wait_for(parts[-1], lambda m, k: k == 0)
        later = [{0: outs[m][0]} for m in range(2)]
        spread_step(later, 1, lambda m, k: True)
    gain_scratch = pltpu.VMEM((2, mp, 1, part), jnp.float32)
    block = jax.ShapeDtypeStruct((2, rows, part), jnp.bfloat16)
    keep, send = call(
        functools.partial(ffn_kernel, half),
        (
            jax.ShapeDtypeStruct((half, 2, rows, part), jnp.float32),
            jax.ShapeDtypeStruct((half, 2, rows, part), jnp.bfloat16),
        ),
        (ids, *gains[:2], up_policy, up_reference, down_policy, down_reference, *parts),
        [
            gain_scratch,
            pltpu.VMEM((2,) + up_policy.shape, jnp.bfloat16),
            pltpu.VMEM((2,) + down_policy.shape, jnp.bfloat16),
            pltpu.VMEM((2, mp, rows, part), jnp.bfloat16),
            pltpu.VMEM((2, mp, rows, part), jnp.float32),
            pltpu.SemaphoreType.DMA((6,)),
        ],
        far=range(1, 7),
        mib=22,
    )
    send = wait_for(send, lambda m, k: k > 0)
    came = exchange(send, "mp", 1)
    own, *pieces = call(
        pair_kernel,
        (jax.ShapeDtypeStruct((2, rows, part), jnp.float32),) + (block,) * (half - 1),
        (ids, keep, came),
    )
    arrived = {k: exchange(pieces[k - 1], "mp", 2 * k) for k in far}
    if len(bits) > 1:
        for m in range(2):
            outs[m].update(later[m])
        arrived[far[0]] = wait_for(arrived[far[0]], lambda m, k: True)
        spread_step(outs, 1, lambda m, k: k == bit_orders[m][0])
    for k in range(1, half):
        own = own + arrived[k].astype(jnp.float32)
    stream = own.astype(jnp.bfloat16)
    for step in range(2, len(bits)):
        stream = wait_for(stream, lambda m, k: True)
        spread_step(outs, step, lambda m, k: True)

    owner_code = codes(slot_ids).reshape(-1)
    my_ranks = dp_index * rows + jnp.arange(rows, dtype=jnp.int32)
    wanted = jnp.sum(
        jnp.where(owner_code[None] == my_ranks[:, None], all_targets[None], 0),
        axis=1,
        keepdims=True,
    )
    partial, tail = call(
        functools.partial(score_kernel, half, dp),
        (
            jax.ShapeDtypeStruct((2, rows, out_policy.shape[1]), jnp.float32),
            jax.ShapeDtypeStruct((2, rows, out_policy.shape[0]), jnp.bfloat16),
        ),
        (
            ids,
            *gains[2:],
            *gather_pair(stream),
            *[outs[m][k] for m in range(2) for k in range(dp - 1)],
        ),
        [
            gain_scratch,
            pltpu.VMEM((2, mp, rows, part), jnp.bfloat16),
            pltpu.VMEM((2,) + out_policy.shape, jnp.bfloat16),
            pltpu.SemaphoreType.DMA((4,)),
        ],
        far=(1, 2, 3 + mp, 2 + mp + dp),
        mib=14,
    )
    stats = call(
        finish_kernel,
        jax.ShapeDtypeStruct((mp, 8, rows), jnp.float32),
        (ids, wanted, partial, tail, outs[0][dp - 1], outs[1][dp - 1]),
        mib=8,
    )
    diff = call(
        last_kernel,
        jax.ShapeDtypeStruct((dp, 1, rows), jnp.float32),
        (ids, lax.all_to_all(stats, "mp", split_axis=0, concat_axis=0, tiled=True)),
    )
    diff = lax.all_to_all(diff, "dp", split_axis=0, concat_axis=0, tiled=True)
    ranks = jnp.arange(dp * rows, dtype=jnp.int32)
    my_code = codes(dp_index * reqs + jnp.arange(reqs, dtype=jnp.int32))
    hit = my_code[:, :, None] == ranks[None, None]
    token_diff = jnp.sum(jnp.where(hit, diff.reshape(1, 1, -1), 0.0), axis=2)
    return (token_diff, jnp.sum(token_diff, axis=1))


def solution(mesh):
    return jax.shard_map(
        local,
        mesh=mesh,
        in_specs=(
            P("dp", None, "mp"),
            P("dp", None, "mp"),
            P(),
            P(),
            P(None, "mp"),
            P(None, "mp"),
            P("mp", None),
            P("mp", None),
            P(),
            P(),
            P("dp", "mp"),
            P("dp", "mp"),
            P(),
            P("dp"),
            P("dp", None),
        ),
        out_specs=(P("dp", None), P("dp")),
        check_vma=False,
    )
```

```python
import functools

import jax
import jax.numpy as jnp
from jax import lax
from jax.experimental import pallas as pl
from jax.experimental.pallas import tpu as pltpu
from jax.sharding import PartitionSpec as P

epsilon = 1e-05
vmem = pl.BlockSpec(memory_space=pltpu.VMEM)
smem = pl.BlockSpec(memory_space=pltpu.SMEM)
anywhere = pl.BlockSpec(memory_space=pltpu.HBM)


def call(kernel, out_shape, ops, scratch=(), far=(), mib=4, cost=None):
    specs = [anywhere if i in far else vmem if i else smem for i in range(len(ops))]
    ops = [
        pltpu.with_memory_space_constraint(op, pltpu.HBM) if i in far else op
        for i, op in enumerate(ops)
    ]
    return pl.pallas_call(
        kernel,
        out_shape=out_shape,
        in_specs=specs,
        out_specs=jax.tree.map(lambda _: vmem, out_shape),
        scratch_shapes=list(scratch),
        cost_estimate=cost and pl.CostEstimate(flops=cost, bytes_accessed=0, transcendentals=0),
        compiler_params=pltpu.CompilerParams(vmem_limit_bytes=mib * 1024 * 1024),
    )(*ops)


def exchange(values, axis, flip):
    count = lax.axis_size(axis)
    return lax.ppermute(values, axis, [(i, i ^ flip) for i in range(count)])


def fetch(sources, targets, sems):
    copies = [
        pltpu.make_async_copy(source, target, sems.at[i])
        for i, (source, target) in enumerate(zip(sources, targets))
    ]
    for copy in copies:
        copy.start()
    return copies


def pack_kernel(lengths_far, targets_far, hidden, out, lengths, targets, sems):
    reqs = hidden.shape[0]
    copies = fetch(
        [lengths_far, targets_far, hidden], [lengths, targets, out.at[pl.ds(0, reqs)]], sems
    )
    copies[1].wait()
    slots, part = targets.shape[1], hidden.shape[2]
    row = lax.broadcasted_iota(jnp.int32, (slots, part), 0)
    lane = lax.broadcasted_iota(jnp.int32, (slots, part), 1)
    high = lax.shift_right_logical(targets[...], 7)
    low = targets[...] - high * 128
    block = jnp.zeros((reqs, part), jnp.float32)
    for first, values in ((1, high), (1 + slots, low)):
        spot = (lane == row + first).astype(jnp.float32).astype(jnp.bfloat16)
        values = values.astype(jnp.float32).astype(jnp.bfloat16)
        block = block + jnp.dot(values, spot, preferred_element_type=jnp.float32)
    row = lax.broadcasted_iota(jnp.int32, (reqs, part), 0)
    lane = lax.broadcasted_iota(jnp.int32, (reqs, part), 1)
    copies[0].wait()
    for r in range(reqs):
        here = jnp.logical_and(row == r, lane == 0)
        block = jnp.where(here, lengths[r].astype(jnp.float32), block)
    out[reqs] = block.astype(jnp.bfloat16)
    copies[2].wait()


def select_kernel(dp, ids, plan_far, *refs):
    parts, (out, facts, own, plan, sems) = list(refs[: 2 * dp]), refs[2 * dp :]
    plan_copy, copy = fetch([plan_far, parts[0]], [plan, own], sems)
    parts[0] = own
    rows = out.shape[1]
    reqs, slots, _ = own.shape
    here = reqs * slots
    me = ids[0]
    for k in range(dp):
        facts[k] = parts[dp + k][reqs].astype(jnp.float32)
    lengths = [facts[k][:, 0:1].astype(jnp.int32) for k in range(dp)]
    lengths = jnp.concatenate(lengths, axis=0)
    row = lax.broadcasted_iota(jnp.int32, (reqs, here), 0)
    slot = jnp.concatenate([row + (me ^ k) * reqs for k in range(dp)], axis=0)
    position = lax.rem(lax.broadcasted_iota(jnp.int32, (1, here), 1), slots)
    wanted = me * rows + lax.broadcasted_iota(jnp.int32, (rows, here), 0)
    request = lax.div(lax.broadcasted_iota(jnp.int32, (1, here), 1), slots)
    hots = []
    plan_copy.wait()
    for k in range(dp):
        owner = jnp.zeros((1, here), jnp.int32)
        for r in range(reqs):
            owner = jnp.where(request == r, plan[(me ^ k) * reqs + r], owner)
        start = jnp.sum(jnp.where(slot < owner, lengths, 0), axis=0, keepdims=True)
        live = jnp.sum(jnp.where(slot == owner, lengths, 0), axis=0, keepdims=True)
        code = jnp.where(position < live, start + position, -1)
        hots.append((code == wanted).astype(jnp.float32).astype(jnp.bfloat16))
    copy.wait()
    for m in range(2):
        total = None
        for k in range(dp):
            values = parts[m * dp + k][0:reqs]
            values = values.reshape(-1, values.shape[-1])
            found = jnp.dot(hots[k], values, preferred_element_type=jnp.float32)
            total = found if total is None else total + found
        out[m] = total.astype(out.dtype)


def normalise(values, gain, chip, core, store, copy):
    half = len(values) // 2
    part = values[0].shape[1]
    width = part * len(values)
    values = [v.astype(jnp.float32) for v in values]
    center = sum(jnp.sum(v, axis=1, keepdims=True) for v in values) / width
    values = [v - center for v in values]
    spread = sum(jnp.sum(v * v, axis=1, keepdims=True) for v in values) / width
    scale = lax.rsqrt(spread + epsilon)
    copy.wait()
    for k, v in enumerate(values):
        place = 2 * (chip ^ (k % half)) + (core if k < half else 1 - core)
        store[place] = (v * scale * gain[place]).astype(jnp.bfloat16)
    return values[0]


def blocks_dot(normed, weight, order):
    part = normed.shape[2]
    total = None
    for b, place in enumerate(order):
        rows = weight[b * part : (b + 1) * part, :]
        piece = jnp.dot(normed[place], rows, preferred_element_type=jnp.float32)
        total = piece if total is None else total + piece
    return total


def ffn_kernel(half, ids, *refs):
    parts = refs[6 : 6 + 2 * half]
    keep, send, gains, ups, downs, normed, terms, sems = refs[6 + 2 * half :]
    copies = fetch(
        refs[:6], [store.at[m] for store in (gains, ups, downs) for m in range(2)], sems
    )
    chip, core = ids[1], ids[2]
    part = parts[0].shape[2]
    bases = [
        normalise([part[m] for part in parts], gains.at[m], chip, core, normed.at[m], copies[m])
        for m in range(2)
    ]
    for m in range(2):
        copies[2 + m].wait()
        pre = blocks_dot(normed.at[m], ups.at[m], range(2 * half))
        units = jax.nn.gelu(pre).astype(jnp.bfloat16)
        copies[4 + m].wait()
        full = jnp.dot(units, downs[m], preferred_element_type=jnp.float32)
        for b in range(2 * half):
            terms[m, b] = full[:, b * part : (b + 1) * part]
        for k in range(half):
            place = 2 * (chip ^ k)
            kept = terms[m, place + core]
            keep[k, m] = kept + bases[m] if k == 0 else kept
            send[k, m] = terms[m, place + 1 - core].astype(jnp.bfloat16)


def pair_kernel(ids, keep, came, own, *outs):
    own[...] = keep[0] + came[0].astype(jnp.float32)
    for k, out in enumerate(outs):
        out[...] = (keep[k + 1] + came[k + 1].astype(jnp.float32)).astype(jnp.bfloat16)


def score_kernel(half, dp, ids, *refs):
    parts = refs[2 : 2 + 2 * half]
    *outs, partial, tail, gains, normed, out_store, sems = refs[2 + 2 * half :]
    here = dp - 1
    copies = fetch(
        [refs[0], refs[1], outs[0], outs[here]],
        [store.at[m] for store in (gains, out_store) for m in range(2)],
        sems,
    )
    me, chip, core = ids[0], ids[1], ids[2]
    ratio = 2 * half // dp
    part = parts[0].shape[2]
    for m in range(2):
        values = [part[m] for part in parts]
        normalise(values, gains.at[m], chip, core, normed.at[m], copies[m])
        for b in range(ratio):
            tail[m, :, b * part : (b + 1) * part] = normed[m, (me ^ here) * ratio + b]
    for m in range(2):
        logits = None
        for k in [*range(1, here), 0]:
            if k == 0:
                copies[2 + m].wait()
                outs[m * here] = out_store.at[m]
            order = [(me ^ k) * ratio + b for b in range(ratio)]
            piece = blocks_dot(normed.at[m], outs[m * here + k], order)
            logits = piece if logits is None else logits + piece
        partial[m] = logits


def finish_kernel(ids, wanted, partial, tail, last_policy, last_reference, stats):
    lane = lax.broadcasted_iota(jnp.int32, (tail.shape[1], 128), 1)
    table = jnp.zeros(lane.shape, jnp.float32)
    for m, last in enumerate((last_policy, last_reference)):
        logits = partial[m] + jnp.dot(tail[m], last[...], preferred_element_type=jnp.float32)
        entries = lax.broadcasted_iota(jnp.int32, logits.shape, 1) + ids[3] * logits.shape[1]
        picked = jnp.sum(jnp.where(entries == wanted[...], logits, 0.0), axis=1, keepdims=True)
        top = jnp.max(logits, axis=1, keepdims=True)
        total = jnp.sum(jnp.exp(logits - top), axis=1, keepdims=True)
        table = jnp.where(lane == m, top, table)
        table = jnp.where(lane == 2 + m, total, table)
        table = jnp.where(lane == 4 + m, picked, table)
    stats[...] = jnp.transpose(table)[:8]


def merge(tables):
    top = functools.reduce(jnp.maximum, [t[0:2] for t in tables])
    total = sum(t[2:4] * jnp.exp(t[0:2] - top) for t in tables)
    return top, total, sum(t[4:6] for t in tables)


def merge_kernel(ids, *refs):
    out = refs[-1]
    out[0:2], out[2:4], out[4:6] = merge(refs[:-1])
    out[6:8] = jnp.zeros((2, out.shape[1]), jnp.float32)


def last_kernel(ids, *refs):
    out = refs[-1]
    top, total, picked = merge(refs[:-1])
    logprob = picked - (top + jnp.log(total))
    out[...] = logprob[0:1] - logprob[1:2]


def local(
    hidden_policy,
    hidden_reference,
    ffn_gain_policy,
    ffn_gain_reference,
    up_policy,
    up_reference,
    down_policy,
    down_reference,
    final_gain_policy,
    final_gain_reference,
    out_policy,
    out_reference,
    move_plan,
    lengths,
    targets,
):
    dp = lax.axis_size("dp")
    mp = lax.axis_size("mp")
    half = mp // 2
    dp_index = lax.axis_index("dp")
    mp_index = lax.axis_index("mp")
    ids = jnp.stack([dp_index, mp_index // 2, mp_index % 2, mp_index]).astype(jnp.int32)
    reqs, slots, part = hidden_policy.shape
    here = reqs * slots
    rows = here // 2
    ffn_gains = (ffn_gain_policy, ffn_gain_reference)
    final_gains = (final_gain_policy, final_gain_reference)
    gains = [gain.reshape(mp, 1, part) for gain in (*ffn_gains, *final_gains)]
    bits = [1 << b for b in range(dp.bit_length() - 1)]

    bit_orders = []
    for m in range(2):
        bit_orders.append([bits[(b ^ m) if (b ^ m) < len(bits) else b] for b in range(len(bits))])

    def spread_step(blocks, step, places):
        for m in range(2):
            bit = bit_orders[m][step]
            for k in [k for k in blocks[m] if places(m, k)]:
                blocks[m][k ^ bit] = exchange(blocks[m][k], "dp", bit)

    packed = call(
        pack_kernel,
        jax.ShapeDtypeStruct((reqs + 1, slots, part), jnp.bfloat16),
        (lengths, targets, hidden_reference),
        [
            pltpu.SMEM(lengths.shape, jnp.int32),
            pltpu.VMEM(targets.shape, jnp.int32),
            pltpu.SemaphoreType.DMA((3,)),
        ],
        far=(0, 1, 2),
    )
    hiddens = [{0: hidden_policy}, {0: packed}]
    outs = [{0: out_policy}, {0: out_reference}]

    def wait_for(first, places):
        flat = [(m, k) for m in range(2) for k in outs[m] if places(m, k)]
        first, values = lax.optimization_barrier((first, [outs[m][k] for m, k in flat]))
        for (m, k), value in zip(flat, values):
            outs[m][k] = value
        return first

    for step in range(len(bits)):
        spread_step(hiddens, step, lambda m, k: k == 0)
        if step:
            blocks, place = hiddens[0], bit_orders[0][step]
            passed = [k for k in blocks if 0 < k and not k & place]
            values = [blocks[k] for k in passed]
            blocks[place], values = lax.optimization_barrier((blocks[place], values))
            blocks.update(zip(passed, values))
        spread_step(hiddens, step, lambda m, k: 0 < k and not k & bit_orders[m][step])
    early = [(0, b) for b in bits] + [(1, bit_orders[1][0])]
    values = wait_for([hiddens[m][b] for m, b in early], lambda m, k: True)
    for (m, b), value in zip(early, values):
        hiddens[m][b] = value
    spread_step(outs, 0, lambda m, k: True)
    hidden_parts = [hiddens[m][k] for m in range(2) for k in range(dp)]

    order = jnp.arange(dp, dtype=jnp.int32)
    moved, facts = call(
        functools.partial(select_kernel, dp),
        (
            jax.ShapeDtypeStruct((2, rows, part), jnp.bfloat16),
            jax.ShapeDtypeStruct((dp, reqs, part), jnp.float32),
        ),
        (ids, move_plan, *hidden_parts),
        [
            pltpu.VMEM(hidden_policy.shape, jnp.bfloat16),
            pltpu.SMEM(move_plan.shape, jnp.int32),
            pltpu.SemaphoreType.DMA((2,)),
        ],
        far=(1, 2),
        cost=10000000000,
    )

    facts = facts[:, :, : 2 * slots + 1].astype(jnp.int32)
    all_lengths = facts[:, :, 0].reshape(-1)
    all_targets = (facts[:, :, 1 : slots + 1] * 128 + facts[:, :, slots + 1 :]).reshape(-1)
    slot_ids = ((order ^ dp_index)[:, None] * reqs + jnp.arange(reqs, dtype=jnp.int32)).reshape(-1)
    positions = jnp.arange(slots, dtype=jnp.int32)

    def codes(slot):
        start = jnp.sum(jnp.where(slot_ids[None] < slot[:, None], all_lengths[None], 0), axis=1)
        live = jnp.sum(jnp.where(slot_ids[None] == slot[:, None], all_lengths[None], 0), axis=1)
        return jnp.where(
            positions[None] < live[:, None], start[:, None] + positions[None], jnp.int32(-1)
        )

    far = sorted(range(1, half), key=lambda k: (k.bit_length() <= 1, k))

    def gather_pair(own):
        same = {0: own}
        for k in far:
            same[k] = exchange(own, "mp", 2 * k)
        same = [same[k] for k in range(half)]
        return same + [exchange(v, "mp", 1) for v in same]

    parts = gather_pair(moved)
    if len(bits) > 1:
        parts[-1] = wait_for(parts[-1], lambda m, k: k == 0)
        later = [{0: outs[m][0]} for m in range(2)]
        spread_step(later, 1, lambda m, k: True)
    gain_scratch = pltpu.VMEM((2, mp, 1, part), jnp.float32)
    block = jax.ShapeDtypeStruct((2, rows, part), jnp.bfloat16)
    keep, send = call(
        functools.partial(ffn_kernel, half),
        (
            jax.ShapeDtypeStruct((half, 2, rows, part), jnp.float32),
            jax.ShapeDtypeStruct((half, 2, rows, part), jnp.bfloat16),
        ),
        (ids, *gains[:2], up_policy, up_reference, down_policy, down_reference, *parts),
        [
            gain_scratch,
            pltpu.VMEM((2,) + up_policy.shape, jnp.bfloat16),
            pltpu.VMEM((2,) + down_policy.shape, jnp.bfloat16),
            pltpu.VMEM((2, mp, rows, part), jnp.bfloat16),
            pltpu.VMEM((2, mp, rows, part), jnp.float32),
            pltpu.SemaphoreType.DMA((6,)),
        ],
        far=range(1, 7),
        mib=22,
    )
    send = wait_for(send, lambda m, k: k > 0)
    came = exchange(send, "mp", 1)
    own, *pieces = call(
        pair_kernel,
        (jax.ShapeDtypeStruct((2, rows, part), jnp.float32),) + (block,) * (half - 1),
        (ids, keep, came),
    )
    arrived = {k: exchange(pieces[k - 1], "mp", 2 * k) for k in far}
    if len(bits) > 1:
        for m in range(2):
            outs[m].update(later[m])
        arrived[far[0]] = wait_for(arrived[far[0]], lambda m, k: True)
        spread_step(outs, 1, lambda m, k: k == bit_orders[m][0])
    for k in range(1, half):
        own = own + arrived[k].astype(jnp.float32)
    stream = own.astype(jnp.bfloat16)
    for step in range(2, len(bits)):
        stream = wait_for(stream, lambda m, k: True)
        spread_step(outs, step, lambda m, k: True)

    owner_code = codes(slot_ids).reshape(-1)
    my_ranks = dp_index * rows + jnp.arange(rows, dtype=jnp.int32)
    wanted = jnp.sum(
        jnp.where(owner_code[None] == my_ranks[:, None], all_targets[None], 0),
        axis=1,
        keepdims=True,
    )
    partial, tail = call(
        functools.partial(score_kernel, half, dp),
        (
            jax.ShapeDtypeStruct((2, rows, out_policy.shape[1]), jnp.float32),
            jax.ShapeDtypeStruct((2, rows, out_policy.shape[0]), jnp.bfloat16),
        ),
        (
            ids,
            *gains[2:],
            *gather_pair(stream),
            *[outs[m][k] for m in range(2) for k in range(dp - 1)],
        ),
        [
            gain_scratch,
            pltpu.VMEM((2, mp, rows, part), jnp.bfloat16),
            pltpu.VMEM((2,) + out_policy.shape, jnp.bfloat16),
            pltpu.SemaphoreType.DMA((4,)),
        ],
        far=(1, 2, 3 + mp, 2 + mp + dp),
        mib=14,
    )
    stats = call(
        finish_kernel,
        jax.ShapeDtypeStruct((8, rows), jnp.float32),
        (ids, wanted, partial, tail, outs[0][dp - 1], outs[1][dp - 1]),
        mib=8,
    )
    stats = call(
        merge_kernel,
        jax.ShapeDtypeStruct((8, rows), jnp.float32),
        (ids, stats, exchange(stats, "mp", 1)),
    )
    diff = call(
        last_kernel,
        jax.ShapeDtypeStruct((1, rows), jnp.float32),
        (ids, stats, *[exchange(stats, "mp", 2 * k) for k in range(half - 1, 0, -1)]),
    )
    came = [exchange(diff, "dp", k) for k in range(dp - 1, 0, -1)]
    diff = jnp.concatenate(came + [diff])
    ranks = ((order[::-1] ^ dp_index)[:, None] * rows + jnp.arange(rows, dtype=jnp.int32)).reshape(-1)
    my_code = codes(dp_index * reqs + jnp.arange(reqs, dtype=jnp.int32))
    hit = my_code[:, :, None] == ranks[None, None]
    token_diff = jnp.sum(jnp.where(hit, diff.reshape(1, 1, -1), 0.0), axis=2)
    return (token_diff, jnp.sum(token_diff, axis=1))


def solution(mesh):
    return jax.shard_map(
        local,
        mesh=mesh,
        in_specs=(
            P("dp", None, "mp"),
            P("dp", None, "mp"),
            P(),
            P(),
            P(None, "mp"),
            P(None, "mp"),
            P("mp", None),
            P("mp", None),
            P(),
            P(),
            P("dp", "mp"),
            P("dp", "mp"),
            P(),
            P("dp"),
            P("dp", None),
        ),
        out_specs=(P("dp", None), P("dp")),
        check_vma=False,
    )
```

```python
import functools

import jax
import jax.numpy as jnp
from jax import lax
from jax.experimental import pallas as pl
from jax.experimental.pallas import tpu as pltpu
from jax.sharding import PartitionSpec as P

epsilon = 1e-05
vmem = pl.BlockSpec(memory_space=pltpu.VMEM)
smem = pl.BlockSpec(memory_space=pltpu.SMEM)
anywhere = pl.BlockSpec(memory_space=pltpu.HBM)


def call(kernel, out_shape, ops, scratch=(), far=(), mib=4, cost=None):
    specs = [anywhere if i in far else vmem if i else smem for i in range(len(ops))]
    ops = [
        pltpu.with_memory_space_constraint(op, pltpu.HBM) if i in far else op
        for i, op in enumerate(ops)
    ]
    return pl.pallas_call(
        kernel,
        out_shape=out_shape,
        in_specs=specs,
        out_specs=jax.tree.map(lambda _: vmem, out_shape),
        scratch_shapes=list(scratch),
        cost_estimate=cost and pl.CostEstimate(flops=cost, bytes_accessed=0, transcendentals=0),
        compiler_params=pltpu.CompilerParams(vmem_limit_bytes=mib * 1024 * 1024),
    )(*ops)


def exchange(values, axis, flip):
    count = lax.axis_size(axis)
    return lax.ppermute(values, axis, [(i, i ^ flip) for i in range(count)])


def fetch(sources, targets, sems):
    copies = [
        pltpu.make_async_copy(source, target, sems.at[i])
        for i, (source, target) in enumerate(zip(sources, targets))
    ]
    for copy in copies:
        copy.start()
    return copies


def pack_kernel(lengths_far, targets_far, hidden, out, lengths, targets, sems):
    reqs = hidden.shape[0]
    copies = fetch(
        [lengths_far, targets_far, hidden], [lengths, targets, out.at[pl.ds(0, reqs)]], sems
    )
    copies[1].wait()
    slots, part = targets.shape[1], hidden.shape[2]
    row = lax.broadcasted_iota(jnp.int32, (slots, part), 0)
    lane = lax.broadcasted_iota(jnp.int32, (slots, part), 1)
    high = lax.shift_right_logical(targets[...], 7)
    low = targets[...] - high * 128
    block = jnp.zeros((reqs, part), jnp.float32)
    for first, values in ((1, high), (1 + slots, low)):
        spot = (lane == row + first).astype(jnp.float32).astype(jnp.bfloat16)
        values = values.astype(jnp.float32).astype(jnp.bfloat16)
        block = block + jnp.dot(values, spot, preferred_element_type=jnp.float32)
    row = lax.broadcasted_iota(jnp.int32, (reqs, part), 0)
    lane = lax.broadcasted_iota(jnp.int32, (reqs, part), 1)
    copies[0].wait()
    for r in range(reqs):
        here = jnp.logical_and(row == r, lane == 0)
        block = jnp.where(here, lengths[r].astype(jnp.float32), block)
    out[reqs] = block.astype(jnp.bfloat16)
    copies[2].wait()


def select_kernel(dp, ids, plan_far, *refs):
    parts, (out, facts, own, plan, sems) = list(refs[: 2 * dp]), refs[2 * dp :]
    plan_copy, copy = fetch([plan_far, parts[0]], [plan, own], sems)
    parts[0] = own
    rows = out.shape[1]
    reqs, slots, _ = own.shape
    here = reqs * slots
    me = ids[0]
    for k in range(dp):
        facts[k] = parts[dp + k][reqs].astype(jnp.float32)
    lengths = [facts[k][:, 0:1].astype(jnp.int32) for k in range(dp)]
    lengths = jnp.concatenate(lengths, axis=0)
    row = lax.broadcasted_iota(jnp.int32, (reqs, here), 0)
    slot = jnp.concatenate([row + (me ^ k) * reqs for k in range(dp)], axis=0)
    position = lax.rem(lax.broadcasted_iota(jnp.int32, (1, here), 1), slots)
    wanted = me * rows + lax.broadcasted_iota(jnp.int32, (rows, here), 0)
    request = lax.div(lax.broadcasted_iota(jnp.int32, (1, here), 1), slots)
    hots = []
    plan_copy.wait()
    for k in range(dp):
        owner = jnp.zeros((1, here), jnp.int32)
        for r in range(reqs):
            owner = jnp.where(request == r, plan[(me ^ k) * reqs + r], owner)
        start = jnp.sum(jnp.where(slot < owner, lengths, 0), axis=0, keepdims=True)
        live = jnp.sum(jnp.where(slot == owner, lengths, 0), axis=0, keepdims=True)
        code = jnp.where(position < live, start + position, -1)
        hots.append((code == wanted).astype(jnp.float32).astype(jnp.bfloat16))
    copy.wait()
    for m in range(2):
        total = None
        for k in range(dp):
            values = parts[m * dp + k][0:reqs]
            values = values.reshape(-1, values.shape[-1])
            found = jnp.dot(hots[k], values, preferred_element_type=jnp.float32)
            total = found if total is None else total + found
        out[m] = total.astype(out.dtype)


def normalise(values, gain, chip, core, store, copy):
    half = len(values) // 2
    part = values[0].shape[1]
    width = part * len(values)
    values = [v.astype(jnp.float32) for v in values]
    center = sum(jnp.sum(v, axis=1, keepdims=True) for v in values) / width
    values = [v - center for v in values]
    spread = sum(jnp.sum(v * v, axis=1, keepdims=True) for v in values) / width
    scale = lax.rsqrt(spread + epsilon)
    copy.wait()
    for k, v in enumerate(values):
        place = 2 * (chip ^ (k % half)) + (core if k < half else 1 - core)
        store[place] = (v * scale * gain[place]).astype(jnp.bfloat16)
    return values[0]


def blocks_dot(normed, weight, order):
    part = normed.shape[2]
    total = None
    for b, place in enumerate(order):
        rows = weight[b * part : (b + 1) * part, :]
        piece = jnp.dot(normed[place], rows, preferred_element_type=jnp.float32)
        total = piece if total is None else total + piece
    return total


def ffn_kernel(half, ids, *refs):
    parts = refs[6 : 6 + 2 * half]
    keep, send, gains, ups, downs, normed, terms, sems = refs[6 + 2 * half :]
    copies = fetch(
        refs[:6], [store.at[m] for store in (gains, ups, downs) for m in range(2)], sems
    )
    chip, core = ids[1], ids[2]
    part = parts[0].shape[2]
    bases = [
        normalise([part[m] for part in parts], gains.at[m], chip, core, normed.at[m], copies[m])
        for m in range(2)
    ]
    for m in range(2):
        copies[2 + m].wait()
        pre = blocks_dot(normed.at[m], ups.at[m], range(2 * half))
        units = jax.nn.gelu(pre).astype(jnp.bfloat16)
        copies[4 + m].wait()
        full = jnp.dot(units, downs[m], preferred_element_type=jnp.float32)
        for b in range(2 * half):
            terms[m, b] = full[:, b * part : (b + 1) * part]
        for k in range(half):
            place = 2 * (chip ^ k)
            kept = terms[m, place + core]
            keep[k, m] = kept + bases[m] if k == 0 else kept
            send[k, m] = terms[m, place + 1 - core].astype(jnp.bfloat16)


def pair_kernel(ids, keep, came, own, *outs):
    own[...] = keep[0] + came[0].astype(jnp.float32)
    for k, out in enumerate(outs):
        out[...] = (keep[k + 1] + came[k + 1].astype(jnp.float32)).astype(jnp.bfloat16)


def score_kernel(half, dp, ids, *refs):
    parts = refs[2 : 2 + 2 * half]
    *outs, partial, tail, gains, normed, out_store, sems = refs[2 + 2 * half :]
    here = dp - 1
    copies = fetch(
        [refs[0], refs[1], outs[0], outs[here]],
        [store.at[m] for store in (gains, out_store) for m in range(2)],
        sems,
    )
    me, chip, core = ids[0], ids[1], ids[2]
    ratio = 2 * half // dp
    part = parts[0].shape[2]
    for m in range(2):
        values = [part[m] for part in parts]
        normalise(values, gains.at[m], chip, core, normed.at[m], copies[m])
        for b in range(ratio):
            tail[m, :, b * part : (b + 1) * part] = normed[m, (me ^ here) * ratio + b]
    for m in range(2):
        logits = None
        for k in [*range(1, here), 0]:
            if k == 0:
                copies[2 + m].wait()
                outs[m * here] = out_store.at[m]
            order = [(me ^ k) * ratio + b for b in range(ratio)]
            piece = blocks_dot(normed.at[m], outs[m * here + k], order)
            logits = piece if logits is None else logits + piece
        partial[m] = logits


def finish_kernel(ids, wanted, partial, tail, last_policy, last_reference, stats):
    lane = lax.broadcasted_iota(jnp.int32, (tail.shape[1], 128), 1)
    table = jnp.zeros(lane.shape, jnp.float32)
    for m, last in enumerate((last_policy, last_reference)):
        logits = partial[m] + jnp.dot(tail[m], last[...], preferred_element_type=jnp.float32)
        entries = lax.broadcasted_iota(jnp.int32, logits.shape, 1) + ids[3] * logits.shape[1]
        picked = jnp.sum(jnp.where(entries == wanted[...], logits, 0.0), axis=1, keepdims=True)
        top = jnp.max(logits, axis=1, keepdims=True)
        total = jnp.sum(jnp.exp(logits - top), axis=1, keepdims=True)
        table = jnp.where(lane == m, top, table)
        table = jnp.where(lane == 2 + m, total, table)
        table = jnp.where(lane == 4 + m, picked, table)
    stats[...] = jnp.transpose(table)[:8]


def merge(tables):
    top = functools.reduce(jnp.maximum, [t[0:2] for t in tables])
    total = sum(t[2:4] * jnp.exp(t[0:2] - top) for t in tables)
    return top, total, sum(t[4:6] for t in tables)


def merge_kernel(ids, *refs):
    out = refs[-1]
    out[0:2], out[2:4], out[4:6] = merge(refs[:-1])
    out[6:8] = jnp.zeros((2, out.shape[1]), jnp.float32)


def last_kernel(ids, *refs):
    out = refs[-1]
    top, total, picked = merge(refs[:-1])
    logprob = picked - (top + jnp.log(total))
    out[...] = logprob[0:1] - logprob[1:2]


def local(
    hidden_policy,
    hidden_reference,
    ffn_gain_policy,
    ffn_gain_reference,
    up_policy,
    up_reference,
    down_policy,
    down_reference,
    final_gain_policy,
    final_gain_reference,
    out_policy,
    out_reference,
    move_plan,
    lengths,
    targets,
):
    dp = lax.axis_size("dp")
    mp = lax.axis_size("mp")
    half = mp // 2
    dp_index = lax.axis_index("dp")
    mp_index = lax.axis_index("mp")
    ids = jnp.stack([dp_index, mp_index // 2, mp_index % 2, mp_index]).astype(jnp.int32)
    reqs, slots, part = hidden_policy.shape
    here = reqs * slots
    rows = here // 2
    ffn_gains = (ffn_gain_policy, ffn_gain_reference)
    final_gains = (final_gain_policy, final_gain_reference)
    gains = [gain.reshape(mp, 1, part) for gain in (*ffn_gains, *final_gains)]
    bits = [1 << b for b in range(dp.bit_length() - 1)]

    bit_orders = []
    for m in range(2):
        bit_orders.append([bits[(b ^ m) if (b ^ m) < len(bits) else b] for b in range(len(bits))])

    def spread_step(blocks, step, places):
        for m in range(2):
            bit = bit_orders[m][step]
            for k in [k for k in blocks[m] if places(m, k)]:
                blocks[m][k ^ bit] = exchange(blocks[m][k], "dp", bit)

    packed = call(
        pack_kernel,
        jax.ShapeDtypeStruct((reqs + 1, slots, part), jnp.bfloat16),
        (lengths, targets, hidden_reference),
        [
            pltpu.SMEM(lengths.shape, jnp.int32),
            pltpu.VMEM(targets.shape, jnp.int32),
            pltpu.SemaphoreType.DMA((3,)),
        ],
        far=(0, 1, 2),
    )
    hiddens = [{0: hidden_policy}, {0: packed}]
    outs = [{0: out_policy}, {0: out_reference}]

    def wait_for(first, places):
        flat = [(m, k) for m in range(2) for k in outs[m] if places(m, k)]
        first, values = lax.optimization_barrier((first, [outs[m][k] for m, k in flat]))
        for (m, k), value in zip(flat, values):
            outs[m][k] = value
        return first

    for step in range(len(bits)):
        spread_step(hiddens, step, lambda m, k: k == 0)
        if step:
            blocks, place = hiddens[0], bit_orders[0][step]
            passed = [k for k in blocks if 0 < k and not k & place]
            values = [blocks[k] for k in passed]
            blocks[place], values = lax.optimization_barrier((blocks[place], values))
            blocks.update(zip(passed, values))
        spread_step(hiddens, step, lambda m, k: 0 < k and not k & bit_orders[m][step])
    early = [(m, b) for m in range(2) for b in bits]
    values = wait_for([hiddens[m][b] for m, b in early], lambda m, k: True)
    for (m, b), value in zip(early, values):
        hiddens[m][b] = value
    spread_step(outs, 0, lambda m, k: True)
    hidden_parts = [hiddens[m][k] for m in range(2) for k in range(dp)]

    order = jnp.arange(dp, dtype=jnp.int32)
    moved, facts = call(
        functools.partial(select_kernel, dp),
        (
            jax.ShapeDtypeStruct((2, rows, part), jnp.bfloat16),
            jax.ShapeDtypeStruct((dp, reqs, part), jnp.float32),
        ),
        (ids, move_plan, *hidden_parts),
        [
            pltpu.VMEM(hidden_policy.shape, jnp.bfloat16),
            pltpu.SMEM(move_plan.shape, jnp.int32),
            pltpu.SemaphoreType.DMA((2,)),
        ],
        far=(1, 2),
        cost=10000000000,
    )

    facts = facts[:, :, : 2 * slots + 1].astype(jnp.int32)
    all_lengths = facts[:, :, 0].reshape(-1)
    all_targets = (facts[:, :, 1 : slots + 1] * 128 + facts[:, :, slots + 1 :]).reshape(-1)
    slot_ids = ((order ^ dp_index)[:, None] * reqs + jnp.arange(reqs, dtype=jnp.int32)).reshape(-1)
    positions = jnp.arange(slots, dtype=jnp.int32)

    def codes(slot):
        start = jnp.sum(jnp.where(slot_ids[None] < slot[:, None], all_lengths[None], 0), axis=1)
        live = jnp.sum(jnp.where(slot_ids[None] == slot[:, None], all_lengths[None], 0), axis=1)
        return jnp.where(
            positions[None] < live[:, None], start[:, None] + positions[None], jnp.int32(-1)
        )

    far = sorted(range(1, half), key=lambda k: (k.bit_length() <= 1, k))

    def gather_pair(own):
        same = {0: own}
        for k in far:
            same[k] = exchange(own, "mp", 2 * k)
        same = [same[k] for k in range(half)]
        return same + [exchange(v, "mp", 1) for v in same]

    parts = gather_pair(moved)
    if len(bits) > 1:
        parts[-1] = wait_for(parts[-1], lambda m, k: k == 0)
        later = [{0: outs[m][0]} for m in range(2)]
        spread_step(later, 1, lambda m, k: True)
    gain_scratch = pltpu.VMEM((2, mp, 1, part), jnp.float32)
    block = jax.ShapeDtypeStruct((2, rows, part), jnp.bfloat16)
    keep, send = call(
        functools.partial(ffn_kernel, half),
        (
            jax.ShapeDtypeStruct((half, 2, rows, part), jnp.float32),
            jax.ShapeDtypeStruct((half, 2, rows, part), jnp.bfloat16),
        ),
        (ids, *gains[:2], up_policy, up_reference, down_policy, down_reference, *parts),
        [
            gain_scratch,
            pltpu.VMEM((2,) + up_policy.shape, jnp.bfloat16),
            pltpu.VMEM((2,) + down_policy.shape, jnp.bfloat16),
            pltpu.VMEM((2, mp, rows, part), jnp.bfloat16),
            pltpu.VMEM((2, mp, rows, part), jnp.float32),
            pltpu.SemaphoreType.DMA((6,)),
        ],
        far=range(1, 7),
        mib=15,
    )
    send = wait_for(send, lambda m, k: k > 0)
    came = exchange(send, "mp", 1)
    own, *pieces = call(
        pair_kernel,
        (jax.ShapeDtypeStruct((2, rows, part), jnp.float32),) + (block,) * (half - 1),
        (ids, keep, came),
    )
    arrived = {k: exchange(pieces[k - 1], "mp", 2 * k) for k in far}
    if len(bits) > 1:
        for m in range(2):
            outs[m].update(later[m])
        arrived[far[0]] = wait_for(arrived[far[0]], lambda m, k: True)
        spread_step(outs, 1, lambda m, k: k == bit_orders[m][0])
    for k in range(1, half):
        own = own + arrived[k].astype(jnp.float32)
    stream = own.astype(jnp.bfloat16)
    for step in range(2, len(bits)):
        stream = wait_for(stream, lambda m, k: True)
        spread_step(outs, step, lambda m, k: True)

    owner_code = codes(slot_ids).reshape(-1)
    my_ranks = dp_index * rows + jnp.arange(rows, dtype=jnp.int32)
    wanted = jnp.sum(
        jnp.where(owner_code[None] == my_ranks[:, None], all_targets[None], 0),
        axis=1,
        keepdims=True,
    )
    partial, tail = call(
        functools.partial(score_kernel, half, dp),
        (
            jax.ShapeDtypeStruct((2, rows, out_policy.shape[1]), jnp.float32),
            jax.ShapeDtypeStruct((2, rows, out_policy.shape[0]), jnp.bfloat16),
        ),
        (
            ids,
            *gains[2:],
            *gather_pair(stream),
            *[outs[m][k] for m in range(2) for k in range(dp - 1)],
        ),
        [
            gain_scratch,
            pltpu.VMEM((2, mp, rows, part), jnp.bfloat16),
            pltpu.VMEM((2,) + out_policy.shape, jnp.bfloat16),
            pltpu.SemaphoreType.DMA((4,)),
        ],
        far=(1, 2, 3 + mp, 2 + mp + dp),
        mib=8,
    )
    stats = call(
        finish_kernel,
        jax.ShapeDtypeStruct((8, rows), jnp.float32),
        (ids, wanted, partial, tail, outs[0][dp - 1], outs[1][dp - 1]),
        mib=8,
    )
    stats = call(
        merge_kernel,
        jax.ShapeDtypeStruct((8, rows), jnp.float32),
        (ids, stats, exchange(stats, "mp", 1)),
    )
    diff = call(
        last_kernel,
        jax.ShapeDtypeStruct((1, rows), jnp.float32),
        (ids, stats, *[exchange(stats, "mp", 2 * k) for k in range(half - 1, 0, -1)]),
    )
    came = [exchange(diff, "dp", k) for k in range(dp - 1, 0, -1)]
    diff = jnp.concatenate(came + [diff])
    ranks = ((order[::-1] ^ dp_index)[:, None] * rows + jnp.arange(rows, dtype=jnp.int32)).reshape(-1)
    my_code = codes(dp_index * reqs + jnp.arange(reqs, dtype=jnp.int32))
    hit = my_code[:, :, None] == ranks[None, None]
    token_diff = jnp.sum(jnp.where(hit, diff.reshape(1, 1, -1), 0.0), axis=2)
    return (token_diff, jnp.sum(token_diff, axis=1))


def solution(mesh):
    return jax.shard_map(
        local,
        mesh=mesh,
        in_specs=(
            P("dp", None, "mp"),
            P("dp", None, "mp"),
            P(),
            P(),
            P(None, "mp"),
            P(None, "mp"),
            P("mp", None),
            P("mp", None),
            P(),
            P(),
            P("dp", "mp"),
            P("dp", "mp"),
            P(),
            P("dp"),
            P("dp", None),
        ),
        out_specs=(P("dp", None), P("dp")),
        check_vma=False,
    )
```

```python
import functools

import jax
import jax.numpy as jnp
from jax import lax
from jax.experimental import pallas as pl
from jax.experimental.pallas import tpu as pltpu
from jax.sharding import PartitionSpec as P

epsilon = 1e-05
vmem = pl.BlockSpec(memory_space=pltpu.VMEM)
smem = pl.BlockSpec(memory_space=pltpu.SMEM)
anywhere = pl.BlockSpec(memory_space=pltpu.HBM)


def call(kernel, out_shape, ops, scratch=(), far=(), mib=4, cost=None):
    specs = [anywhere if i in far else vmem if i else smem for i in range(len(ops))]
    ops = [
        pltpu.with_memory_space_constraint(op, pltpu.HBM) if i in far else op
        for i, op in enumerate(ops)
    ]
    return pl.pallas_call(
        kernel,
        out_shape=out_shape,
        in_specs=specs,
        out_specs=jax.tree.map(lambda _: vmem, out_shape),
        scratch_shapes=list(scratch),
        cost_estimate=cost and pl.CostEstimate(flops=cost, bytes_accessed=0, transcendentals=0),
        compiler_params=pltpu.CompilerParams(vmem_limit_bytes=mib * 1024 * 1024),
    )(*ops)


def exchange(values, axis, flip):
    count = lax.axis_size(axis)
    return lax.ppermute(values, axis, [(i, i ^ flip) for i in range(count)])


def fetch(sources, targets, sems):
    copies = [
        pltpu.make_async_copy(source, target, sems.at[i])
        for i, (source, target) in enumerate(zip(sources, targets))
    ]
    for copy in copies:
        copy.start()
    return copies


def pack_kernel(lengths_far, targets_far, hidden, out, lengths, targets, sems):
    reqs = hidden.shape[0]
    copies = fetch(
        [lengths_far, targets_far, hidden], [lengths, targets, out.at[pl.ds(0, reqs)]], sems
    )
    copies[1].wait()
    slots, part = targets.shape[1], hidden.shape[2]
    row = lax.broadcasted_iota(jnp.int32, (slots, part), 0)
    lane = lax.broadcasted_iota(jnp.int32, (slots, part), 1)
    high = lax.shift_right_logical(targets[...], 7)
    low = targets[...] - high * 128
    block = jnp.zeros((reqs, part), jnp.float32)
    for first, values in ((1, high), (1 + slots, low)):
        spot = (lane == row + first).astype(jnp.float32).astype(jnp.bfloat16)
        values = values.astype(jnp.float32).astype(jnp.bfloat16)
        block = block + jnp.dot(values, spot, preferred_element_type=jnp.float32)
    row = lax.broadcasted_iota(jnp.int32, (reqs, part), 0)
    lane = lax.broadcasted_iota(jnp.int32, (reqs, part), 1)
    copies[0].wait()
    for r in range(reqs):
        here = jnp.logical_and(row == r, lane == 0)
        block = jnp.where(here, lengths[r].astype(jnp.float32), block)
    out[reqs] = block.astype(jnp.bfloat16)
    copies[2].wait()


def select_kernel(dp, ids, plan_far, *refs):
    parts, (out, facts, own, plan, sems) = list(refs[: 2 * dp]), refs[2 * dp :]
    plan_copy, copy = fetch([plan_far, parts[0]], [plan, own], sems)
    parts[0] = own
    rows = out.shape[1]
    reqs, slots, _ = own.shape
    here = reqs * slots
    me = ids[0]
    for k in range(dp):
        facts[k] = parts[dp + k][reqs].astype(jnp.float32)
    lengths = [facts[k][:, 0:1].astype(jnp.int32) for k in range(dp)]
    lengths = jnp.concatenate(lengths, axis=0)
    row = lax.broadcasted_iota(jnp.int32, (reqs, here), 0)
    slot = jnp.concatenate([row + (me ^ k) * reqs for k in range(dp)], axis=0)
    position = lax.rem(lax.broadcasted_iota(jnp.int32, (1, here), 1), slots)
    wanted = me * rows + lax.broadcasted_iota(jnp.int32, (rows, here), 0)
    request = lax.div(lax.broadcasted_iota(jnp.int32, (1, here), 1), slots)
    hots = []
    plan_copy.wait()
    for k in range(dp):
        owner = jnp.zeros((1, here), jnp.int32)
        for r in range(reqs):
            owner = jnp.where(request == r, plan[(me ^ k) * reqs + r], owner)
        start = jnp.sum(jnp.where(slot < owner, lengths, 0), axis=0, keepdims=True)
        live = jnp.sum(jnp.where(slot == owner, lengths, 0), axis=0, keepdims=True)
        code = jnp.where(position < live, start + position, -1)
        hots.append((code == wanted).astype(jnp.float32).astype(jnp.bfloat16))
    copy.wait()
    for m in range(2):
        total = None
        for k in range(dp):
            values = parts[m * dp + k][0:reqs]
            values = values.reshape(-1, values.shape[-1])
            found = jnp.dot(hots[k], values, preferred_element_type=jnp.float32)
            total = found if total is None else total + found
        out[m] = total.astype(out.dtype)


def normalise(values, gain, chip, core, store, copy):
    half = len(values) // 2
    part = values[0].shape[1]
    width = part * len(values)
    values = [v.astype(jnp.float32) for v in values]
    center = sum(jnp.sum(v, axis=1, keepdims=True) for v in values) / width
    values = [v - center for v in values]
    spread = sum(jnp.sum(v * v, axis=1, keepdims=True) for v in values) / width
    scale = lax.rsqrt(spread + epsilon)
    copy.wait()
    for k, v in enumerate(values):
        place = 2 * (chip ^ (k % half)) + (core if k < half else 1 - core)
        store[place] = (v * scale * gain[place]).astype(jnp.bfloat16)
    return values[0]


def blocks_dot(normed, weight, order):
    part = normed.shape[2]
    total = None
    for b, place in enumerate(order):
        rows = weight[b * part : (b + 1) * part, :]
        piece = jnp.dot(normed[place], rows, preferred_element_type=jnp.float32)
        total = piece if total is None else total + piece
    return total


def ffn_kernel(half, ids, *refs):
    parts = refs[6 : 6 + 2 * half]
    keep, send, gains, ups, downs, normed, terms, sems = refs[6 + 2 * half :]
    copies = fetch(
        refs[:6], [store.at[m] for store in (gains, ups, downs) for m in range(2)], sems
    )
    chip, core = ids[1], ids[2]
    part = parts[0].shape[2]
    bases = [
        normalise([part[m] for part in parts], gains.at[m], chip, core, normed.at[m], copies[m])
        for m in range(2)
    ]
    for m in range(2):
        copies[2 + m].wait()
        pre = blocks_dot(normed.at[m], ups.at[m], range(2 * half))
        units = jax.nn.gelu(pre).astype(jnp.bfloat16)
        copies[4 + m].wait()
        full = jnp.dot(units, downs[m], preferred_element_type=jnp.float32)
        for b in range(2 * half):
            terms[m, b] = full[:, b * part : (b + 1) * part]
        for k in range(half):
            place = 2 * (chip ^ k)
            kept = terms[m, place + core]
            keep[k, m] = kept + bases[m] if k == 0 else kept
            send[k, m] = terms[m, place + 1 - core].astype(jnp.bfloat16)


def pair_kernel(ids, keep, came, own, *outs):
    own[...] = keep[0] + came[0].astype(jnp.float32)
    for k, out in enumerate(outs):
        out[...] = (keep[k + 1] + came[k + 1].astype(jnp.float32)).astype(jnp.bfloat16)


def score_kernel(half, dp, ids, *refs):
    parts = refs[2 : 2 + 2 * half]
    *outs, partial, tail, gains, normed, out_store, sems = refs[2 + 2 * half :]
    here = dp - 1
    copies = fetch(
        [refs[0], refs[1], outs[0], outs[here]],
        [store.at[m] for store in (gains, out_store) for m in range(2)],
        sems,
    )
    me, chip, core = ids[0], ids[1], ids[2]
    ratio = 2 * half // dp
    part = parts[0].shape[2]
    for m in range(2):
        values = [part[m] for part in parts]
        normalise(values, gains.at[m], chip, core, normed.at[m], copies[m])
        for b in range(ratio):
            tail[m, :, b * part : (b + 1) * part] = normed[m, (me ^ here) * ratio + b]
    for m in range(2):
        logits = None
        for k in [*range(1, here), 0]:
            if k == 0:
                copies[2 + m].wait()
                outs[m * here] = out_store.at[m]
            order = [(me ^ k) * ratio + b for b in range(ratio)]
            piece = blocks_dot(normed.at[m], outs[m * here + k], order)
            logits = piece if logits is None else logits + piece
        partial[m] = logits


def finish_kernel(ids, wanted, partial, tail, last_policy, last_reference, stats):
    lane = lax.broadcasted_iota(jnp.int32, (tail.shape[1], 128), 1)
    table = jnp.zeros(lane.shape, jnp.float32)
    for m, last in enumerate((last_policy, last_reference)):
        logits = partial[m] + jnp.dot(tail[m], last[...], preferred_element_type=jnp.float32)
        entries = lax.broadcasted_iota(jnp.int32, logits.shape, 1) + ids[3] * logits.shape[1]
        picked = jnp.sum(jnp.where(entries == wanted[...], logits, 0.0), axis=1, keepdims=True)
        top = jnp.max(logits, axis=1, keepdims=True)
        total = jnp.sum(jnp.exp(logits - top), axis=1, keepdims=True)
        table = jnp.where(lane == m, top, table)
        table = jnp.where(lane == 2 + m, total, table)
        table = jnp.where(lane == 4 + m, picked, table)
    stats[...] = jnp.transpose(table)[:8]


def merge(tables):
    top = functools.reduce(jnp.maximum, [t[0:2] for t in tables])
    total = sum(t[2:4] * jnp.exp(t[0:2] - top) for t in tables)
    return top, total, sum(t[4:6] for t in tables)


def merge_kernel(ids, *refs):
    out = refs[-1]
    out[0:2], out[2:4], out[4:6] = merge(refs[:-1])
    out[6:8] = jnp.zeros((2, out.shape[1]), jnp.float32)


def last_kernel(ids, *refs):
    out = refs[-1]
    top, total, picked = merge(refs[:-1])
    logprob = picked - (top + jnp.log(total))
    out[...] = logprob[0:1] - logprob[1:2]


def local(
    hidden_policy,
    hidden_reference,
    ffn_gain_policy,
    ffn_gain_reference,
    up_policy,
    up_reference,
    down_policy,
    down_reference,
    final_gain_policy,
    final_gain_reference,
    out_policy,
    out_reference,
    move_plan,
    lengths,
    targets,
):
    dp = lax.axis_size("dp")
    mp = lax.axis_size("mp")
    half = mp // 2
    dp_index = lax.axis_index("dp")
    mp_index = lax.axis_index("mp")
    ids = jnp.stack([dp_index, mp_index // 2, mp_index % 2, mp_index]).astype(jnp.int32)
    reqs, slots, part = hidden_policy.shape
    here = reqs * slots
    rows = here // 2
    ffn_gains = (ffn_gain_policy, ffn_gain_reference)
    final_gains = (final_gain_policy, final_gain_reference)
    gains = [gain.reshape(mp, 1, part) for gain in (*ffn_gains, *final_gains)]
    bits = [1 << b for b in range(dp.bit_length() - 1)]

    bit_orders = []
    for m in range(2):
        bit_orders.append([bits[(b ^ m) if (b ^ m) < len(bits) else b] for b in range(len(bits))])

    def spread_step(blocks, step, places):
        for m in range(2):
            bit = bit_orders[m][step]
            for k in [k for k in blocks[m] if places(m, k)]:
                blocks[m][k ^ bit] = exchange(blocks[m][k], "dp", bit)

    packed = call(
        pack_kernel,
        jax.ShapeDtypeStruct((reqs + 1, slots, part), jnp.bfloat16),
        (lengths, targets, hidden_reference),
        [
            pltpu.SMEM(lengths.shape, jnp.int32),
            pltpu.VMEM(targets.shape, jnp.int32),
            pltpu.SemaphoreType.DMA((3,)),
        ],
        far=(0, 1, 2),
    )
    hiddens = [{0: hidden_policy}, {0: packed}]
    outs = [{0: out_policy}, {0: out_reference}]

    def wait_for(first, places):
        flat = [(m, k) for m in range(2) for k in outs[m] if places(m, k)]
        first, values = lax.optimization_barrier((first, [outs[m][k] for m, k in flat]))
        for (m, k), value in zip(flat, values):
            outs[m][k] = value
        return first

    for step in range(len(bits)):
        spread_step(hiddens, step, lambda m, k: k == 0)
        if step:
            blocks, place = hiddens[0], bit_orders[0][step]
            passed = [k for k in blocks if 0 < k and not k & place]
            values = [blocks[k] for k in passed]
            blocks[place], values = lax.optimization_barrier((blocks[place], values))
            blocks.update(zip(passed, values))
        spread_step(hiddens, step, lambda m, k: 0 < k and not k & bit_orders[m][step])
    early = [(m, b) for m in range(2) for b in bits]
    values = wait_for([hiddens[m][b] for m, b in early], lambda m, k: True)
    for (m, b), value in zip(early, values):
        hiddens[m][b] = value
    spread_step(outs, 0, lambda m, k: True)
    hidden_parts = [hiddens[m][k] for m in range(2) for k in range(dp)]

    order = jnp.arange(dp, dtype=jnp.int32)
    moved, facts = call(
        functools.partial(select_kernel, dp),
        (
            jax.ShapeDtypeStruct((2, rows, part), jnp.bfloat16),
            jax.ShapeDtypeStruct((dp, reqs, part), jnp.float32),
        ),
        (ids, move_plan, *hidden_parts),
        [
            pltpu.VMEM(hidden_policy.shape, jnp.bfloat16),
            pltpu.SMEM(move_plan.shape, jnp.int32),
            pltpu.SemaphoreType.DMA((2,)),
        ],
        far=(1, 2),
        cost=10000000000,
    )

    facts = facts[:, :, : 2 * slots + 1].astype(jnp.int32)
    all_lengths = facts[:, :, 0].reshape(-1)
    all_targets = (facts[:, :, 1 : slots + 1] * 128 + facts[:, :, slots + 1 :]).reshape(-1)
    slot_ids = ((order ^ dp_index)[:, None] * reqs + jnp.arange(reqs, dtype=jnp.int32)).reshape(-1)
    positions = jnp.arange(slots, dtype=jnp.int32)

    def codes(slot):
        start = jnp.sum(jnp.where(slot_ids[None] < slot[:, None], all_lengths[None], 0), axis=1)
        live = jnp.sum(jnp.where(slot_ids[None] == slot[:, None], all_lengths[None], 0), axis=1)
        return jnp.where(
            positions[None] < live[:, None], start[:, None] + positions[None], jnp.int32(-1)
        )

    far = sorted(range(1, half), key=lambda k: (k.bit_length() <= 1, k))

    def gather_pair(own):
        same = {0: own}
        for k in far:
            same[k] = exchange(own, "mp", 2 * k)
        same = [same[k] for k in range(half)]
        return same + [exchange(v, "mp", 1) for v in same]

    parts = gather_pair(moved)
    if len(bits) > 1:
        parts[-1] = wait_for(parts[-1], lambda m, k: k == 0)
        later = [{0: outs[m][0]} for m in range(2)]
        spread_step(later, 1, lambda m, k: True)
    gain_scratch = pltpu.VMEM((2, mp, 1, part), jnp.float32)
    block = jax.ShapeDtypeStruct((2, rows, part), jnp.bfloat16)
    keep, send = call(
        functools.partial(ffn_kernel, half),
        (
            jax.ShapeDtypeStruct((half, 2, rows, part), jnp.float32),
            jax.ShapeDtypeStruct((half, 2, rows, part), jnp.bfloat16),
        ),
        (ids, *gains[:2], up_policy, up_reference, down_policy, down_reference, *parts),
        [
            gain_scratch,
            pltpu.VMEM((2,) + up_policy.shape, jnp.bfloat16),
            pltpu.VMEM((2,) + down_policy.shape, jnp.bfloat16),
            pltpu.VMEM((2, mp, rows, part), jnp.bfloat16),
            pltpu.VMEM((2, mp, rows, part), jnp.float32),
            pltpu.SemaphoreType.DMA((6,)),
        ],
        far=range(1, 7),
        mib=22,
    )
    send = wait_for(send, lambda m, k: k > 0)
    came = exchange(send, "mp", 1)
    own, *pieces = call(
        pair_kernel,
        (jax.ShapeDtypeStruct((2, rows, part), jnp.float32),) + (block,) * (half - 1),
        (ids, keep, came),
    )
    arrived = {k: exchange(pieces[k - 1], "mp", 2 * k) for k in far}
    if len(bits) > 1:
        for m in range(2):
            outs[m].update(later[m])
        arrived[far[0]] = wait_for(arrived[far[0]], lambda m, k: True)
        spread_step(outs, 1, lambda m, k: k == bit_orders[m][0])
    for k in range(1, half):
        own = own + arrived[k].astype(jnp.float32)
    stream = own.astype(jnp.bfloat16)
    for step in range(2, len(bits)):
        stream = wait_for(stream, lambda m, k: True)
        spread_step(outs, step, lambda m, k: True)

    owner_code = codes(slot_ids).reshape(-1)
    my_ranks = dp_index * rows + jnp.arange(rows, dtype=jnp.int32)
    wanted = jnp.sum(
        jnp.where(owner_code[None] == my_ranks[:, None], all_targets[None], 0),
        axis=1,
        keepdims=True,
    )
    partial, tail = call(
        functools.partial(score_kernel, half, dp),
        (
            jax.ShapeDtypeStruct((2, rows, out_policy.shape[1]), jnp.float32),
            jax.ShapeDtypeStruct((2, rows, out_policy.shape[0]), jnp.bfloat16),
        ),
        (
            ids,
            *gains[2:],
            *gather_pair(stream),
            *[outs[m][k] for m in range(2) for k in range(dp - 1)],
        ),
        [
            gain_scratch,
            pltpu.VMEM((2, mp, rows, part), jnp.bfloat16),
            pltpu.VMEM((2,) + out_policy.shape, jnp.bfloat16),
            pltpu.SemaphoreType.DMA((4,)),
        ],
        far=(1, 2, 3 + mp, 2 + mp + dp),
        mib=14,
    )
    stats = call(
        finish_kernel,
        jax.ShapeDtypeStruct((8, rows), jnp.float32),
        (ids, wanted, partial, tail, outs[0][dp - 1], outs[1][dp - 1]),
        mib=8,
    )
    stats = call(
        merge_kernel,
        jax.ShapeDtypeStruct((8, rows), jnp.float32),
        (ids, stats, exchange(stats, "mp", 1)),
    )
    diff = call(
        last_kernel,
        jax.ShapeDtypeStruct((1, rows), jnp.float32),
        (ids, stats, *[exchange(stats, "mp", 2 * k) for k in range(half - 1, 0, -1)]),
    )
    came = [exchange(diff, "dp", k) for k in range(dp - 1, 0, -1)]
    diff = jnp.concatenate(came + [diff])
    ranks = ((order[::-1] ^ dp_index)[:, None] * rows + jnp.arange(rows, dtype=jnp.int32)).reshape(-1)
    my_code = codes(dp_index * reqs + jnp.arange(reqs, dtype=jnp.int32))
    hit = my_code[:, :, None] == ranks[None, None]
    token_diff = jnp.sum(jnp.where(hit, diff.reshape(1, 1, -1), 0.0), axis=2)
    return (token_diff, jnp.sum(token_diff, axis=1))


def solution(mesh):
    return jax.shard_map(
        local,
        mesh=mesh,
        in_specs=(
            P("dp", None, "mp"),
            P("dp", None, "mp"),
            P(),
            P(),
            P(None, "mp"),
            P(None, "mp"),
            P("mp", None),
            P("mp", None),
            P(),
            P(),
            P("dp", "mp"),
            P("dp", "mp"),
            P(),
            P("dp"),
            P("dp", None),
        ),
        out_specs=(P("dp", None), P("dp")),
        check_vma=False,
    )
```

```python
import functools

import jax
import jax.numpy as jnp
from jax import lax
from jax.experimental import pallas as pl
from jax.experimental.pallas import tpu as pltpu
from jax.sharding import PartitionSpec as P

epsilon = 1e-05
vmem = pl.BlockSpec(memory_space=pltpu.VMEM)
smem = pl.BlockSpec(memory_space=pltpu.SMEM)
anywhere = pl.BlockSpec(memory_space=pltpu.HBM)


def call(kernel, out_shape, ops, scratch=(), far=(), mib=4, cost=None):
    specs = [anywhere if i in far else vmem if i else smem for i in range(len(ops))]
    ops = [
        pltpu.with_memory_space_constraint(op, pltpu.HBM) if i in far else op
        for i, op in enumerate(ops)
    ]
    return pl.pallas_call(
        kernel,
        out_shape=out_shape,
        in_specs=specs,
        out_specs=jax.tree.map(lambda _: vmem, out_shape),
        scratch_shapes=list(scratch),
        cost_estimate=cost and pl.CostEstimate(flops=cost, bytes_accessed=0, transcendentals=0),
        compiler_params=pltpu.CompilerParams(vmem_limit_bytes=mib * 1024 * 1024),
    )(*ops)


def exchange(values, axis, flip):
    count = lax.axis_size(axis)
    return lax.ppermute(values, axis, [(i, i ^ flip) for i in range(count)])


def fetch(sources, targets, sems):
    copies = [
        pltpu.make_async_copy(source, target, sems.at[i])
        for i, (source, target) in enumerate(zip(sources, targets))
    ]
    for copy in copies:
        copy.start()
    return copies


def pack_kernel(lengths_far, targets_far, hidden, out, lengths, targets, sems):
    reqs = hidden.shape[0]
    copies = fetch(
        [lengths_far, targets_far, hidden], [lengths, targets, out.at[pl.ds(0, reqs)]], sems
    )
    copies[1].wait()
    slots, part = targets.shape[1], hidden.shape[2]
    row = lax.broadcasted_iota(jnp.int32, (slots, part), 0)
    lane = lax.broadcasted_iota(jnp.int32, (slots, part), 1)
    high = lax.shift_right_logical(targets[...], 7)
    low = targets[...] - high * 128
    block = jnp.zeros((reqs, part), jnp.float32)
    for first, values in ((1, high), (1 + slots, low)):
        spot = (lane == row + first).astype(jnp.float32).astype(jnp.bfloat16)
        values = values.astype(jnp.float32).astype(jnp.bfloat16)
        block = block + jnp.dot(values, spot, preferred_element_type=jnp.float32)
    row = lax.broadcasted_iota(jnp.int32, (reqs, part), 0)
    lane = lax.broadcasted_iota(jnp.int32, (reqs, part), 1)
    copies[0].wait()
    for r in range(reqs):
        here = jnp.logical_and(row == r, lane == 0)
        block = jnp.where(here, lengths[r].astype(jnp.float32), block)
    out[reqs] = block.astype(jnp.bfloat16)
    copies[2].wait()


def select_kernel(dp, ids, plan_far, *refs):
    parts, (out, picks, marks, own, plan, sems) = list(refs[: 2 * dp]), refs[2 * dp :]
    plan_copy, copy = fetch([plan_far, parts[0]], [plan, own], sems)
    parts[0] = own
    rows = out.shape[1]
    reqs, slots, _ = own.shape
    here = reqs * slots
    me = ids[0]
    facts = jnp.concatenate([parts[dp + k][reqs].astype(jnp.float32) for k in range(dp)], axis=0)
    lengths = facts[:, 0:1].astype(jnp.int32)
    row = lax.broadcasted_iota(jnp.int32, (reqs, here), 0)
    slot = jnp.concatenate([row + (me ^ k) * reqs for k in range(dp)], axis=0)
    position = lax.rem(lax.broadcasted_iota(jnp.int32, (1, here), 1), slots)
    wanted = me * rows + lax.broadcasted_iota(jnp.int32, (rows, here), 0)
    request = lax.div(lax.broadcasted_iota(jnp.int32, (1, here), 1), slots)
    hots = []
    plan_copy.wait()
    for k in range(dp):
        owner = jnp.zeros((1, here), jnp.int32)
        for r in range(reqs):
            owner = jnp.where(request == r, plan[(me ^ k) * reqs + r], owner)
        start = jnp.sum(jnp.where(slot < owner, lengths, 0), axis=0, keepdims=True)
        live = jnp.sum(jnp.where(slot == owner, lengths, 0), axis=0, keepdims=True)
        code = jnp.where(position < live, start + position, -1)
        hots.append((code == wanted).astype(jnp.float32).astype(jnp.bfloat16))
    copy.wait()
    for m in range(2):
        total = None
        for k in range(dp):
            values = parts[m * dp + k][0:reqs]
            values = values.reshape(-1, values.shape[-1])
            found = jnp.dot(hots[k], values, preferred_element_type=jnp.float32)
            total = found if total is None else total + found
        out[m] = total.astype(out.dtype)

    count = dp * reqs
    down = lax.broadcasted_iota(jnp.int32, (reqs, count), 0)
    along = lax.broadcasted_iota(jnp.int32, (1, count), 1)
    here_slot = lax.rem(along, reqs)
    for k in range(dp):
        here_slot = jnp.where(lax.div(along, reqs) == k, here_slot + (me ^ k) * reqs, here_slot)
    slot = jnp.concatenate([down + (me ^ k) * reqs for k in range(dp)], axis=0)
    start = jnp.sum(jnp.where(slot < here_slot, lengths, 0), axis=0, keepdims=True)
    live = jnp.sum(jnp.where(slot == here_slot, lengths, 0), axis=0, keepdims=True)

    rank = me * rows + lax.broadcasted_iota(jnp.int32, (rows, count), 0)
    held = jnp.logical_and(rank >= start, rank < start + live)
    first = jnp.sum(jnp.where(held, start, 0), axis=1, keepdims=True)
    spot = rank[:, 0:1] - first
    held = held.astype(jnp.float32).astype(jnp.bfloat16)
    rows_of = jnp.dot(held, facts.astype(jnp.bfloat16), preferred_element_type=jnp.float32)
    lane = lax.broadcasted_iota(jnp.int32, rows_of.shape, 1)
    high = jnp.sum(jnp.where(lane == spot + 1, rows_of, 0.0), axis=1, keepdims=True)
    low = jnp.sum(jnp.where(lane == spot + 1 + slots, rows_of, 0.0), axis=1, keepdims=True)
    picks[...] = (high * 128.0 + low).astype(jnp.int32)

    mine = me * reqs + down
    begin = jnp.sum(jnp.where(here_slot < mine, live, 0), axis=1, keepdims=True)
    length = jnp.sum(jnp.where(here_slot == mine, live, 0), axis=1, keepdims=True)
    position = lax.broadcasted_iota(jnp.int32, (reqs, slots), 1)
    marks[...] = jnp.where(position < length, begin + position, -1)


def normalise(values, gain, chip, core, store, copy):
    half = len(values) // 2
    part = values[0].shape[1]
    width = part * len(values)
    values = [v.astype(jnp.float32) for v in values]
    center = sum(jnp.sum(v, axis=1, keepdims=True) for v in values) / width
    values = [v - center for v in values]
    spread = sum(jnp.sum(v * v, axis=1, keepdims=True) for v in values) / width
    scale = lax.rsqrt(spread + epsilon)
    copy.wait()
    for k, v in enumerate(values):
        place = 2 * (chip ^ (k % half)) + (core if k < half else 1 - core)
        store[place] = (v * scale * gain[place]).astype(jnp.bfloat16)
    return values[0]


def blocks_dot(normed, weight, order):
    part = normed.shape[2]
    total = None
    for b, place in enumerate(order):
        rows = weight[b * part : (b + 1) * part, :]
        piece = jnp.dot(normed[place], rows, preferred_element_type=jnp.float32)
        total = piece if total is None else total + piece
    return total


def ffn_kernel(half, ids, *refs):
    parts = refs[6 : 6 + 2 * half]
    keep, send, gains, ups, downs, normed, terms, sems = refs[6 + 2 * half :]
    copies = fetch(
        refs[:6], [store.at[m] for store in (gains, ups, downs) for m in range(2)], sems
    )
    chip, core = ids[1], ids[2]
    part = parts[0].shape[2]
    bases = [
        normalise([part[m] for part in parts], gains.at[m], chip, core, normed.at[m], copies[m])
        for m in range(2)
    ]
    for m in range(2):
        copies[2 + m].wait()
        pre = blocks_dot(normed.at[m], ups.at[m], range(2 * half))
        units = jax.nn.gelu(pre).astype(jnp.bfloat16)
        copies[4 + m].wait()
        full = jnp.dot(units, downs[m], preferred_element_type=jnp.float32)
        for b in range(2 * half):
            terms[m, b] = full[:, b * part : (b + 1) * part]
        for k in range(half):
            place = 2 * (chip ^ k)
            kept = terms[m, place + core]
            keep[k, m] = kept + bases[m] if k == 0 else kept
            send[k, m] = terms[m, place + 1 - core].astype(jnp.bfloat16)


def pair_kernel(ids, keep, came, own, *outs):
    own[...] = keep[0] + came[0].astype(jnp.float32)
    for k, out in enumerate(outs):
        out[...] = (keep[k + 1] + came[k + 1].astype(jnp.float32)).astype(jnp.bfloat16)


def score_kernel(half, dp, ids, *refs):
    parts = refs[2 : 2 + 2 * half]
    *outs, partial, tail, gains, normed, out_store, sems = refs[2 + 2 * half :]
    here = dp - 1
    copies = fetch(
        [refs[0], refs[1], outs[0], outs[here]],
        [store.at[m] for store in (gains, out_store) for m in range(2)],
        sems,
    )
    me, chip, core = ids[0], ids[1], ids[2]
    ratio = 2 * half // dp
    part = parts[0].shape[2]
    for m in range(2):
        values = [part[m] for part in parts]
        normalise(values, gains.at[m], chip, core, normed.at[m], copies[m])
        for b in range(ratio):
            tail[m, :, b * part : (b + 1) * part] = normed[m, (me ^ here) * ratio + b]
    for m in range(2):
        logits = None
        for k in [*range(1, here), 0]:
            if k == 0:
                copies[2 + m].wait()
                outs[m * here] = out_store.at[m]
            order = [(me ^ k) * ratio + b for b in range(ratio)]
            piece = blocks_dot(normed.at[m], outs[m * here + k], order)
            logits = piece if logits is None else logits + piece
        partial[m] = logits


def finish_kernel(ids, wanted, partial, tail, last_policy, last_reference, stats):
    lane = lax.broadcasted_iota(jnp.int32, (tail.shape[1], 128), 1)
    table = jnp.zeros(lane.shape, jnp.float32)
    for m, last in enumerate((last_policy, last_reference)):
        logits = partial[m] + jnp.dot(tail[m], last[...], preferred_element_type=jnp.float32)
        entries = lax.broadcasted_iota(jnp.int32, logits.shape, 1) + ids[3] * logits.shape[1]
        picked = jnp.sum(jnp.where(entries == wanted[...], logits, 0.0), axis=1, keepdims=True)
        top = jnp.max(logits, axis=1, keepdims=True)
        total = jnp.sum(jnp.exp(logits - top), axis=1, keepdims=True)
        table = jnp.where(lane == m, top, table)
        table = jnp.where(lane == 2 + m, total, table)
        table = jnp.where(lane == 4 + m, picked, table)
    stats[...] = jnp.transpose(table)[:8]


def merge(tables):
    top = functools.reduce(jnp.maximum, [t[0:2] for t in tables])
    total = sum(t[2:4] * jnp.exp(t[0:2] - top) for t in tables)
    return top, total, sum(t[4:6] for t in tables)


def merge_kernel(ids, *refs):
    out = refs[-1]
    out[0:2], out[2:4], out[4:6] = merge(refs[:-1])
    out[6:8] = jnp.zeros((2, out.shape[1]), jnp.float32)


def last_kernel(ids, *refs):
    out = refs[-1]
    top, total, picked = merge(refs[:-1])
    logprob = picked - (top + jnp.log(total))
    out[...] = logprob[0:1] - logprob[1:2]


def place_kernel(dp, ids, marks, *refs):
    *diffs, tokens, sums = refs
    reqs, slots = marks.shape
    rows = diffs[0].shape[1]
    along = lax.broadcasted_iota(jnp.int32, (1, rows), 1)
    lane = lax.broadcasted_iota(jnp.int32, (reqs, slots), 1)
    codes = marks[...]
    result = jnp.zeros((reqs, slots), jnp.float32)
    for p in range(slots):
        code = codes[:, p : p + 1]
        found = jnp.zeros((reqs, rows), jnp.float32)
        for k in range(dp):
            ranks = (ids[0] ^ ((k + 1) % dp)) * rows + along
            found = jnp.where(code == ranks, diffs[k][...], found)
        value = jnp.sum(found, axis=1, keepdims=True)
        result = jnp.where(lane == p, value, result)
    tokens[...] = result
    total = jnp.sum(result, axis=1, keepdims=True)
    down = lax.broadcasted_iota(jnp.int32, (reqs, reqs), 0)
    across = lax.broadcasted_iota(jnp.int32, (reqs, reqs), 1)
    sums[...] = jnp.sum(jnp.where(down == across, total, 0.0), axis=0, keepdims=True)


def local(
    hidden_policy,
    hidden_reference,
    ffn_gain_policy,
    ffn_gain_reference,
    up_policy,
    up_reference,
    down_policy,
    down_reference,
    final_gain_policy,
    final_gain_reference,
    out_policy,
    out_reference,
    move_plan,
    lengths,
    targets,
):
    dp = lax.axis_size("dp")
    mp = lax.axis_size("mp")
    half = mp // 2
    dp_index = lax.axis_index("dp")
    mp_index = lax.axis_index("mp")
    ids = jnp.stack([dp_index, mp_index // 2, mp_index % 2, mp_index]).astype(jnp.int32)
    reqs, slots, part = hidden_policy.shape
    here = reqs * slots
    rows = here // 2
    ffn_gains = (ffn_gain_policy, ffn_gain_reference)
    final_gains = (final_gain_policy, final_gain_reference)
    gains = [gain.reshape(mp, 1, part) for gain in (*ffn_gains, *final_gains)]
    bits = [1 << b for b in range(dp.bit_length() - 1)]

    bit_orders = []
    for m in range(2):
        bit_orders.append([bits[(b ^ m) if (b ^ m) < len(bits) else b] for b in range(len(bits))])

    def spread_step(blocks, step, places):
        for m in range(2):
            bit = bit_orders[m][step]
            for k in [k for k in blocks[m] if places(m, k)]:
                blocks[m][k ^ bit] = exchange(blocks[m][k], "dp", bit)

    packed = call(
        pack_kernel,
        jax.ShapeDtypeStruct((reqs + 1, slots, part), jnp.bfloat16),
        (lengths, targets, hidden_reference),
        [
            pltpu.SMEM(lengths.shape, jnp.int32),
            pltpu.VMEM(targets.shape, jnp.int32),
            pltpu.SemaphoreType.DMA((3,)),
        ],
        far=(0, 1, 2),
    )
    hiddens = [{0: hidden_policy}, {0: packed}]
    outs = [{0: out_policy}, {0: out_reference}]

    def wait_for(first, places):
        flat = [(m, k) for m in range(2) for k in outs[m] if places(m, k)]
        first, values = lax.optimization_barrier((first, [outs[m][k] for m, k in flat]))
        for (m, k), value in zip(flat, values):
            outs[m][k] = value
        return first

    for step in range(len(bits)):
        spread_step(hiddens, step, lambda m, k: k == 0)
        if step:
            blocks, place = hiddens[0], bit_orders[0][step]
            passed = [k for k in blocks if 0 < k and not k & place]
            values = [blocks[k] for k in passed]
            blocks[place], values = lax.optimization_barrier((blocks[place], values))
            blocks.update(zip(passed, values))
        spread_step(hiddens, step, lambda m, k: 0 < k and not k & bit_orders[m][step])
    early = [(m, b) for m in range(2) for b in bits]
    values = wait_for([hiddens[m][b] for m, b in early], lambda m, k: True)
    for (m, b), value in zip(early, values):
        hiddens[m][b] = value
    spread_step(outs, 0, lambda m, k: True)
    hidden_parts = [hiddens[m][k] for m in range(2) for k in range(dp)]

    moved, wanted, marks = call(
        functools.partial(select_kernel, dp),
        (
            jax.ShapeDtypeStruct((2, rows, part), jnp.bfloat16),
            jax.ShapeDtypeStruct((rows, 1), jnp.int32),
            jax.ShapeDtypeStruct((reqs, slots), jnp.int32),
        ),
        (ids, move_plan, *hidden_parts),
        [
            pltpu.VMEM(hidden_policy.shape, jnp.bfloat16),
            pltpu.SMEM(move_plan.shape, jnp.int32),
            pltpu.SemaphoreType.DMA((2,)),
        ],
        far=(1, 2),
        cost=10000000000,
    )

    far = sorted(range(1, half), key=lambda k: (k.bit_length() <= 1, k))

    def gather_pair(own):
        same = {0: own}
        for k in far:
            same[k] = exchange(own, "mp", 2 * k)
        same = [same[k] for k in range(half)]
        return same + [exchange(v, "mp", 1) for v in same]

    parts = gather_pair(moved)
    if len(bits) > 1:
        parts[-1] = wait_for(parts[-1], lambda m, k: k == 0)
        later = [{0: outs[m][0]} for m in range(2)]
        spread_step(later, 1, lambda m, k: True)
    gain_scratch = pltpu.VMEM((2, mp, 1, part), jnp.float32)
    block = jax.ShapeDtypeStruct((2, rows, part), jnp.bfloat16)
    keep, send = call(
        functools.partial(ffn_kernel, half),
        (
            jax.ShapeDtypeStruct((half, 2, rows, part), jnp.float32),
            jax.ShapeDtypeStruct((half, 2, rows, part), jnp.bfloat16),
        ),
        (ids, *gains[:2], up_policy, up_reference, down_policy, down_reference, *parts),
        [
            gain_scratch,
            pltpu.VMEM((2,) + up_policy.shape, jnp.bfloat16),
            pltpu.VMEM((2,) + down_policy.shape, jnp.bfloat16),
            pltpu.VMEM((2, mp, rows, part), jnp.bfloat16),
            pltpu.VMEM((2, mp, rows, part), jnp.float32),
            pltpu.SemaphoreType.DMA((6,)),
        ],
        far=range(1, 7),
        mib=22,
    )
    send = wait_for(send, lambda m, k: k > 0)
    came = exchange(send, "mp", 1)
    own, *pieces = call(
        pair_kernel,
        (jax.ShapeDtypeStruct((2, rows, part), jnp.float32),) + (block,) * (half - 1),
        (ids, keep, came),
    )
    arrived = {k: exchange(pieces[k - 1], "mp", 2 * k) for k in far}
    if len(bits) > 1:
        for m in range(2):
            outs[m].update(later[m])
        arrived[far[0]] = wait_for(arrived[far[0]], lambda m, k: True)
        spread_step(outs, 1, lambda m, k: k == bit_orders[m][0])
    for k in range(1, half):
        own = own + arrived[k].astype(jnp.float32)
    stream = own.astype(jnp.bfloat16)
    for step in range(2, len(bits)):
        stream = wait_for(stream, lambda m, k: True)
        spread_step(outs, step, lambda m, k: True)

    partial, tail = call(
        functools.partial(score_kernel, half, dp),
        (
            jax.ShapeDtypeStruct((2, rows, out_policy.shape[1]), jnp.float32),
            jax.ShapeDtypeStruct((2, rows, out_policy.shape[0]), jnp.bfloat16),
        ),
        (
            ids,
            *gains[2:],
            *gather_pair(stream),
            *[outs[m][k] for m in range(2) for k in range(dp - 1)],
        ),
        [
            gain_scratch,
            pltpu.VMEM((2, mp, rows, part), jnp.bfloat16),
            pltpu.VMEM((2,) + out_policy.shape, jnp.bfloat16),
            pltpu.SemaphoreType.DMA((4,)),
        ],
        far=(1, 2, 3 + mp, 2 + mp + dp),
        mib=14,
    )
    stats = call(
        finish_kernel,
        jax.ShapeDtypeStruct((8, rows), jnp.float32),
        (ids, wanted, partial, tail, outs[0][dp - 1], outs[1][dp - 1]),
        mib=8,
    )
    stats = call(
        merge_kernel,
        jax.ShapeDtypeStruct((8, rows), jnp.float32),
        (ids, stats, exchange(stats, "mp", 1)),
    )
    diff = call(
        last_kernel,
        jax.ShapeDtypeStruct((1, rows), jnp.float32),
        (ids, stats, *[exchange(stats, "mp", 2 * k) for k in range(1, half)]),
    )
    came = [exchange(diff, "dp", k) for k in range(1, dp)]
    token_diff, seq_diff = call(
        functools.partial(place_kernel, dp),
        (
            jax.ShapeDtypeStruct((reqs, slots), jnp.float32),
            jax.ShapeDtypeStruct((1, reqs), jnp.float32),
        ),
        (ids, marks, *came, diff),
    )
    return (token_diff, seq_diff.reshape(reqs))


def solution(mesh):
    return jax.shard_map(
        local,
        mesh=mesh,
        in_specs=(
            P("dp", None, "mp"),
            P("dp", None, "mp"),
            P(),
            P(),
            P(None, "mp"),
            P(None, "mp"),
            P("mp", None),
            P("mp", None),
            P(),
            P(),
            P("dp", "mp"),
            P("dp", "mp"),
            P(),
            P("dp"),
            P("dp", None),
        ),
        out_specs=(P("dp", None), P("dp")),
        check_vma=False,
    )
```

```python
import functools

import jax
import jax.numpy as jnp
from jax import lax
from jax.experimental import pallas as pl
from jax.experimental.pallas import tpu as pltpu
from jax.sharding import PartitionSpec as P

epsilon = 1e-05
vmem = pl.BlockSpec(memory_space=pltpu.VMEM)
smem = pl.BlockSpec(memory_space=pltpu.SMEM)
anywhere = pl.BlockSpec(memory_space=pltpu.HBM)


def call(kernel, out_shape, ops, scratch=(), far=(), mib=4, cost=None):
    specs = [anywhere if i in far else vmem if i else smem for i in range(len(ops))]
    ops = [
        pltpu.with_memory_space_constraint(op, pltpu.HBM) if i in far else op
        for i, op in enumerate(ops)
    ]
    return pl.pallas_call(
        kernel,
        out_shape=out_shape,
        in_specs=specs,
        out_specs=jax.tree.map(lambda _: vmem, out_shape),
        scratch_shapes=list(scratch),
        cost_estimate=cost and pl.CostEstimate(flops=cost, bytes_accessed=0, transcendentals=0),
        compiler_params=pltpu.CompilerParams(vmem_limit_bytes=mib * 1024 * 1024),
    )(*ops)


def exchange(values, axis, flip):
    count = lax.axis_size(axis)
    return lax.ppermute(values, axis, [(i, i ^ flip) for i in range(count)])


def fetch(sources, targets, sems):
    copies = [
        pltpu.make_async_copy(source, target, sems.at[i])
        for i, (source, target) in enumerate(zip(sources, targets))
    ]
    for copy in copies:
        copy.start()
    return copies


def pack_kernel(lengths_far, targets_far, hidden, out, lengths, targets, sems):
    reqs = hidden.shape[0]
    copies = fetch(
        [lengths_far, targets_far, hidden], [lengths, targets, out.at[pl.ds(0, reqs)]], sems
    )
    copies[1].wait()
    slots, part = targets.shape[1], hidden.shape[2]
    row = lax.broadcasted_iota(jnp.int32, (slots, part), 0)
    lane = lax.broadcasted_iota(jnp.int32, (slots, part), 1)
    high = lax.shift_right_logical(targets[...], 7)
    low = targets[...] - high * 128
    block = jnp.zeros((reqs, part), jnp.float32)
    for first, values in ((1, high), (1 + slots, low)):
        spot = (lane == row + first).astype(jnp.float32).astype(jnp.bfloat16)
        values = values.astype(jnp.float32).astype(jnp.bfloat16)
        block = block + jnp.dot(values, spot, preferred_element_type=jnp.float32)
    row = lax.broadcasted_iota(jnp.int32, (reqs, part), 0)
    lane = lax.broadcasted_iota(jnp.int32, (reqs, part), 1)
    copies[0].wait()
    for r in range(reqs):
        here = jnp.logical_and(row == r, lane == 0)
        block = jnp.where(here, lengths[r].astype(jnp.float32), block)
    out[reqs] = block.astype(jnp.bfloat16)
    copies[2].wait()


def select_kernel(dp, ids, plan_far, *refs):
    parts, (out, picks, marks, own, plan, sems) = list(refs[: 2 * dp]), refs[2 * dp :]
    plan_copy, copy = fetch([plan_far, parts[0]], [plan, own], sems)
    parts[0] = own
    rows = out.shape[1]
    reqs, slots, _ = own.shape
    here = reqs * slots
    me = ids[0]
    facts = jnp.concatenate([parts[dp + k][reqs].astype(jnp.float32) for k in range(dp)], axis=0)
    lengths = facts[:, 0:1].astype(jnp.int32)
    row = lax.broadcasted_iota(jnp.int32, (reqs, here), 0)
    slot = jnp.concatenate([row + (me ^ k) * reqs for k in range(dp)], axis=0)
    position = lax.rem(lax.broadcasted_iota(jnp.int32, (1, here), 1), slots)
    wanted = me * rows + lax.broadcasted_iota(jnp.int32, (rows, here), 0)
    request = lax.div(lax.broadcasted_iota(jnp.int32, (1, here), 1), slots)
    hots = []
    plan_copy.wait()
    for k in range(dp):
        owner = jnp.zeros((1, here), jnp.int32)
        for r in range(reqs):
            owner = jnp.where(request == r, plan[(me ^ k) * reqs + r], owner)
        start = jnp.sum(jnp.where(slot < owner, lengths, 0), axis=0, keepdims=True)
        live = jnp.sum(jnp.where(slot == owner, lengths, 0), axis=0, keepdims=True)
        code = jnp.where(position < live, start + position, -1)
        hots.append((code == wanted).astype(jnp.float32).astype(jnp.bfloat16))
    copy.wait()
    for m in range(2):
        total = None
        for k in range(dp):
            values = parts[m * dp + k][0:reqs]
            values = values.reshape(-1, values.shape[-1])
            found = jnp.dot(hots[k], values, preferred_element_type=jnp.float32)
            total = found if total is None else total + found
        out[m] = total.astype(out.dtype)

    count = dp * reqs
    down = lax.broadcasted_iota(jnp.int32, (reqs, count), 0)
    along = lax.broadcasted_iota(jnp.int32, (1, count), 1)
    here_slot = lax.rem(along, reqs)
    for k in range(dp):
        here_slot = jnp.where(lax.div(along, reqs) == k, here_slot + (me ^ k) * reqs, here_slot)
    slot = jnp.concatenate([down + (me ^ k) * reqs for k in range(dp)], axis=0)
    start = jnp.sum(jnp.where(slot < here_slot, lengths, 0), axis=0, keepdims=True)
    live = jnp.sum(jnp.where(slot == here_slot, lengths, 0), axis=0, keepdims=True)

    rank = me * rows + lax.broadcasted_iota(jnp.int32, (rows, count), 0)
    held = jnp.logical_and(rank >= start, rank < start + live)
    first = jnp.sum(jnp.where(held, start, 0), axis=1, keepdims=True)
    spot = rank[:, 0:1] - first
    held = held.astype(jnp.float32).astype(jnp.bfloat16)
    rows_of = jnp.dot(held, facts.astype(jnp.bfloat16), preferred_element_type=jnp.float32)
    lane = lax.broadcasted_iota(jnp.int32, rows_of.shape, 1)
    high = jnp.sum(jnp.where(lane == spot + 1, rows_of, 0.0), axis=1, keepdims=True)
    low = jnp.sum(jnp.where(lane == spot + 1 + slots, rows_of, 0.0), axis=1, keepdims=True)
    picks[...] = (high * 128.0 + low).astype(jnp.int32)

    mine = me * reqs + down
    begin = jnp.sum(jnp.where(here_slot < mine, live, 0), axis=1, keepdims=True)
    length = jnp.sum(jnp.where(here_slot == mine, live, 0), axis=1, keepdims=True)
    position = lax.broadcasted_iota(jnp.int32, (reqs, slots), 1)
    marks[...] = jnp.where(position < length, begin + position, -1)


def normalise(values, gain, chip, core, store, copy):
    half = len(values) // 2
    part = values[0].shape[1]
    width = part * len(values)
    values = [v.astype(jnp.float32) for v in values]
    center = sum(jnp.sum(v, axis=1, keepdims=True) for v in values) / width
    values = [v - center for v in values]
    spread = sum(jnp.sum(v * v, axis=1, keepdims=True) for v in values) / width
    scale = lax.rsqrt(spread + epsilon)
    copy.wait()
    for k, v in enumerate(values):
        place = 2 * (chip ^ (k % half)) + (core if k < half else 1 - core)
        store[place] = (v * scale * gain[place]).astype(jnp.bfloat16)
    return values[0]


def blocks_dot(normed, weight, order):
    part = normed.shape[2]
    total = None
    for b, place in enumerate(order):
        rows = weight[b * part : (b + 1) * part, :]
        piece = jnp.dot(normed[place], rows, preferred_element_type=jnp.float32)
        total = piece if total is None else total + piece
    return total


def ffn_kernel(half, ids, *refs):
    parts = refs[6 : 6 + 2 * half]
    keep, send, gains, ups, downs, normed, terms, sems = refs[6 + 2 * half :]
    copies = fetch(
        refs[:6], [store.at[m] for store in (gains, ups, downs) for m in range(2)], sems
    )
    chip, core = ids[1], ids[2]
    part = parts[0].shape[2]
    bases = [
        normalise([part[m] for part in parts], gains.at[m], chip, core, normed.at[m], copies[m])
        for m in range(2)
    ]
    for m in range(2):
        copies[2 + m].wait()
        pre = blocks_dot(normed.at[m], ups.at[m], range(2 * half))
        units = jax.nn.gelu(pre).astype(jnp.bfloat16)
        copies[4 + m].wait()
        full = jnp.dot(units, downs[m], preferred_element_type=jnp.float32)
        for b in range(2 * half):
            terms[m, b] = full[:, b * part : (b + 1) * part]
        for k in range(half):
            place = 2 * (chip ^ k)
            kept = terms[m, place + core]
            keep[k, m] = kept + bases[m] if k == 0 else kept
            send[k, m] = terms[m, place + 1 - core].astype(jnp.bfloat16)


def pair_kernel(ids, keep, came, own, *outs):
    own[...] = keep[0] + came[0].astype(jnp.float32)
    for k, out in enumerate(outs):
        out[...] = (keep[k + 1] + came[k + 1].astype(jnp.float32)).astype(jnp.bfloat16)


def score_kernel(half, dp, ids, *refs):
    parts = refs[2 : 2 + 2 * half]
    *outs, partial, tail, gains, normed, out_store, sems = refs[2 + 2 * half :]
    here = dp - 1
    copies = fetch(
        [refs[0], refs[1], outs[0], outs[here]],
        [store.at[m] for store in (gains, out_store) for m in range(2)],
        sems,
    )
    me, chip, core = ids[0], ids[1], ids[2]
    ratio = 2 * half // dp
    part = parts[0].shape[2]
    for m in range(2):
        values = [part[m] for part in parts]
        normalise(values, gains.at[m], chip, core, normed.at[m], copies[m])
        for b in range(ratio):
            tail[m, :, b * part : (b + 1) * part] = normed[m, (me ^ here) * ratio + b]
    for m in range(2):
        logits = None
        for k in [*range(1, here), 0]:
            if k == 0:
                copies[2 + m].wait()
                outs[m * here] = out_store.at[m]
            order = [(me ^ k) * ratio + b for b in range(ratio)]
            piece = blocks_dot(normed.at[m], outs[m * here + k], order)
            logits = piece if logits is None else logits + piece
        partial[m] = logits


def finish_kernel(ids, wanted, partial, tail, last_policy, last_reference, stats):
    lane = lax.broadcasted_iota(jnp.int32, (tail.shape[1], 128), 1)
    table = jnp.zeros(lane.shape, jnp.float32)
    for m, last in enumerate((last_policy, last_reference)):
        logits = partial[m] + jnp.dot(tail[m], last[...], preferred_element_type=jnp.float32)
        entries = lax.broadcasted_iota(jnp.int32, logits.shape, 1) + ids[3] * logits.shape[1]
        picked = jnp.sum(jnp.where(entries == wanted[...], logits, 0.0), axis=1, keepdims=True)
        top = jnp.max(logits, axis=1, keepdims=True)
        total = jnp.sum(jnp.exp(logits - top), axis=1, keepdims=True)
        table = jnp.where(lane == m, top, table)
        table = jnp.where(lane == 2 + m, total, table)
        table = jnp.where(lane == 4 + m, picked, table)
    stats[...] = jnp.transpose(table)[:8]


def merge(tables):
    top = functools.reduce(jnp.maximum, [t[0:2] for t in tables])
    total = sum(t[2:4] * jnp.exp(t[0:2] - top) for t in tables)
    return top, total, sum(t[4:6] for t in tables)


def merge_kernel(ids, *refs):
    out = refs[-1]
    out[0:2], out[2:4], out[4:6] = merge(refs[:-1])
    out[6:8] = jnp.zeros((2, out.shape[1]), jnp.float32)


def last_kernel(ids, *refs):
    out = refs[-1]
    top, total, picked = merge(refs[:-1])
    logprob = picked - (top + jnp.log(total))
    out[...] = logprob[0:1] - logprob[1:2]


def local(
    hidden_policy,
    hidden_reference,
    ffn_gain_policy,
    ffn_gain_reference,
    up_policy,
    up_reference,
    down_policy,
    down_reference,
    final_gain_policy,
    final_gain_reference,
    out_policy,
    out_reference,
    move_plan,
    lengths,
    targets,
):
    dp = lax.axis_size("dp")
    mp = lax.axis_size("mp")
    half = mp // 2
    dp_index = lax.axis_index("dp")
    mp_index = lax.axis_index("mp")
    ids = jnp.stack([dp_index, mp_index // 2, mp_index % 2, mp_index]).astype(jnp.int32)
    reqs, slots, part = hidden_policy.shape
    here = reqs * slots
    rows = here // 2
    ffn_gains = (ffn_gain_policy, ffn_gain_reference)
    final_gains = (final_gain_policy, final_gain_reference)
    gains = [gain.reshape(mp, 1, part) for gain in (*ffn_gains, *final_gains)]
    bits = [1 << b for b in range(dp.bit_length() - 1)]

    bit_orders = []
    for m in range(2):
        bit_orders.append([bits[(b ^ m) if (b ^ m) < len(bits) else b] for b in range(len(bits))])

    def spread_step(blocks, step, places):
        for m in range(2):
            bit = bit_orders[m][step]
            for k in [k for k in blocks[m] if places(m, k)]:
                blocks[m][k ^ bit] = exchange(blocks[m][k], "dp", bit)

    packed = call(
        pack_kernel,
        jax.ShapeDtypeStruct((reqs + 1, slots, part), jnp.bfloat16),
        (lengths, targets, hidden_reference),
        [
            pltpu.SMEM(lengths.shape, jnp.int32),
            pltpu.VMEM(targets.shape, jnp.int32),
            pltpu.SemaphoreType.DMA((3,)),
        ],
        far=(0, 1, 2),
    )
    hiddens = [{0: hidden_policy}, {0: packed}]
    outs = [{0: out_policy}, {0: out_reference}]

    def wait_for(first, places):
        flat = [(m, k) for m in range(2) for k in outs[m] if places(m, k)]
        first, values = lax.optimization_barrier((first, [outs[m][k] for m, k in flat]))
        for (m, k), value in zip(flat, values):
            outs[m][k] = value
        return first

    for step in range(len(bits)):
        spread_step(hiddens, step, lambda m, k: k == 0)
        if step:
            blocks, place = hiddens[0], bit_orders[0][step]
            passed = [k for k in blocks if 0 < k and not k & place]
            values = [blocks[k] for k in passed]
            blocks[place], values = lax.optimization_barrier((blocks[place], values))
            blocks.update(zip(passed, values))
        spread_step(hiddens, step, lambda m, k: 0 < k and not k & bit_orders[m][step])
    early = [(m, b) for m in range(2) for b in bits]
    values = wait_for([hiddens[m][b] for m, b in early], lambda m, k: True)
    for (m, b), value in zip(early, values):
        hiddens[m][b] = value
    spread_step(outs, 0, lambda m, k: True)
    hidden_parts = [hiddens[m][k] for m in range(2) for k in range(dp)]

    moved, wanted, marks = call(
        functools.partial(select_kernel, dp),
        (
            jax.ShapeDtypeStruct((2, rows, part), jnp.bfloat16),
            jax.ShapeDtypeStruct((rows, 1), jnp.int32),
            jax.ShapeDtypeStruct((reqs, slots), jnp.int32),
        ),
        (ids, move_plan, *hidden_parts),
        [
            pltpu.VMEM(hidden_policy.shape, jnp.bfloat16),
            pltpu.SMEM(move_plan.shape, jnp.int32),
            pltpu.SemaphoreType.DMA((2,)),
        ],
        far=(1, 2),
        cost=10000000000,
    )

    far = sorted(range(1, half), key=lambda k: (k.bit_length() <= 1, k))

    def gather_pair(own):
        same = {0: own}
        for k in far:
            same[k] = exchange(own, "mp", 2 * k)
        passed = lax.optimization_barrier([same[k] for k in far])
        same.update(zip(far, passed))
        same = [same[k] for k in range(half)]
        return same + [exchange(v, "mp", 1) for v in same]

    parts = gather_pair(moved)
    if len(bits) > 1:
        parts[-1] = wait_for(parts[-1], lambda m, k: k == 0)
        later = [{0: outs[m][0]} for m in range(2)]
        spread_step(later, 1, lambda m, k: True)
    gain_scratch = pltpu.VMEM((2, mp, 1, part), jnp.float32)
    block = jax.ShapeDtypeStruct((2, rows, part), jnp.bfloat16)
    keep, send = call(
        functools.partial(ffn_kernel, half),
        (
            jax.ShapeDtypeStruct((half, 2, rows, part), jnp.float32),
            jax.ShapeDtypeStruct((half, 2, rows, part), jnp.bfloat16),
        ),
        (ids, *gains[:2], up_policy, up_reference, down_policy, down_reference, *parts),
        [
            gain_scratch,
            pltpu.VMEM((2,) + up_policy.shape, jnp.bfloat16),
            pltpu.VMEM((2,) + down_policy.shape, jnp.bfloat16),
            pltpu.VMEM((2, mp, rows, part), jnp.bfloat16),
            pltpu.VMEM((2, mp, rows, part), jnp.float32),
            pltpu.SemaphoreType.DMA((6,)),
        ],
        far=range(1, 7),
        mib=22,
    )
    send = wait_for(send, lambda m, k: k > 0)
    came = exchange(send, "mp", 1)
    own, *pieces = call(
        pair_kernel,
        (jax.ShapeDtypeStruct((2, rows, part), jnp.float32),) + (block,) * (half - 1),
        (ids, keep, came),
    )
    arrived = {k: exchange(pieces[k - 1], "mp", 2 * k) for k in far}
    if len(bits) > 1:
        for m in range(2):
            outs[m].update(later[m])
        arrived = wait_for(arrived, lambda m, k: True)
        spread_step(outs, 1, lambda m, k: k == bit_orders[m][0])
    for k in range(1, half):
        own = own + arrived[k].astype(jnp.float32)
    stream = own.astype(jnp.bfloat16)
    for step in range(2, len(bits)):
        stream = wait_for(stream, lambda m, k: True)
        spread_step(outs, step, lambda m, k: True)

    partial, tail = call(
        functools.partial(score_kernel, half, dp),
        (
            jax.ShapeDtypeStruct((2, rows, out_policy.shape[1]), jnp.float32),
            jax.ShapeDtypeStruct((2, rows, out_policy.shape[0]), jnp.bfloat16),
        ),
        (
            ids,
            *gains[2:],
            *gather_pair(stream),
            *[outs[m][k] for m in range(2) for k in range(dp - 1)],
        ),
        [
            gain_scratch,
            pltpu.VMEM((2, mp, rows, part), jnp.bfloat16),
            pltpu.VMEM((2,) + out_policy.shape, jnp.bfloat16),
            pltpu.SemaphoreType.DMA((4,)),
        ],
        far=(1, 2, 3 + mp, 2 + mp + dp),
        mib=14,
    )
    stats = call(
        finish_kernel,
        jax.ShapeDtypeStruct((8, rows), jnp.float32),
        (ids, wanted, partial, tail, outs[0][dp - 1], outs[1][dp - 1]),
        mib=8,
    )
    stats = call(
        merge_kernel,
        jax.ShapeDtypeStruct((8, rows), jnp.float32),
        (ids, stats, exchange(stats, "mp", 1)),
    )
    diff = call(
        last_kernel,
        jax.ShapeDtypeStruct((1, rows), jnp.float32),
        (ids, stats, *[exchange(stats, "mp", 2 * k) for k in range(half - 1, 0, -1)]),
    )
    came = [exchange(diff, "dp", k) for k in range(dp - 1, 0, -1)]
    places = jnp.arange(dp, dtype=jnp.int32)[::-1] ^ dp_index
    ranks = places[:, None] * rows + jnp.arange(rows, dtype=jnp.int32)
    values = jnp.concatenate(came + [diff])
    hit = marks[:, :, None, None] == ranks
    token_diff = jnp.sum(jnp.where(hit, values, 0.0), axis=(2, 3))
    return (token_diff, jnp.sum(token_diff, axis=1))


def solution(mesh):
    return jax.shard_map(
        local,
        mesh=mesh,
        in_specs=(
            P("dp", None, "mp"),
            P("dp", None, "mp"),
            P(),
            P(),
            P(None, "mp"),
            P(None, "mp"),
            P("mp", None),
            P("mp", None),
            P(),
            P(),
            P("dp", "mp"),
            P("dp", "mp"),
            P(),
            P("dp"),
            P("dp", None),
        ),
        out_specs=(P("dp", None), P("dp")),
        check_vma=False,
    )
```

```python
import functools

import jax
import jax.numpy as jnp
from jax import lax
from jax.experimental import pallas as pl
from jax.experimental.pallas import tpu as pltpu
from jax.sharding import PartitionSpec as P

epsilon = 1e-05
vmem = pl.BlockSpec(memory_space=pltpu.VMEM)
smem = pl.BlockSpec(memory_space=pltpu.SMEM)
anywhere = pl.BlockSpec(memory_space=pltpu.HBM)


def call(kernel, out_shape, ops, scratch=(), far=(), mib=4, cost=None):
    specs = [anywhere if i in far else vmem if i else smem for i in range(len(ops))]
    ops = [
        pltpu.with_memory_space_constraint(op, pltpu.HBM) if i in far else op
        for i, op in enumerate(ops)
    ]
    return pl.pallas_call(
        kernel,
        out_shape=out_shape,
        in_specs=specs,
        out_specs=jax.tree.map(lambda _: vmem, out_shape),
        scratch_shapes=list(scratch),
        cost_estimate=cost and pl.CostEstimate(flops=cost, bytes_accessed=0, transcendentals=0),
        compiler_params=pltpu.CompilerParams(vmem_limit_bytes=mib * 1024 * 1024),
    )(*ops)


def exchange(values, axis, flip):
    count = lax.axis_size(axis)
    return lax.ppermute(values, axis, [(i, i ^ flip) for i in range(count)])


def fetch(sources, targets, sems):
    copies = [
        pltpu.make_async_copy(source, target, sems.at[i])
        for i, (source, target) in enumerate(zip(sources, targets))
    ]
    for copy in copies:
        copy.start()
    return copies


def pack_kernel(lengths_far, targets_far, hidden, out, lengths, targets, sems):
    reqs = hidden.shape[0]
    copies = fetch(
        [lengths_far, targets_far, hidden], [lengths, targets, out.at[pl.ds(0, reqs)]], sems
    )
    copies[1].wait()
    slots, part = targets.shape[1], hidden.shape[2]
    row = lax.broadcasted_iota(jnp.int32, (slots, part), 0)
    lane = lax.broadcasted_iota(jnp.int32, (slots, part), 1)
    high = lax.shift_right_logical(targets[...], 7)
    low = targets[...] - high * 128
    block = jnp.zeros((reqs, part), jnp.float32)
    for first, values in ((1, high), (1 + slots, low)):
        spot = (lane == row + first).astype(jnp.float32).astype(jnp.bfloat16)
        values = values.astype(jnp.float32).astype(jnp.bfloat16)
        block = block + jnp.dot(values, spot, preferred_element_type=jnp.float32)
    row = lax.broadcasted_iota(jnp.int32, (reqs, part), 0)
    lane = lax.broadcasted_iota(jnp.int32, (reqs, part), 1)
    copies[0].wait()
    for r in range(reqs):
        here = jnp.logical_and(row == r, lane == 0)
        block = jnp.where(here, lengths[r].astype(jnp.float32), block)
    out[reqs] = block.astype(jnp.bfloat16)
    copies[2].wait()


def select_kernel(dp, ids, plan_far, *refs):
    parts, (out, facts, own, plan, sems) = list(refs[: 2 * dp]), refs[2 * dp :]
    plan_copy, copy = fetch([plan_far, parts[0]], [plan, own], sems)
    parts[0] = own
    rows = out.shape[1]
    reqs, slots, _ = own.shape
    here = reqs * slots
    me = ids[0]
    for k in range(dp):
        facts[k] = parts[dp + k][reqs].astype(jnp.float32)
    lengths = [facts[k][:, 0:1].astype(jnp.int32) for k in range(dp)]
    lengths = jnp.concatenate(lengths, axis=0)
    row = lax.broadcasted_iota(jnp.int32, (reqs, here), 0)
    slot = jnp.concatenate([row + (me ^ k) * reqs for k in range(dp)], axis=0)
    position = lax.rem(lax.broadcasted_iota(jnp.int32, (1, here), 1), slots)
    wanted = me * rows + lax.broadcasted_iota(jnp.int32, (rows, here), 0)
    request = lax.div(lax.broadcasted_iota(jnp.int32, (1, here), 1), slots)
    hots = []
    plan_copy.wait()
    for k in range(dp):
        owner = jnp.zeros((1, here), jnp.int32)
        for r in range(reqs):
            owner = jnp.where(request == r, plan[(me ^ k) * reqs + r], owner)
        start = jnp.sum(jnp.where(slot < owner, lengths, 0), axis=0, keepdims=True)
        live = jnp.sum(jnp.where(slot == owner, lengths, 0), axis=0, keepdims=True)
        code = jnp.where(position < live, start + position, -1)
        hots.append((code == wanted).astype(jnp.float32).astype(jnp.bfloat16))
    copy.wait()
    for m in range(2):
        total = None
        for k in range(dp):
            values = parts[m * dp + k][0:reqs]
            values = values.reshape(-1, values.shape[-1])
            found = jnp.dot(hots[k], values, preferred_element_type=jnp.float32)
            total = found if total is None else total + found
        out[m] = total.astype(out.dtype)


def normalise(values, gain, chip, core, store, copy):
    half = len(values) // 2
    part = values[0].shape[1]
    width = part * len(values)
    values = [v.astype(jnp.float32) for v in values]
    center = sum(jnp.sum(v, axis=1, keepdims=True) for v in values) / width
    values = [v - center for v in values]
    spread = sum(jnp.sum(v * v, axis=1, keepdims=True) for v in values) / width
    scale = lax.rsqrt(spread + epsilon)
    copy.wait()
    for k, v in enumerate(values):
        place = 2 * (chip ^ (k % half)) + (core if k < half else 1 - core)
        store[place] = (v * scale * gain[place]).astype(jnp.bfloat16)
    return values[0]


def blocks_dot(normed, weight, order):
    part = normed.shape[2]
    total = None
    for b, place in enumerate(order):
        rows = weight[b * part : (b + 1) * part, :]
        piece = jnp.dot(normed[place], rows, preferred_element_type=jnp.float32)
        total = piece if total is None else total + piece
    return total


def ffn_kernel(half, ids, *refs):
    parts = refs[6 : 6 + 2 * half]
    keep, send, gains, ups, downs, normed, terms, sems = refs[6 + 2 * half :]
    copies = fetch(
        refs[:6], [store.at[m] for store in (gains, ups, downs) for m in range(2)], sems
    )
    chip, core = ids[1], ids[2]
    part = parts[0].shape[2]
    bases = [
        normalise([part[m] for part in parts], gains.at[m], chip, core, normed.at[m], copies[m])
        for m in range(2)
    ]
    for m in range(2):
        copies[2 + m].wait()
        pre = blocks_dot(normed.at[m], ups.at[m], range(2 * half))
        units = jax.nn.gelu(pre).astype(jnp.bfloat16)
        copies[4 + m].wait()
        full = jnp.dot(units, downs[m], preferred_element_type=jnp.float32)
        for b in range(2 * half):
            terms[m, b] = full[:, b * part : (b + 1) * part]
        for k in range(half):
            place = 2 * (chip ^ k)
            kept = terms[m, place + core]
            keep[k, m] = kept + bases[m] if k == 0 else kept
            send[k, m] = terms[m, place + 1 - core].astype(jnp.bfloat16)


def pair_kernel(ids, keep, came, own, *outs):
    own[...] = keep[0] + came[0].astype(jnp.float32)
    for k, out in enumerate(outs):
        out[...] = (keep[k + 1] + came[k + 1].astype(jnp.float32)).astype(jnp.bfloat16)


def score_kernel(half, dp, ids, *refs):
    parts = refs[2 : 2 + 2 * half]
    *outs, partial, tail, gains, normed, out_store, sems = refs[2 + 2 * half :]
    here = dp - 1
    copies = fetch(
        [refs[0], refs[1], outs[0], outs[here]],
        [store.at[m] for store in (gains, out_store) for m in range(2)],
        sems,
    )
    me, chip, core = ids[0], ids[1], ids[2]
    ratio = 2 * half // dp
    part = parts[0].shape[2]
    for m in range(2):
        values = [part[m] for part in parts]
        normalise(values, gains.at[m], chip, core, normed.at[m], copies[m])
        for b in range(ratio):
            tail[m, :, b * part : (b + 1) * part] = normed[m, (me ^ here) * ratio + b]
    for m in range(2):
        logits = None
        for k in [*range(1, here), 0]:
            if k == 0:
                copies[2 + m].wait()
                outs[m * here] = out_store.at[m]
            order = [(me ^ k) * ratio + b for b in range(ratio)]
            piece = blocks_dot(normed.at[m], outs[m * here + k], order)
            logits = piece if logits is None else logits + piece
        partial[m] = logits


def finish_kernel(ids, wanted, partial, tail, last_policy, last_reference, stats):
    lane = lax.broadcasted_iota(jnp.int32, (tail.shape[1], 128), 1)
    table = jnp.zeros(lane.shape, jnp.float32)
    for m, last in enumerate((last_policy, last_reference)):
        logits = partial[m] + jnp.dot(tail[m], last[...], preferred_element_type=jnp.float32)
        entries = lax.broadcasted_iota(jnp.int32, logits.shape, 1) + ids[3] * logits.shape[1]
        picked = jnp.sum(jnp.where(entries == wanted[...], logits, 0.0), axis=1, keepdims=True)
        top = jnp.max(logits, axis=1, keepdims=True)
        total = jnp.sum(jnp.exp(logits - top), axis=1, keepdims=True)
        table = jnp.where(lane == m, top, table)
        table = jnp.where(lane == 2 + m, total, table)
        table = jnp.where(lane == 4 + m, picked, table)
    stats[...] = jnp.transpose(table)[:8]


def merge(tables):
    top = functools.reduce(jnp.maximum, [t[0:2] for t in tables])
    total = sum(t[2:4] * jnp.exp(t[0:2] - top) for t in tables)
    return top, total, sum(t[4:6] for t in tables)


def merge_kernel(ids, *refs):
    out = refs[-1]
    out[0:2], out[2:4], out[4:6] = merge(refs[:-1])
    out[6:8] = jnp.zeros((2, out.shape[1]), jnp.float32)


def last_kernel(ids, *refs):
    out = refs[-1]
    top, total, picked = merge(refs[:-1])
    logprob = picked - (top + jnp.log(total))
    out[...] = logprob[0:1] - logprob[1:2]


def local(
    hidden_policy,
    hidden_reference,
    ffn_gain_policy,
    ffn_gain_reference,
    up_policy,
    up_reference,
    down_policy,
    down_reference,
    final_gain_policy,
    final_gain_reference,
    out_policy,
    out_reference,
    move_plan,
    lengths,
    targets,
):
    dp = lax.axis_size("dp")
    mp = lax.axis_size("mp")
    half = mp // 2
    dp_index = lax.axis_index("dp")
    mp_index = lax.axis_index("mp")
    ids = jnp.stack([dp_index, mp_index // 2, mp_index % 2, mp_index]).astype(jnp.int32)
    reqs, slots, part = hidden_policy.shape
    here = reqs * slots
    rows = here // 2
    ffn_gains = (ffn_gain_policy, ffn_gain_reference)
    final_gains = (final_gain_policy, final_gain_reference)
    gains = [gain.reshape(mp, 1, part) for gain in (*ffn_gains, *final_gains)]
    bits = [1 << b for b in range(dp.bit_length() - 1)]

    bit_orders = []
    for m in range(2):
        bit_orders.append([bits[(b ^ m) if (b ^ m) < len(bits) else b] for b in range(len(bits))])

    def spread_step(blocks, step, places):
        for m in range(2):
            bit = bit_orders[m][step]
            for k in [k for k in blocks[m] if places(m, k)]:
                blocks[m][k ^ bit] = exchange(blocks[m][k], "dp", bit)

    packed = call(
        pack_kernel,
        jax.ShapeDtypeStruct((reqs + 1, slots, part), jnp.bfloat16),
        (lengths, targets, hidden_reference),
        [
            pltpu.SMEM(lengths.shape, jnp.int32),
            pltpu.VMEM(targets.shape, jnp.int32),
            pltpu.SemaphoreType.DMA((3,)),
        ],
        far=(0, 1, 2),
    )
    hiddens = [{0: hidden_policy}, {0: packed}]
    outs = [{0: out_policy}, {0: out_reference}]

    def wait_for(first, places):
        flat = [(m, k) for m in range(2) for k in outs[m] if places(m, k)]
        first, values = lax.optimization_barrier((first, [outs[m][k] for m, k in flat]))
        for (m, k), value in zip(flat, values):
            outs[m][k] = value
        return first

    for step in range(len(bits)):
        spread_step(hiddens, step, lambda m, k: k == 0)
        if step:
            blocks, place = hiddens[0], bit_orders[0][step]
            passed = [k for k in blocks if 0 < k and not k & place]
            values = [blocks[k] for k in passed]
            blocks[place], values = lax.optimization_barrier((blocks[place], values))
            blocks.update(zip(passed, values))
        spread_step(hiddens, step, lambda m, k: 0 < k and not k & bit_orders[m][step])
    early = [(m, b) for m in range(2) for b in bits]
    values = wait_for([hiddens[m][b] for m, b in early], lambda m, k: True)
    for (m, b), value in zip(early, values):
        hiddens[m][b] = value
    spread_step(outs, 0, lambda m, k: True)
    hidden_parts = [hiddens[m][k] for m in range(2) for k in range(dp)]

    order = jnp.arange(dp, dtype=jnp.int32)
    moved, facts = call(
        functools.partial(select_kernel, dp),
        (
            jax.ShapeDtypeStruct((2, rows, part), jnp.bfloat16),
            jax.ShapeDtypeStruct((dp, reqs, part), jnp.float32),
        ),
        (ids, move_plan, *hidden_parts),
        [
            pltpu.VMEM(hidden_policy.shape, jnp.bfloat16),
            pltpu.SMEM(move_plan.shape, jnp.int32),
            pltpu.SemaphoreType.DMA((2,)),
        ],
        far=(1, 2),
        cost=10000000000,
    )

    facts = facts[:, :, : 2 * slots + 1].astype(jnp.int32)
    all_lengths = facts[:, :, 0].reshape(-1)
    all_targets = (facts[:, :, 1 : slots + 1] * 128 + facts[:, :, slots + 1 :]).reshape(-1)
    slot_ids = ((order ^ dp_index)[:, None] * reqs + jnp.arange(reqs, dtype=jnp.int32)).reshape(-1)
    positions = jnp.arange(slots, dtype=jnp.int32)

    def codes(slot):
        start = jnp.sum(jnp.where(slot_ids[None] < slot[:, None], all_lengths[None], 0), axis=1)
        live = jnp.sum(jnp.where(slot_ids[None] == slot[:, None], all_lengths[None], 0), axis=1)
        return jnp.where(
            positions[None] < live[:, None], start[:, None] + positions[None], jnp.int32(-1)
        )

    far = sorted(range(1, half), key=lambda k: (k.bit_length() <= 1, k))

    def gather_pair(own):
        same = {0: own}
        for k in far:
            same[k] = exchange(own, "mp", 2 * k)
        passed = lax.optimization_barrier([same[k] for k in far])
        same.update(zip(far, passed))
        same = [same[k] for k in range(half)]
        return same + [exchange(v, "mp", 1) for v in same]

    parts = gather_pair(moved)
    if len(bits) > 1:
        parts[-1] = wait_for(parts[-1], lambda m, k: k == 0)
        later = [{0: outs[m][0]} for m in range(2)]
        spread_step(later, 1, lambda m, k: True)
    gain_scratch = pltpu.VMEM((2, mp, 1, part), jnp.float32)
    block = jax.ShapeDtypeStruct((2, rows, part), jnp.bfloat16)
    keep, send = call(
        functools.partial(ffn_kernel, half),
        (
            jax.ShapeDtypeStruct((half, 2, rows, part), jnp.float32),
            jax.ShapeDtypeStruct((half, 2, rows, part), jnp.bfloat16),
        ),
        (ids, *gains[:2], up_policy, up_reference, down_policy, down_reference, *parts),
        [
            gain_scratch,
            pltpu.VMEM((2,) + up_policy.shape, jnp.bfloat16),
            pltpu.VMEM((2,) + down_policy.shape, jnp.bfloat16),
            pltpu.VMEM((2, mp, rows, part), jnp.bfloat16),
            pltpu.VMEM((2, mp, rows, part), jnp.float32),
            pltpu.SemaphoreType.DMA((6,)),
        ],
        far=range(1, 7),
        mib=22,
    )
    send = wait_for(send, lambda m, k: k > 0)
    came = exchange(send, "mp", 1)
    own, *pieces = call(
        pair_kernel,
        (jax.ShapeDtypeStruct((2, rows, part), jnp.float32),) + (block,) * (half - 1),
        (ids, keep, came),
    )
    arrived = {k: exchange(pieces[k - 1], "mp", 2 * k) for k in far}
    if len(bits) > 1:
        for m in range(2):
            outs[m].update(later[m])
        arrived[far[0]] = wait_for(arrived[far[0]], lambda m, k: True)
        spread_step(outs, 1, lambda m, k: k == bit_orders[m][0])
    for k in range(1, half):
        own = own + arrived[k].astype(jnp.float32)
    stream = own.astype(jnp.bfloat16)
    for step in range(2, len(bits)):
        stream = wait_for(stream, lambda m, k: True)
        spread_step(outs, step, lambda m, k: True)

    owner_code = codes(slot_ids).reshape(-1)
    my_ranks = dp_index * rows + jnp.arange(rows, dtype=jnp.int32)
    wanted = jnp.sum(
        jnp.where(owner_code[None] == my_ranks[:, None], all_targets[None], 0),
        axis=1,
        keepdims=True,
    )
    partial, tail = call(
        functools.partial(score_kernel, half, dp),
        (
            jax.ShapeDtypeStruct((2, rows, out_policy.shape[1]), jnp.float32),
            jax.ShapeDtypeStruct((2, rows, out_policy.shape[0]), jnp.bfloat16),
        ),
        (
            ids,
            *gains[2:],
            *gather_pair(stream),
            *[outs[m][k] for m in range(2) for k in range(dp - 1)],
        ),
        [
            gain_scratch,
            pltpu.VMEM((2, mp, rows, part), jnp.bfloat16),
            pltpu.VMEM((2,) + out_policy.shape, jnp.bfloat16),
            pltpu.SemaphoreType.DMA((4,)),
        ],
        far=(1, 2, 3 + mp, 2 + mp + dp),
        mib=14,
    )
    stats = call(
        finish_kernel,
        jax.ShapeDtypeStruct((8, rows), jnp.float32),
        (ids, wanted, partial, tail, outs[0][dp - 1], outs[1][dp - 1]),
        mib=8,
    )
    stats = call(
        merge_kernel,
        jax.ShapeDtypeStruct((8, rows), jnp.float32),
        (ids, stats, exchange(stats, "mp", 1)),
    )
    diff = call(
        last_kernel,
        jax.ShapeDtypeStruct((1, rows), jnp.float32),
        (ids, stats, *[exchange(stats, "mp", 2 * k) for k in range(half - 1, 0, -1)]),
    )
    diff = jnp.concatenate([diff] + [exchange(diff, "dp", k) for k in range(1, dp)])
    ranks = ((order ^ dp_index)[:, None] * rows + jnp.arange(rows, dtype=jnp.int32)).reshape(-1)
    my_code = codes(dp_index * reqs + jnp.arange(reqs, dtype=jnp.int32))
    hit = my_code[:, :, None] == ranks[None, None]
    token_diff = jnp.sum(jnp.where(hit, diff.reshape(1, 1, -1), 0.0), axis=2)
    return (token_diff, jnp.sum(token_diff, axis=1))


def solution(mesh):
    return jax.shard_map(
        local,
        mesh=mesh,
        in_specs=(
            P("dp", None, "mp"),
            P("dp", None, "mp"),
            P(),
            P(),
            P(None, "mp"),
            P(None, "mp"),
            P("mp", None),
            P("mp", None),
            P(),
            P(),
            P("dp", "mp"),
            P("dp", "mp"),
            P(),
            P("dp"),
            P("dp", None),
        ),
        out_specs=(P("dp", None), P("dp")),
        check_vma=False,
    )
```

```python
import functools

import jax
import jax.numpy as jnp
from jax import lax
from jax.experimental import pallas as pl
from jax.experimental.pallas import tpu as pltpu
from jax.sharding import PartitionSpec as P

epsilon = 1e-05
vmem = pl.BlockSpec(memory_space=pltpu.VMEM)
smem = pl.BlockSpec(memory_space=pltpu.SMEM)
anywhere = pl.BlockSpec(memory_space=pltpu.HBM)


def call(kernel, out_shape, ops, scratch=(), far=(), mib=4, cost=None):
    specs = [anywhere if i in far else vmem if i else smem for i in range(len(ops))]
    ops = [
        pltpu.with_memory_space_constraint(op, pltpu.HBM) if i in far else op
        for i, op in enumerate(ops)
    ]
    return pl.pallas_call(
        kernel,
        out_shape=out_shape,
        in_specs=specs,
        out_specs=jax.tree.map(lambda _: vmem, out_shape),
        scratch_shapes=list(scratch),
        cost_estimate=cost and pl.CostEstimate(flops=cost, bytes_accessed=0, transcendentals=0),
        compiler_params=pltpu.CompilerParams(vmem_limit_bytes=mib * 1024 * 1024),
    )(*ops)


def exchange(values, axis, flip):
    count = lax.axis_size(axis)
    return lax.ppermute(values, axis, [(i, i ^ flip) for i in range(count)])


def fetch(sources, targets, sems):
    copies = [
        pltpu.make_async_copy(source, target, sems.at[i])
        for i, (source, target) in enumerate(zip(sources, targets))
    ]
    for copy in copies:
        copy.start()
    return copies


def pack_kernel(lengths_far, targets_far, hidden, out, lengths, targets, sems):
    reqs = hidden.shape[0]
    copies = fetch(
        [lengths_far, targets_far, hidden], [lengths, targets, out.at[pl.ds(0, reqs)]], sems
    )
    copies[1].wait()
    slots, part = targets.shape[1], hidden.shape[2]
    row = lax.broadcasted_iota(jnp.int32, (slots, part), 0)
    lane = lax.broadcasted_iota(jnp.int32, (slots, part), 1)
    high = lax.shift_right_logical(targets[...], 7)
    low = targets[...] - high * 128
    block = jnp.zeros((reqs, part), jnp.float32)
    for first, values in ((1, high), (1 + slots, low)):
        spot = (lane == row + first).astype(jnp.float32).astype(jnp.bfloat16)
        values = values.astype(jnp.float32).astype(jnp.bfloat16)
        block = block + jnp.dot(values, spot, preferred_element_type=jnp.float32)
    row = lax.broadcasted_iota(jnp.int32, (reqs, part), 0)
    lane = lax.broadcasted_iota(jnp.int32, (reqs, part), 1)
    copies[0].wait()
    for r in range(reqs):
        here = jnp.logical_and(row == r, lane == 0)
        block = jnp.where(here, lengths[r].astype(jnp.float32), block)
    out[reqs] = block.astype(jnp.bfloat16)
    copies[2].wait()


def select_kernel(dp, ids, plan_far, *refs):
    parts, (out, picks, marks, own, plan, sems) = list(refs[: 2 * dp]), refs[2 * dp :]
    plan_copy, copy = fetch([plan_far, parts[0]], [plan, own], sems)
    parts[0] = own
    rows = out.shape[1]
    reqs, slots, _ = own.shape
    here = reqs * slots
    me = ids[0]
    facts = jnp.concatenate([parts[dp + k][reqs].astype(jnp.float32) for k in range(dp)], axis=0)
    lengths = facts[:, 0:1].astype(jnp.int32)
    row = lax.broadcasted_iota(jnp.int32, (reqs, here), 0)
    slot = jnp.concatenate([row + (me ^ k) * reqs for k in range(dp)], axis=0)
    position = lax.rem(lax.broadcasted_iota(jnp.int32, (1, here), 1), slots)
    wanted = me * rows + lax.broadcasted_iota(jnp.int32, (rows, here), 0)
    request = lax.div(lax.broadcasted_iota(jnp.int32, (1, here), 1), slots)
    hots = []
    plan_copy.wait()
    for k in range(dp):
        owner = jnp.zeros((1, here), jnp.int32)
        for r in range(reqs):
            owner = jnp.where(request == r, plan[(me ^ k) * reqs + r], owner)
        start = jnp.sum(jnp.where(slot < owner, lengths, 0), axis=0, keepdims=True)
        live = jnp.sum(jnp.where(slot == owner, lengths, 0), axis=0, keepdims=True)
        code = jnp.where(position < live, start + position, -1)
        hots.append((code == wanted).astype(jnp.float32).astype(jnp.bfloat16))
    copy.wait()
    for m in range(2):
        total = None
        for k in range(dp):
            values = parts[m * dp + k][0:reqs]
            values = values.reshape(-1, values.shape[-1])
            found = jnp.dot(hots[k], values, preferred_element_type=jnp.float32)
            total = found if total is None else total + found
        out[m] = total.astype(out.dtype)

    count = dp * reqs
    down = lax.broadcasted_iota(jnp.int32, (reqs, count), 0)
    along = lax.broadcasted_iota(jnp.int32, (1, count), 1)
    here_slot = lax.rem(along, reqs)
    for k in range(dp):
        here_slot = jnp.where(lax.div(along, reqs) == k, here_slot + (me ^ k) * reqs, here_slot)
    slot = jnp.concatenate([down + (me ^ k) * reqs for k in range(dp)], axis=0)
    start = jnp.sum(jnp.where(slot < here_slot, lengths, 0), axis=0, keepdims=True)
    live = jnp.sum(jnp.where(slot == here_slot, lengths, 0), axis=0, keepdims=True)

    rank = me * rows + lax.broadcasted_iota(jnp.int32, (rows, count), 0)
    held = jnp.logical_and(rank >= start, rank < start + live)
    first = jnp.sum(jnp.where(held, start, 0), axis=1, keepdims=True)
    spot = rank[:, 0:1] - first
    held = held.astype(jnp.float32).astype(jnp.bfloat16)
    rows_of = jnp.dot(held, facts.astype(jnp.bfloat16), preferred_element_type=jnp.float32)
    lane = lax.broadcasted_iota(jnp.int32, rows_of.shape, 1)
    high = jnp.sum(jnp.where(lane == spot + 1, rows_of, 0.0), axis=1, keepdims=True)
    low = jnp.sum(jnp.where(lane == spot + 1 + slots, rows_of, 0.0), axis=1, keepdims=True)
    picks[...] = (high * 128.0 + low).astype(jnp.int32)

    mine = me * reqs + down
    begin = jnp.sum(jnp.where(here_slot < mine, live, 0), axis=1, keepdims=True)
    length = jnp.sum(jnp.where(here_slot == mine, live, 0), axis=1, keepdims=True)
    position = lax.broadcasted_iota(jnp.int32, (reqs, slots), 1)
    marks[...] = jnp.where(position < length, begin + position, -1)


def normalise(values, gain, chip, core, store, copy):
    half = len(values) // 2
    part = values[0].shape[1]
    width = part * len(values)
    values = [v.astype(jnp.float32) for v in values]
    center = sum(jnp.sum(v, axis=1, keepdims=True) for v in values) / width
    values = [v - center for v in values]
    spread = sum(jnp.sum(v * v, axis=1, keepdims=True) for v in values) / width
    scale = lax.rsqrt(spread + epsilon)
    copy.wait()
    for k, v in enumerate(values):
        place = 2 * (chip ^ (k % half)) + (core if k < half else 1 - core)
        store[place] = (v * scale * gain[place]).astype(jnp.bfloat16)
    return values[0]


def blocks_dot(normed, weight, order):
    part = normed.shape[2]
    total = None
    for b, place in enumerate(order):
        rows = weight[b * part : (b + 1) * part, :]
        piece = jnp.dot(normed[place], rows, preferred_element_type=jnp.float32)
        total = piece if total is None else total + piece
    return total


def ffn_kernel(half, ids, *refs):
    parts = refs[6 : 6 + 2 * half]
    keep, send, gains, ups, downs, normed, terms, sems = refs[6 + 2 * half :]
    copies = fetch(
        refs[:6], [store.at[m] for store in (gains, ups, downs) for m in range(2)], sems
    )
    chip, core = ids[1], ids[2]
    part = parts[0].shape[2]
    bases = [
        normalise([part[m] for part in parts], gains.at[m], chip, core, normed.at[m], copies[m])
        for m in range(2)
    ]
    for m in range(2):
        copies[2 + m].wait()
        pre = blocks_dot(normed.at[m], ups.at[m], range(2 * half))
        units = jax.nn.gelu(pre).astype(jnp.bfloat16)
        copies[4 + m].wait()
        full = jnp.dot(units, downs[m], preferred_element_type=jnp.float32)
        for b in range(2 * half):
            terms[m, b] = full[:, b * part : (b + 1) * part]
        for k in range(half):
            place = 2 * (chip ^ k)
            kept = terms[m, place + core]
            keep[k, m] = kept + bases[m] if k == 0 else kept
            send[k, m] = terms[m, place + 1 - core].astype(jnp.bfloat16)


def pair_kernel(ids, keep, came, own, *outs):
    own[...] = keep[0] + came[0].astype(jnp.float32)
    for k, out in enumerate(outs):
        out[...] = (keep[k + 1] + came[k + 1].astype(jnp.float32)).astype(jnp.bfloat16)


def score_kernel(half, dp, ids, *refs):
    parts = refs[2 : 2 + 2 * half]
    *outs, partial, tail, gains, normed, out_store, sems = refs[2 + 2 * half :]
    here = dp - 1
    copies = fetch(
        [refs[0], refs[1], outs[0], outs[here]],
        [store.at[m] for store in (gains, out_store) for m in range(2)],
        sems,
    )
    me, chip, core = ids[0], ids[1], ids[2]
    ratio = 2 * half // dp
    part = parts[0].shape[2]
    for m in range(2):
        values = [part[m] for part in parts]
        normalise(values, gains.at[m], chip, core, normed.at[m], copies[m])
        for b in range(ratio):
            tail[m, :, b * part : (b + 1) * part] = normed[m, (me ^ here) * ratio + b]
    for m in range(2):
        logits = None
        for k in [*range(1, here), 0]:
            if k == 0:
                copies[2 + m].wait()
                outs[m * here] = out_store.at[m]
            order = [(me ^ k) * ratio + b for b in range(ratio)]
            piece = blocks_dot(normed.at[m], outs[m * here + k], order)
            logits = piece if logits is None else logits + piece
        partial[m] = logits


def finish_kernel(ids, wanted, partial, tail, last_policy, last_reference, stats):
    lane = lax.broadcasted_iota(jnp.int32, (tail.shape[1], 128), 1)
    table = jnp.zeros(lane.shape, jnp.float32)
    for m, last in enumerate((last_policy, last_reference)):
        logits = partial[m] + jnp.dot(tail[m], last[...], preferred_element_type=jnp.float32)
        entries = lax.broadcasted_iota(jnp.int32, logits.shape, 1) + ids[3] * logits.shape[1]
        picked = jnp.sum(jnp.where(entries == wanted[...], logits, 0.0), axis=1, keepdims=True)
        top = jnp.max(logits, axis=1, keepdims=True)
        total = jnp.sum(jnp.exp(logits - top), axis=1, keepdims=True)
        table = jnp.where(lane == m, top, table)
        table = jnp.where(lane == 2 + m, total, table)
        table = jnp.where(lane == 4 + m, picked, table)
    stats[...] = jnp.transpose(table)[:8]


def merge(tables):
    top = functools.reduce(jnp.maximum, [t[0:2] for t in tables])
    total = sum(t[2:4] * jnp.exp(t[0:2] - top) for t in tables)
    return top, total, sum(t[4:6] for t in tables)


def merge_kernel(ids, *refs):
    out = refs[-1]
    out[0:2], out[2:4], out[4:6] = merge(refs[:-1])
    out[6:8] = jnp.zeros((2, out.shape[1]), jnp.float32)


def last_kernel(ids, *refs):
    out = refs[-1]
    top, total, picked = merge(refs[:-1])
    logprob = picked - (top + jnp.log(total))
    out[...] = logprob[0:1] - logprob[1:2]


def local(
    hidden_policy,
    hidden_reference,
    ffn_gain_policy,
    ffn_gain_reference,
    up_policy,
    up_reference,
    down_policy,
    down_reference,
    final_gain_policy,
    final_gain_reference,
    out_policy,
    out_reference,
    move_plan,
    lengths,
    targets,
):
    dp = lax.axis_size("dp")
    mp = lax.axis_size("mp")
    half = mp // 2
    dp_index = lax.axis_index("dp")
    mp_index = lax.axis_index("mp")
    ids = jnp.stack([dp_index, mp_index // 2, mp_index % 2, mp_index]).astype(jnp.int32)
    reqs, slots, part = hidden_policy.shape
    here = reqs * slots
    rows = here // 2
    ffn_gains = (ffn_gain_policy, ffn_gain_reference)
    final_gains = (final_gain_policy, final_gain_reference)
    gains = [gain.reshape(mp, 1, part) for gain in (*ffn_gains, *final_gains)]
    bits = [1 << b for b in range(dp.bit_length() - 1)]

    bit_orders = []
    for m in range(2):
        bit_orders.append([bits[(b ^ m) if (b ^ m) < len(bits) else b] for b in range(len(bits))])

    def spread_step(blocks, step, places):
        for m in range(2):
            bit = bit_orders[m][step]
            for k in [k for k in blocks[m] if places(m, k)]:
                blocks[m][k ^ bit] = exchange(blocks[m][k], "dp", bit)

    packed = call(
        pack_kernel,
        jax.ShapeDtypeStruct((reqs + 1, slots, part), jnp.bfloat16),
        (lengths, targets, hidden_reference),
        [
            pltpu.SMEM(lengths.shape, jnp.int32),
            pltpu.VMEM(targets.shape, jnp.int32),
            pltpu.SemaphoreType.DMA((3,)),
        ],
        far=(0, 1, 2),
    )
    hiddens = [{0: hidden_policy}, {0: packed}]
    outs = [{0: out_policy}, {0: out_reference}]

    def wait_for(first, places):
        flat = [(m, k) for m in range(2) for k in outs[m] if places(m, k)]
        first, values = lax.optimization_barrier((first, [outs[m][k] for m, k in flat]))
        for (m, k), value in zip(flat, values):
            outs[m][k] = value
        return first

    for step in range(len(bits)):
        spread_step(hiddens, step, lambda m, k: k == 0)
        if step:
            blocks, place = hiddens[0], bit_orders[0][step]
            passed = [k for k in blocks if 0 < k and not k & place]
            values = [blocks[k] for k in passed]
            blocks[place], values = lax.optimization_barrier((blocks[place], values))
            blocks.update(zip(passed, values))
        spread_step(hiddens, step, lambda m, k: 0 < k and not k & bit_orders[m][step])
    early = [(m, b) for m in range(2) for b in bits]
    values = wait_for([hiddens[m][b] for m, b in early], lambda m, k: True)
    for (m, b), value in zip(early, values):
        hiddens[m][b] = value
    spread_step(outs, 0, lambda m, k: True)
    hidden_parts = [hiddens[m][k] for m in range(2) for k in range(dp)]

    moved, wanted, marks = call(
        functools.partial(select_kernel, dp),
        (
            jax.ShapeDtypeStruct((2, rows, part), jnp.bfloat16),
            jax.ShapeDtypeStruct((rows, 1), jnp.int32),
            jax.ShapeDtypeStruct((reqs, slots), jnp.int32),
        ),
        (ids, move_plan, *hidden_parts),
        [
            pltpu.VMEM(hidden_policy.shape, jnp.bfloat16),
            pltpu.SMEM(move_plan.shape, jnp.int32),
            pltpu.SemaphoreType.DMA((2,)),
        ],
        far=(1, 2),
        cost=10000000000,
    )

    far = sorted(range(1, half), key=lambda k: (k.bit_length() <= 1, k))

    def gather_pair(own):
        same = {0: own}
        for k in far:
            same[k] = exchange(own, "mp", 2 * k)
        *passed, beside = lax.optimization_barrier(
            [same[k] for k in far] + [exchange(own, "mp", 1)]
        )
        same.update(zip(far, passed))
        same = [same[k] for k in range(half)]
        return same + [beside] + [exchange(v, "mp", 1) for v in same[1:]]

    parts = gather_pair(moved)
    if len(bits) > 1:
        parts[-1] = wait_for(parts[-1], lambda m, k: k == 0)
        later = [{0: outs[m][0]} for m in range(2)]
        spread_step(later, 1, lambda m, k: True)
    gain_scratch = pltpu.VMEM((2, mp, 1, part), jnp.float32)
    block = jax.ShapeDtypeStruct((2, rows, part), jnp.bfloat16)
    keep, send = call(
        functools.partial(ffn_kernel, half),
        (
            jax.ShapeDtypeStruct((half, 2, rows, part), jnp.float32),
            jax.ShapeDtypeStruct((half, 2, rows, part), jnp.bfloat16),
        ),
        (ids, *gains[:2], up_policy, up_reference, down_policy, down_reference, *parts),
        [
            gain_scratch,
            pltpu.VMEM((2,) + up_policy.shape, jnp.bfloat16),
            pltpu.VMEM((2,) + down_policy.shape, jnp.bfloat16),
            pltpu.VMEM((2, mp, rows, part), jnp.bfloat16),
            pltpu.VMEM((2, mp, rows, part), jnp.float32),
            pltpu.SemaphoreType.DMA((6,)),
        ],
        far=range(1, 7),
        mib=22,
    )
    send = wait_for(send, lambda m, k: k > 0)
    came = exchange(send, "mp", 1)
    own, *pieces = call(
        pair_kernel,
        (jax.ShapeDtypeStruct((2, rows, part), jnp.float32),) + (block,) * (half - 1),
        (ids, keep, came),
    )
    arrived = {k: exchange(pieces[k - 1], "mp", 2 * k) for k in far}
    if len(bits) > 1:
        for m in range(2):
            outs[m].update(later[m])
        arrived = wait_for(arrived, lambda m, k: True)
        spread_step(outs, 1, lambda m, k: k == bit_orders[m][0])
    for k in range(1, half):
        own = own + arrived[k].astype(jnp.float32)
    stream = own.astype(jnp.bfloat16)
    for step in range(2, len(bits)):
        stream = wait_for(stream, lambda m, k: True)
        spread_step(outs, step, lambda m, k: True)

    partial, tail = call(
        functools.partial(score_kernel, half, dp),
        (
            jax.ShapeDtypeStruct((2, rows, out_policy.shape[1]), jnp.float32),
            jax.ShapeDtypeStruct((2, rows, out_policy.shape[0]), jnp.bfloat16),
        ),
        (
            ids,
            *gains[2:],
            *gather_pair(stream),
            *[outs[m][k] for m in range(2) for k in range(dp - 1)],
        ),
        [
            gain_scratch,
            pltpu.VMEM((2, mp, rows, part), jnp.bfloat16),
            pltpu.VMEM((2,) + out_policy.shape, jnp.bfloat16),
            pltpu.SemaphoreType.DMA((4,)),
        ],
        far=(1, 2, 3 + mp, 2 + mp + dp),
        mib=14,
    )
    stats = call(
        finish_kernel,
        jax.ShapeDtypeStruct((8, rows), jnp.float32),
        (ids, wanted, partial, tail, outs[0][dp - 1], outs[1][dp - 1]),
        mib=8,
    )
    stats = call(
        merge_kernel,
        jax.ShapeDtypeStruct((8, rows), jnp.float32),
        (ids, stats, exchange(stats, "mp", 1)),
    )
    diff = call(
        last_kernel,
        jax.ShapeDtypeStruct((1, rows), jnp.float32),
        (ids, stats, *[exchange(stats, "mp", 2 * k) for k in range(half - 1, 0, -1)]),
    )
    came = [exchange(diff, "dp", k) for k in range(dp - 1, 0, -1)]
    places = jnp.arange(dp, dtype=jnp.int32)[::-1] ^ dp_index
    ranks = places[:, None] * rows + jnp.arange(rows, dtype=jnp.int32)
    values = jnp.concatenate(came + [diff])
    hit = marks[:, :, None, None] == ranks
    token_diff = jnp.sum(jnp.where(hit, values, 0.0), axis=(2, 3))
    return (token_diff, jnp.sum(token_diff, axis=1))


def solution(mesh):
    return jax.shard_map(
        local,
        mesh=mesh,
        in_specs=(
            P("dp", None, "mp"),
            P("dp", None, "mp"),
            P(),
            P(),
            P(None, "mp"),
            P(None, "mp"),
            P("mp", None),
            P("mp", None),
            P(),
            P(),
            P("dp", "mp"),
            P("dp", "mp"),
            P(),
            P("dp"),
            P("dp", None),
        ),
        out_specs=(P("dp", None), P("dp")),
        check_vma=False,
    )
```

```python
import functools

import jax
import jax.numpy as jnp
from jax import lax
from jax.experimental import pallas as pl
from jax.experimental.pallas import tpu as pltpu
from jax.sharding import PartitionSpec as P

epsilon = 1e-05
vmem = pl.BlockSpec(memory_space=pltpu.VMEM)
smem = pl.BlockSpec(memory_space=pltpu.SMEM)
anywhere = pl.BlockSpec(memory_space=pltpu.HBM)


def call(kernel, out_shape, ops, scratch=(), far=(), mib=4, cost=None):
    specs = [anywhere if i in far else vmem if i else smem for i in range(len(ops))]
    ops = [
        pltpu.with_memory_space_constraint(op, pltpu.HBM) if i in far else op
        for i, op in enumerate(ops)
    ]
    return pl.pallas_call(
        kernel,
        out_shape=out_shape,
        in_specs=specs,
        out_specs=jax.tree.map(lambda _: vmem, out_shape),
        scratch_shapes=list(scratch),
        cost_estimate=cost and pl.CostEstimate(flops=cost, bytes_accessed=0, transcendentals=0),
        compiler_params=pltpu.CompilerParams(vmem_limit_bytes=mib * 1024 * 1024),
    )(*ops)


def exchange(values, axis, flip):
    count = lax.axis_size(axis)
    return lax.ppermute(values, axis, [(i, i ^ flip) for i in range(count)])


def fetch(sources, targets, sems):
    copies = [
        pltpu.make_async_copy(source, target, sems.at[i])
        for i, (source, target) in enumerate(zip(sources, targets))
    ]
    for copy in copies:
        copy.start()
    return copies


def pack_kernel(lengths_far, targets_far, hidden, out, lengths, targets, sems):
    reqs = hidden.shape[0]
    copies = fetch(
        [lengths_far, targets_far, hidden], [lengths, targets, out.at[pl.ds(0, reqs)]], sems
    )
    copies[1].wait()
    slots, part = targets.shape[1], hidden.shape[2]
    row = lax.broadcasted_iota(jnp.int32, (slots, part), 0)
    lane = lax.broadcasted_iota(jnp.int32, (slots, part), 1)
    high = lax.shift_right_logical(targets[...], 7)
    low = targets[...] - high * 128
    block = jnp.zeros((reqs, part), jnp.float32)
    for first, values in ((1, high), (1 + slots, low)):
        spot = (lane == row + first).astype(jnp.float32).astype(jnp.bfloat16)
        values = values.astype(jnp.float32).astype(jnp.bfloat16)
        block = block + jnp.dot(values, spot, preferred_element_type=jnp.float32)
    row = lax.broadcasted_iota(jnp.int32, (reqs, part), 0)
    lane = lax.broadcasted_iota(jnp.int32, (reqs, part), 1)
    copies[0].wait()
    for r in range(reqs):
        here = jnp.logical_and(row == r, lane == 0)
        block = jnp.where(here, lengths[r].astype(jnp.float32), block)
    out[reqs] = block.astype(jnp.bfloat16)
    copies[2].wait()


def select_kernel(dp, ids, plan_far, *refs):
    parts, (out, picks, marks, own, plan, sems) = list(refs[: 2 * dp]), refs[2 * dp :]
    plan_copy, copy = fetch([plan_far, parts[0]], [plan, own], sems)
    parts[0] = own
    rows = out.shape[1]
    reqs, slots, _ = own.shape
    here = reqs * slots
    me = ids[0]
    facts = jnp.concatenate([parts[dp + k][reqs].astype(jnp.float32) for k in range(dp)], axis=0)
    lengths = facts[:, 0:1].astype(jnp.int32)
    row = lax.broadcasted_iota(jnp.int32, (reqs, here), 0)
    slot = jnp.concatenate([row + (me ^ k) * reqs for k in range(dp)], axis=0)
    position = lax.rem(lax.broadcasted_iota(jnp.int32, (1, here), 1), slots)
    wanted = me * rows + lax.broadcasted_iota(jnp.int32, (rows, here), 0)
    request = lax.div(lax.broadcasted_iota(jnp.int32, (1, here), 1), slots)
    hots = []
    plan_copy.wait()
    for k in range(dp):
        owner = jnp.zeros((1, here), jnp.int32)
        for r in range(reqs):
            owner = jnp.where(request == r, plan[(me ^ k) * reqs + r], owner)
        start = jnp.sum(jnp.where(slot < owner, lengths, 0), axis=0, keepdims=True)
        live = jnp.sum(jnp.where(slot == owner, lengths, 0), axis=0, keepdims=True)
        code = jnp.where(position < live, start + position, -1)
        hots.append((code == wanted).astype(jnp.float32).astype(jnp.bfloat16))
    copy.wait()
    for m in range(2):
        total = None
        for k in range(dp):
            values = parts[m * dp + k][0:reqs]
            values = values.reshape(-1, values.shape[-1])
            found = jnp.dot(hots[k], values, preferred_element_type=jnp.float32)
            total = found if total is None else total + found
        out[m] = total.astype(out.dtype)

    count = dp * reqs
    down = lax.broadcasted_iota(jnp.int32, (reqs, count), 0)
    along = lax.broadcasted_iota(jnp.int32, (1, count), 1)
    here_slot = lax.rem(along, reqs)
    for k in range(dp):
        here_slot = jnp.where(lax.div(along, reqs) == k, here_slot + (me ^ k) * reqs, here_slot)
    slot = jnp.concatenate([down + (me ^ k) * reqs for k in range(dp)], axis=0)
    start = jnp.sum(jnp.where(slot < here_slot, lengths, 0), axis=0, keepdims=True)
    live = jnp.sum(jnp.where(slot == here_slot, lengths, 0), axis=0, keepdims=True)

    rank = me * rows + lax.broadcasted_iota(jnp.int32, (rows, count), 0)
    held = jnp.logical_and(rank >= start, rank < start + live)
    first = jnp.sum(jnp.where(held, start, 0), axis=1, keepdims=True)
    spot = rank[:, 0:1] - first
    held = held.astype(jnp.float32).astype(jnp.bfloat16)
    rows_of = jnp.dot(held, facts.astype(jnp.bfloat16), preferred_element_type=jnp.float32)
    lane = lax.broadcasted_iota(jnp.int32, rows_of.shape, 1)
    high = jnp.sum(jnp.where(lane == spot + 1, rows_of, 0.0), axis=1, keepdims=True)
    low = jnp.sum(jnp.where(lane == spot + 1 + slots, rows_of, 0.0), axis=1, keepdims=True)
    picks[...] = (high * 128.0 + low).astype(jnp.int32)

    mine = me * reqs + down
    begin = jnp.sum(jnp.where(here_slot < mine, live, 0), axis=1, keepdims=True)
    length = jnp.sum(jnp.where(here_slot == mine, live, 0), axis=1, keepdims=True)
    position = lax.broadcasted_iota(jnp.int32, (reqs, slots), 1)
    marks[...] = jnp.where(position < length, begin + position, -1)


def normalise(values, gain, chip, core, store, copy):
    half = len(values) // 2
    part = values[0].shape[1]
    width = part * len(values)
    values = [v.astype(jnp.float32) for v in values]
    center = sum(jnp.sum(v, axis=1, keepdims=True) for v in values) / width
    values = [v - center for v in values]
    spread = sum(jnp.sum(v * v, axis=1, keepdims=True) for v in values) / width
    scale = lax.rsqrt(spread + epsilon)
    copy.wait()
    for k, v in enumerate(values):
        place = 2 * (chip ^ (k % half)) + (core if k < half else 1 - core)
        store[place] = (v * scale * gain[place]).astype(jnp.bfloat16)
    return values[0]


def blocks_dot(normed, weight, order):
    part = normed.shape[2]
    total = None
    for b, place in enumerate(order):
        rows = weight[b * part : (b + 1) * part, :]
        piece = jnp.dot(normed[place], rows, preferred_element_type=jnp.float32)
        total = piece if total is None else total + piece
    return total


def ffn_kernel(half, ids, *refs):
    parts = refs[6 : 6 + 2 * half]
    keep, send, gains, ups, downs, normed, terms, sems = refs[6 + 2 * half :]
    copies = fetch(
        refs[:6], [store.at[m] for store in (gains, ups, downs) for m in range(2)], sems
    )
    chip, core = ids[1], ids[2]
    part = parts[0].shape[2]
    bases = [
        normalise([part[m] for part in parts], gains.at[m], chip, core, normed.at[m], copies[m])
        for m in range(2)
    ]
    for m in range(2):
        copies[2 + m].wait()
        pre = blocks_dot(normed.at[m], ups.at[m], range(2 * half))
        units = jax.nn.gelu(pre).astype(jnp.bfloat16)
        copies[4 + m].wait()
        full = jnp.dot(units, downs[m], preferred_element_type=jnp.float32)
        for b in range(2 * half):
            terms[m, b] = full[:, b * part : (b + 1) * part]
        for k in range(half):
            place = 2 * (chip ^ k)
            kept = terms[m, place + core]
            keep[k, m] = kept + bases[m] if k == 0 else kept
            send[k, m] = terms[m, place + 1 - core].astype(jnp.bfloat16)


def pair_kernel(ids, keep, came, own, *outs):
    own[...] = keep[0] + came[0].astype(jnp.float32)
    for k, out in enumerate(outs):
        out[...] = (keep[k + 1] + came[k + 1].astype(jnp.float32)).astype(jnp.bfloat16)


def score_kernel(half, dp, ids, *refs):
    parts = refs[2 : 2 + 2 * half]
    *outs, partial, tail, gains, normed, out_store, sems = refs[2 + 2 * half :]
    here = dp - 1
    copies = fetch(
        [refs[0], refs[1], outs[0], outs[here]],
        [store.at[m] for store in (gains, out_store) for m in range(2)],
        sems,
    )
    me, chip, core = ids[0], ids[1], ids[2]
    ratio = 2 * half // dp
    part = parts[0].shape[2]
    for m in range(2):
        values = [part[m] for part in parts]
        normalise(values, gains.at[m], chip, core, normed.at[m], copies[m])
        for b in range(ratio):
            tail[m, :, b * part : (b + 1) * part] = normed[m, (me ^ here) * ratio + b]
    for m in range(2):
        logits = None
        for k in [*range(1, here), 0]:
            if k == 0:
                copies[2 + m].wait()
                outs[m * here] = out_store.at[m]
            order = [(me ^ k) * ratio + b for b in range(ratio)]
            piece = blocks_dot(normed.at[m], outs[m * here + k], order)
            logits = piece if logits is None else logits + piece
        partial[m] = logits


def finish_kernel(ids, wanted, partial, tail, last_policy, last_reference, stats):
    lane = lax.broadcasted_iota(jnp.int32, (tail.shape[1], 128), 1)
    table = jnp.zeros(lane.shape, jnp.float32)
    for m, last in enumerate((last_policy, last_reference)):
        logits = partial[m] + jnp.dot(tail[m], last[...], preferred_element_type=jnp.float32)
        entries = lax.broadcasted_iota(jnp.int32, logits.shape, 1) + ids[3] * logits.shape[1]
        picked = jnp.sum(jnp.where(entries == wanted[...], logits, 0.0), axis=1, keepdims=True)
        top = jnp.max(logits, axis=1, keepdims=True)
        total = jnp.sum(jnp.exp(logits - top), axis=1, keepdims=True)
        table = jnp.where(lane == m, top, table)
        table = jnp.where(lane == 2 + m, total, table)
        table = jnp.where(lane == 4 + m, picked, table)
    stats[...] = jnp.transpose(table)[:8]


def merge(tables):
    top = functools.reduce(jnp.maximum, [t[0:2] for t in tables])
    total = sum(t[2:4] * jnp.exp(t[0:2] - top) for t in tables)
    return top, total, sum(t[4:6] for t in tables)


def merge_kernel(ids, *refs):
    out = refs[-1]
    out[0:2], out[2:4], out[4:6] = merge(refs[:-1])
    out[6:8] = jnp.zeros((2, out.shape[1]), jnp.float32)


def last_kernel(ids, *refs):
    out = refs[-1]
    top, total, picked = merge(refs[:-1])
    logprob = picked - (top + jnp.log(total))
    out[...] = logprob[0:1] - logprob[1:2]


def local(
    hidden_policy,
    hidden_reference,
    ffn_gain_policy,
    ffn_gain_reference,
    up_policy,
    up_reference,
    down_policy,
    down_reference,
    final_gain_policy,
    final_gain_reference,
    out_policy,
    out_reference,
    move_plan,
    lengths,
    targets,
):
    dp = lax.axis_size("dp")
    mp = lax.axis_size("mp")
    half = mp // 2
    dp_index = lax.axis_index("dp")
    mp_index = lax.axis_index("mp")
    ids = jnp.stack([dp_index, mp_index // 2, mp_index % 2, mp_index]).astype(jnp.int32)
    reqs, slots, part = hidden_policy.shape
    here = reqs * slots
    rows = here // 2
    ffn_gains = (ffn_gain_policy, ffn_gain_reference)
    final_gains = (final_gain_policy, final_gain_reference)
    gains = [gain.reshape(mp, 1, part) for gain in (*ffn_gains, *final_gains)]
    bits = [1 << b for b in range(dp.bit_length() - 1)]

    bit_orders = []
    for m in range(2):
        bit_orders.append([bits[(b ^ m) if (b ^ m) < len(bits) else b] for b in range(len(bits))])

    def spread_step(blocks, step, places):
        for m in range(2):
            bit = bit_orders[m][step]
            for k in [k for k in blocks[m] if places(m, k)]:
                blocks[m][k ^ bit] = exchange(blocks[m][k], "dp", bit)

    packed = call(
        pack_kernel,
        jax.ShapeDtypeStruct((reqs + 1, slots, part), jnp.bfloat16),
        (lengths, targets, hidden_reference),
        [
            pltpu.SMEM(lengths.shape, jnp.int32),
            pltpu.VMEM(targets.shape, jnp.int32),
            pltpu.SemaphoreType.DMA((3,)),
        ],
        far=(0, 1, 2),
    )
    hiddens = [{0: hidden_policy}, {0: packed}]
    outs = [{0: out_policy}, {0: out_reference}]

    def wait_for(first, places):
        flat = [(m, k) for m in range(2) for k in outs[m] if places(m, k)]
        first, values = lax.optimization_barrier((first, [outs[m][k] for m, k in flat]))
        for (m, k), value in zip(flat, values):
            outs[m][k] = value
        return first

    for step in range(len(bits)):
        spread_step(hiddens, step, lambda m, k: k == 0)
        if step:
            blocks, place = hiddens[0], bit_orders[0][step]
            passed = [k for k in blocks if 0 < k and not k & place]
            values = [blocks[k] for k in passed]
            blocks[place], values = lax.optimization_barrier((blocks[place], values))
            blocks.update(zip(passed, values))
        spread_step(hiddens, step, lambda m, k: 0 < k and not k & bit_orders[m][step])
    early = [(m, b) for m in range(2) for b in bits]
    values = wait_for([hiddens[m][b] for m, b in early], lambda m, k: True)
    for (m, b), value in zip(early, values):
        hiddens[m][b] = value
    spread_step(outs, 0, lambda m, k: True)
    hidden_parts = [hiddens[m][k] for m in range(2) for k in range(dp)]

    moved, wanted, marks = call(
        functools.partial(select_kernel, dp),
        (
            jax.ShapeDtypeStruct((2, rows, part), jnp.bfloat16),
            jax.ShapeDtypeStruct((rows, 1), jnp.int32),
            jax.ShapeDtypeStruct((reqs, slots), jnp.int32),
        ),
        (ids, move_plan, *hidden_parts),
        [
            pltpu.VMEM(hidden_policy.shape, jnp.bfloat16),
            pltpu.SMEM(move_plan.shape, jnp.int32),
            pltpu.SemaphoreType.DMA((2,)),
        ],
        far=(1, 2),
        cost=10000000000,
    )

    far = sorted(range(1, half), key=lambda k: (k.bit_length() <= 1, k))

    def gather_pair(own):
        same = {0: own}
        for k in far:
            same[k] = exchange(own, "mp", 2 * k)
        *passed, beside = lax.optimization_barrier(
            [same[k] for k in far] + [exchange(own, "mp", 1)]
        )
        same.update(zip(far, passed))
        same = [same[k] for k in range(half)]
        return same + [beside] + [exchange(v, "mp", 1) for v in same[1:]]

    parts = gather_pair(moved)
    if len(bits) > 1:
        parts[-1] = wait_for(parts[-1], lambda m, k: k == 0)
        later = [{0: outs[m][0]} for m in range(2)]
        spread_step(later, 1, lambda m, k: True)
    gain_scratch = pltpu.VMEM((2, mp, 1, part), jnp.float32)
    block = jax.ShapeDtypeStruct((2, rows, part), jnp.bfloat16)
    keep, send = call(
        functools.partial(ffn_kernel, half),
        (
            jax.ShapeDtypeStruct((half, 2, rows, part), jnp.float32),
            jax.ShapeDtypeStruct((half, 2, rows, part), jnp.bfloat16),
        ),
        (ids, *gains[:2], up_policy, up_reference, down_policy, down_reference, *parts),
        [
            gain_scratch,
            pltpu.VMEM((2,) + up_policy.shape, jnp.bfloat16),
            pltpu.VMEM((2,) + down_policy.shape, jnp.bfloat16),
            pltpu.VMEM((2, mp, rows, part), jnp.bfloat16),
            pltpu.VMEM((2, mp, rows, part), jnp.float32),
            pltpu.SemaphoreType.DMA((6,)),
        ],
        far=range(1, 7),
        mib=22,
    )
    send = wait_for(send, lambda m, k: k > 0)
    came = exchange(send, "mp", 1)
    own, *pieces = call(
        pair_kernel,
        (jax.ShapeDtypeStruct((2, rows, part), jnp.float32),) + (block,) * (half - 1),
        (ids, keep, came),
    )
    arrived = {k: exchange(pieces[k - 1], "mp", 2 * k) for k in far}
    if len(bits) > 1:
        for m in range(2):
            outs[m].update(later[m])
        passed = wait_for([arrived[k] for k in far], lambda m, k: True)
        arrived = dict(zip(far, passed))
        spread_step(outs, 1, lambda m, k: k == bit_orders[m][0])
    for k in range(1, half):
        own = own + arrived[k].astype(jnp.float32)
    stream = own.astype(jnp.bfloat16)
    for step in range(2, len(bits)):
        stream = wait_for(stream, lambda m, k: True)
        spread_step(outs, step, lambda m, k: True)

    partial, tail = call(
        functools.partial(score_kernel, half, dp),
        (
            jax.ShapeDtypeStruct((2, rows, out_policy.shape[1]), jnp.float32),
            jax.ShapeDtypeStruct((2, rows, out_policy.shape[0]), jnp.bfloat16),
        ),
        (
            ids,
            *gains[2:],
            *gather_pair(stream),
            *[outs[m][k] for m in range(2) for k in range(dp - 1)],
        ),
        [
            gain_scratch,
            pltpu.VMEM((2, mp, rows, part), jnp.bfloat16),
            pltpu.VMEM((2,) + out_policy.shape, jnp.bfloat16),
            pltpu.SemaphoreType.DMA((4,)),
        ],
        far=(1, 2, 3 + mp, 2 + mp + dp),
        mib=14,
    )
    stats = call(
        finish_kernel,
        jax.ShapeDtypeStruct((8, rows), jnp.float32),
        (ids, wanted, partial, tail, outs[0][dp - 1], outs[1][dp - 1]),
        mib=8,
    )
    stats = call(
        merge_kernel,
        jax.ShapeDtypeStruct((8, rows), jnp.float32),
        (ids, stats, exchange(stats, "mp", 1)),
    )
    diff = call(
        last_kernel,
        jax.ShapeDtypeStruct((1, rows), jnp.float32),
        (ids, stats, *[exchange(stats, "mp", 2 * k) for k in range(half - 1, 0, -1)]),
    )
    came = [exchange(diff, "dp", k) for k in range(dp - 1, 0, -1)]
    places = jnp.arange(dp, dtype=jnp.int32)[::-1] ^ dp_index
    ranks = places[:, None] * rows + jnp.arange(rows, dtype=jnp.int32)
    values = jnp.concatenate(came + [diff])
    hit = marks[:, :, None, None] == ranks
    token_diff = jnp.sum(jnp.where(hit, values, 0.0), axis=(2, 3))
    return (token_diff, jnp.sum(token_diff, axis=1))


def solution(mesh):
    return jax.shard_map(
        local,
        mesh=mesh,
        in_specs=(
            P("dp", None, "mp"),
            P("dp", None, "mp"),
            P(),
            P(),
            P(None, "mp"),
            P(None, "mp"),
            P("mp", None),
            P("mp", None),
            P(),
            P(),
            P("dp", "mp"),
            P("dp", "mp"),
            P(),
            P("dp"),
            P("dp", None),
        ),
        out_specs=(P("dp", None), P("dp")),
        check_vma=False,
    )
```

```python
import functools

import jax
import jax.numpy as jnp
from jax import lax
from jax.experimental import pallas as pl
from jax.experimental.pallas import tpu as pltpu
from jax.sharding import PartitionSpec as P

epsilon = 1e-05
vmem = pl.BlockSpec(memory_space=pltpu.VMEM)
smem = pl.BlockSpec(memory_space=pltpu.SMEM)
anywhere = pl.BlockSpec(memory_space=pltpu.HBM)


def call(kernel, out_shape, ops, scratch=(), far=(), mib=4, cost=None):
    specs = [anywhere if i in far else vmem if i else smem for i in range(len(ops))]
    ops = [
        pltpu.with_memory_space_constraint(op, pltpu.HBM) if i in far else op
        for i, op in enumerate(ops)
    ]
    return pl.pallas_call(
        kernel,
        out_shape=out_shape,
        in_specs=specs,
        out_specs=jax.tree.map(lambda _: vmem, out_shape),
        scratch_shapes=list(scratch),
        cost_estimate=cost and pl.CostEstimate(flops=cost, bytes_accessed=0, transcendentals=0),
        compiler_params=pltpu.CompilerParams(vmem_limit_bytes=mib * 1024 * 1024),
    )(*ops)


def exchange(values, axis, flip):
    count = lax.axis_size(axis)
    return lax.ppermute(values, axis, [(i, i ^ flip) for i in range(count)])


def fetch(sources, targets, sems):
    copies = [
        pltpu.make_async_copy(source, target, sems.at[i])
        for i, (source, target) in enumerate(zip(sources, targets))
    ]
    for copy in copies:
        copy.start()
    return copies


def pack_kernel(lengths_far, targets_far, hidden, out, lengths, targets, sems):
    reqs = hidden.shape[0]
    copies = fetch(
        [lengths_far, targets_far, hidden], [lengths, targets, out.at[pl.ds(0, reqs)]], sems
    )
    copies[1].wait()
    slots, part = targets.shape[1], hidden.shape[2]
    row = lax.broadcasted_iota(jnp.int32, (slots, part), 0)
    lane = lax.broadcasted_iota(jnp.int32, (slots, part), 1)
    high = lax.shift_right_logical(targets[...], 7)
    low = targets[...] - high * 128
    block = jnp.zeros((reqs, part), jnp.float32)
    for first, values in ((1, high), (1 + slots, low)):
        spot = (lane == row + first).astype(jnp.float32).astype(jnp.bfloat16)
        values = values.astype(jnp.float32).astype(jnp.bfloat16)
        block = block + jnp.dot(values, spot, preferred_element_type=jnp.float32)
    row = lax.broadcasted_iota(jnp.int32, (reqs, part), 0)
    lane = lax.broadcasted_iota(jnp.int32, (reqs, part), 1)
    copies[0].wait()
    for r in range(reqs):
        here = jnp.logical_and(row == r, lane == 0)
        block = jnp.where(here, lengths[r].astype(jnp.float32), block)
    out[reqs] = block.astype(jnp.bfloat16)
    copies[2].wait()


def select_kernel(dp, ids, plan_far, *refs):
    parts, (out, picks, marks, own, plan, sems) = list(refs[: 2 * dp]), refs[2 * dp :]
    plan_copy, copy = fetch([plan_far, parts[0]], [plan, own], sems)
    parts[0] = own
    rows = out.shape[1]
    reqs, slots, _ = own.shape
    here = reqs * slots
    me = ids[0]
    facts = jnp.concatenate([parts[dp + k][reqs].astype(jnp.float32) for k in range(dp)], axis=0)
    lengths = facts[:, 0:1].astype(jnp.int32)
    row = lax.broadcasted_iota(jnp.int32, (reqs, here), 0)
    slot = jnp.concatenate([row + (me ^ k) * reqs for k in range(dp)], axis=0)
    position = lax.rem(lax.broadcasted_iota(jnp.int32, (1, here), 1), slots)
    wanted = me * rows + lax.broadcasted_iota(jnp.int32, (rows, here), 0)
    request = lax.div(lax.broadcasted_iota(jnp.int32, (1, here), 1), slots)
    hots = []
    plan_copy.wait()
    for k in range(dp):
        owner = jnp.zeros((1, here), jnp.int32)
        for r in range(reqs):
            owner = jnp.where(request == r, plan[(me ^ k) * reqs + r], owner)
        start = jnp.sum(jnp.where(slot < owner, lengths, 0), axis=0, keepdims=True)
        live = jnp.sum(jnp.where(slot == owner, lengths, 0), axis=0, keepdims=True)
        code = jnp.where(position < live, start + position, -1)
        hots.append((code == wanted).astype(jnp.float32).astype(jnp.bfloat16))
    copy.wait()
    for m in range(2):
        total = None
        for k in range(dp):
            values = parts[m * dp + k][0:reqs]
            values = values.reshape(-1, values.shape[-1])
            found = jnp.dot(hots[k], values, preferred_element_type=jnp.float32)
            total = found if total is None else total + found
        out[m] = total.astype(out.dtype)

    count = dp * reqs
    down = lax.broadcasted_iota(jnp.int32, (reqs, count), 0)
    along = lax.broadcasted_iota(jnp.int32, (1, count), 1)
    here_slot = lax.rem(along, reqs)
    for k in range(dp):
        here_slot = jnp.where(lax.div(along, reqs) == k, here_slot + (me ^ k) * reqs, here_slot)
    slot = jnp.concatenate([down + (me ^ k) * reqs for k in range(dp)], axis=0)
    start = jnp.sum(jnp.where(slot < here_slot, lengths, 0), axis=0, keepdims=True)
    live = jnp.sum(jnp.where(slot == here_slot, lengths, 0), axis=0, keepdims=True)

    rank = me * rows + lax.broadcasted_iota(jnp.int32, (rows, count), 0)
    held = jnp.logical_and(rank >= start, rank < start + live)
    first = jnp.sum(jnp.where(held, start, 0), axis=1, keepdims=True)
    spot = rank[:, 0:1] - first
    held = held.astype(jnp.float32).astype(jnp.bfloat16)
    rows_of = jnp.dot(held, facts.astype(jnp.bfloat16), preferred_element_type=jnp.float32)
    lane = lax.broadcasted_iota(jnp.int32, rows_of.shape, 1)
    high = jnp.sum(jnp.where(lane == spot + 1, rows_of, 0.0), axis=1, keepdims=True)
    low = jnp.sum(jnp.where(lane == spot + 1 + slots, rows_of, 0.0), axis=1, keepdims=True)
    picks[...] = (high * 128.0 + low).astype(jnp.int32)

    mine = me * reqs + down
    begin = jnp.sum(jnp.where(here_slot < mine, live, 0), axis=1, keepdims=True)
    length = jnp.sum(jnp.where(here_slot == mine, live, 0), axis=1, keepdims=True)
    position = lax.broadcasted_iota(jnp.int32, (reqs, slots), 1)
    marks[...] = jnp.where(position < length, begin + position, -1)


def normalise(values, gain, chip, core, store, copy):
    half = len(values) // 2
    part = values[0].shape[1]
    width = part * len(values)
    values = [v.astype(jnp.float32) for v in values]
    center = sum(jnp.sum(v, axis=1, keepdims=True) for v in values) / width
    values = [v - center for v in values]
    spread = sum(jnp.sum(v * v, axis=1, keepdims=True) for v in values) / width
    scale = lax.rsqrt(spread + epsilon)
    copy.wait()
    for k, v in enumerate(values):
        place = 2 * (chip ^ (k % half)) + (core if k < half else 1 - core)
        store[place] = (v * scale * gain[place]).astype(jnp.bfloat16)
    return values[0]


def blocks_dot(normed, weight, order):
    part = normed.shape[2]
    total = None
    for b, place in enumerate(order):
        rows = weight[b * part : (b + 1) * part, :]
        piece = jnp.dot(normed[place], rows, preferred_element_type=jnp.float32)
        total = piece if total is None else total + piece
    return total


def ffn_kernel(half, ids, *refs):
    parts = refs[6 : 6 + 2 * half]
    keep, send, gains, ups, downs, normed, terms, sems = refs[6 + 2 * half :]
    copies = fetch(
        refs[:6], [store.at[m] for store in (gains, ups, downs) for m in range(2)], sems
    )
    chip, core = ids[1], ids[2]
    part = parts[0].shape[2]
    bases = [
        normalise([part[m] for part in parts], gains.at[m], chip, core, normed.at[m], copies[m])
        for m in range(2)
    ]
    for m in range(2):
        copies[2 + m].wait()
        pre = blocks_dot(normed.at[m], ups.at[m], range(2 * half))
        units = jax.nn.gelu(pre).astype(jnp.bfloat16)
        copies[4 + m].wait()
        full = jnp.dot(units, downs[m], preferred_element_type=jnp.float32)
        for b in range(2 * half):
            terms[m, b] = full[:, b * part : (b + 1) * part]
        for k in range(half):
            place = 2 * (chip ^ k)
            kept = terms[m, place + core]
            keep[k, m] = kept + bases[m] if k == 0 else kept
            send[k, m] = terms[m, place + 1 - core].astype(jnp.bfloat16)


def pair_kernel(ids, keep, came, own, *outs):
    own[...] = keep[0] + came[0].astype(jnp.float32)
    for k, out in enumerate(outs):
        out[...] = (keep[k + 1] + came[k + 1].astype(jnp.float32)).astype(jnp.bfloat16)


def score_kernel(half, dp, ids, *refs):
    parts = refs[2 : 2 + 2 * half]
    *outs, partial, tail, gains, normed, out_store, sems = refs[2 + 2 * half :]
    here = dp - 1
    copies = fetch(
        [refs[0], refs[1], outs[0], outs[here]],
        [store.at[m] for store in (gains, out_store) for m in range(2)],
        sems,
    )
    me, chip, core = ids[0], ids[1], ids[2]
    ratio = 2 * half // dp
    part = parts[0].shape[2]
    for m in range(2):
        values = [part[m] for part in parts]
        normalise(values, gains.at[m], chip, core, normed.at[m], copies[m])
        for b in range(ratio):
            tail[m, :, b * part : (b + 1) * part] = normed[m, (me ^ here) * ratio + b]
    for m in range(2):
        logits = None
        for k in [*range(1, here), 0]:
            if k == 0:
                copies[2 + m].wait()
                outs[m * here] = out_store.at[m]
            order = [(me ^ k) * ratio + b for b in range(ratio)]
            piece = blocks_dot(normed.at[m], outs[m * here + k], order)
            logits = piece if logits is None else logits + piece
        partial[m] = logits


def finish_kernel(ids, wanted, partial, tail, last_policy, last_reference, stats):
    lane = lax.broadcasted_iota(jnp.int32, (tail.shape[1], 128), 1)
    table = jnp.zeros(lane.shape, jnp.float32)
    for m, last in enumerate((last_policy, last_reference)):
        logits = partial[m] + jnp.dot(tail[m], last[...], preferred_element_type=jnp.float32)
        entries = lax.broadcasted_iota(jnp.int32, logits.shape, 1) + ids[3] * logits.shape[1]
        picked = jnp.sum(jnp.where(entries == wanted[...], logits, 0.0), axis=1, keepdims=True)
        top = jnp.max(logits, axis=1, keepdims=True)
        total = jnp.sum(jnp.exp(logits - top), axis=1, keepdims=True)
        table = jnp.where(lane == m, top, table)
        table = jnp.where(lane == 2 + m, total, table)
        table = jnp.where(lane == 4 + m, picked, table)
    stats[...] = jnp.transpose(table)[:8]


def merge(tables):
    top = functools.reduce(jnp.maximum, [t[0:2] for t in tables])
    total = sum(t[2:4] * jnp.exp(t[0:2] - top) for t in tables)
    return top, total, sum(t[4:6] for t in tables)


def merge_kernel(ids, *refs):
    out = refs[-1]
    out[0:2], out[2:4], out[4:6] = merge(refs[:-1])
    out[6:8] = jnp.zeros((2, out.shape[1]), jnp.float32)


def last_kernel(ids, *refs):
    out = refs[-1]
    top, total, picked = merge(refs[:-1])
    logprob = picked - (top + jnp.log(total))
    out[...] = logprob[0:1] - logprob[1:2]


def local(
    hidden_policy,
    hidden_reference,
    ffn_gain_policy,
    ffn_gain_reference,
    up_policy,
    up_reference,
    down_policy,
    down_reference,
    final_gain_policy,
    final_gain_reference,
    out_policy,
    out_reference,
    move_plan,
    lengths,
    targets,
):
    dp = lax.axis_size("dp")
    mp = lax.axis_size("mp")
    half = mp // 2
    dp_index = lax.axis_index("dp")
    mp_index = lax.axis_index("mp")
    ids = jnp.stack([dp_index, mp_index // 2, mp_index % 2, mp_index]).astype(jnp.int32)
    reqs, slots, part = hidden_policy.shape
    here = reqs * slots
    rows = here // 2
    ffn_gains = (ffn_gain_policy, ffn_gain_reference)
    final_gains = (final_gain_policy, final_gain_reference)
    gains = [gain.reshape(mp, 1, part) for gain in (*ffn_gains, *final_gains)]
    bits = [1 << b for b in range(dp.bit_length() - 1)]

    bit_orders = []
    for m in range(2):
        bit_orders.append([bits[(b ^ m) if (b ^ m) < len(bits) else b] for b in range(len(bits))])

    def spread_step(blocks, step, places):
        for m in range(2):
            bit = bit_orders[m][step]
            for k in [k for k in blocks[m] if places(m, k)]:
                blocks[m][k ^ bit] = exchange(blocks[m][k], "dp", bit)

    packed = call(
        pack_kernel,
        jax.ShapeDtypeStruct((reqs + 1, slots, part), jnp.bfloat16),
        (lengths, targets, hidden_reference),
        [
            pltpu.SMEM(lengths.shape, jnp.int32),
            pltpu.VMEM(targets.shape, jnp.int32),
            pltpu.SemaphoreType.DMA((3,)),
        ],
        far=(0, 1, 2),
    )
    hiddens = [{0: hidden_policy}, {0: packed}]
    outs = [{0: out_policy}, {0: out_reference}]

    def wait_for(first, places):
        flat = [(m, k) for m in range(2) for k in outs[m] if places(m, k)]
        first, values = lax.optimization_barrier((first, [outs[m][k] for m, k in flat]))
        for (m, k), value in zip(flat, values):
            outs[m][k] = value
        return first

    for step in range(len(bits)):
        spread_step(hiddens, step, lambda m, k: k == 0)
        if step:
            blocks, place = hiddens[0], bit_orders[0][step]
            passed = [k for k in blocks if 0 < k and not k & place]
            values = [blocks[k] for k in passed]
            blocks[place], values = lax.optimization_barrier((blocks[place], values))
            blocks.update(zip(passed, values))
        spread_step(hiddens, step, lambda m, k: 0 < k and not k & bit_orders[m][step])
    early = [(0, b) for b in bits] + [(1, bit_orders[1][0])]
    values = wait_for([hiddens[m][b] for m, b in early], lambda m, k: True)
    for (m, b), value in zip(early, values):
        hiddens[m][b] = value
    spread_step(outs, 0, lambda m, k: True)
    hidden_parts = [hiddens[m][k] for m in range(2) for k in range(dp)]

    moved, wanted, marks = call(
        functools.partial(select_kernel, dp),
        (
            jax.ShapeDtypeStruct((2, rows, part), jnp.bfloat16),
            jax.ShapeDtypeStruct((rows, 1), jnp.int32),
            jax.ShapeDtypeStruct((reqs, slots), jnp.int32),
        ),
        (ids, move_plan, *hidden_parts),
        [
            pltpu.VMEM(hidden_policy.shape, jnp.bfloat16),
            pltpu.SMEM(move_plan.shape, jnp.int32),
            pltpu.SemaphoreType.DMA((2,)),
        ],
        far=(1, 2),
        cost=10000000000,
    )

    far = sorted(range(1, half), key=lambda k: (k.bit_length() <= 1, k))

    def gather_pair(own):
        same = {0: own}
        for k in far:
            same[k] = exchange(own, "mp", 2 * k)
        *passed, beside = lax.optimization_barrier(
            [same[k] for k in far] + [exchange(own, "mp", 1)]
        )
        same.update(zip(far, passed))
        same = [same[k] for k in range(half)]
        return same + [beside] + [exchange(v, "mp", 1) for v in same[1:]]

    parts = gather_pair(moved)
    if len(bits) > 1:
        parts[-1] = wait_for(parts[-1], lambda m, k: k == 0)
        later = [{0: outs[m][0]} for m in range(2)]
        spread_step(later, 1, lambda m, k: True)
    gain_scratch = pltpu.VMEM((2, mp, 1, part), jnp.float32)
    block = jax.ShapeDtypeStruct((2, rows, part), jnp.bfloat16)
    keep, send = call(
        functools.partial(ffn_kernel, half),
        (
            jax.ShapeDtypeStruct((half, 2, rows, part), jnp.float32),
            jax.ShapeDtypeStruct((half, 2, rows, part), jnp.bfloat16),
        ),
        (ids, *gains[:2], up_policy, up_reference, down_policy, down_reference, *parts),
        [
            gain_scratch,
            pltpu.VMEM((2,) + up_policy.shape, jnp.bfloat16),
            pltpu.VMEM((2,) + down_policy.shape, jnp.bfloat16),
            pltpu.VMEM((2, mp, rows, part), jnp.bfloat16),
            pltpu.VMEM((2, mp, rows, part), jnp.float32),
            pltpu.SemaphoreType.DMA((6,)),
        ],
        far=range(1, 7),
        mib=22,
    )
    send = wait_for(send, lambda m, k: k > 0)
    came = exchange(send, "mp", 1)
    own, *pieces = call(
        pair_kernel,
        (jax.ShapeDtypeStruct((2, rows, part), jnp.float32),) + (block,) * (half - 1),
        (ids, keep, came),
    )
    arrived = {k: exchange(pieces[k - 1], "mp", 2 * k) for k in far}
    if len(bits) > 1:
        for m in range(2):
            outs[m].update(later[m])
        arrived = wait_for(arrived, lambda m, k: True)
        spread_step(outs, 1, lambda m, k: k == bit_orders[m][0])
    for k in range(1, half):
        own = own + arrived[k].astype(jnp.float32)
    stream = own.astype(jnp.bfloat16)
    for step in range(2, len(bits)):
        stream = wait_for(stream, lambda m, k: True)
        spread_step(outs, step, lambda m, k: True)

    partial, tail = call(
        functools.partial(score_kernel, half, dp),
        (
            jax.ShapeDtypeStruct((2, rows, out_policy.shape[1]), jnp.float32),
            jax.ShapeDtypeStruct((2, rows, out_policy.shape[0]), jnp.bfloat16),
        ),
        (
            ids,
            *gains[2:],
            *gather_pair(stream),
            *[outs[m][k] for m in range(2) for k in range(dp - 1)],
        ),
        [
            gain_scratch,
            pltpu.VMEM((2, mp, rows, part), jnp.bfloat16),
            pltpu.VMEM((2,) + out_policy.shape, jnp.bfloat16),
            pltpu.SemaphoreType.DMA((4,)),
        ],
        far=(1, 2, 3 + mp, 2 + mp + dp),
        mib=14,
    )
    stats = call(
        finish_kernel,
        jax.ShapeDtypeStruct((8, rows), jnp.float32),
        (ids, wanted, partial, tail, outs[0][dp - 1], outs[1][dp - 1]),
        mib=8,
    )
    stats = call(
        merge_kernel,
        jax.ShapeDtypeStruct((8, rows), jnp.float32),
        (ids, stats, exchange(stats, "mp", 1)),
    )
    diff = call(
        last_kernel,
        jax.ShapeDtypeStruct((1, rows), jnp.float32),
        (ids, stats, *[exchange(stats, "mp", 2 * k) for k in range(half - 1, 0, -1)]),
    )
    came = [exchange(diff, "dp", k) for k in range(dp - 1, 0, -1)]
    places = jnp.arange(dp, dtype=jnp.int32)[::-1] ^ dp_index
    ranks = places[:, None] * rows + jnp.arange(rows, dtype=jnp.int32)
    values = jnp.concatenate(came + [diff])
    hit = marks[:, :, None, None] == ranks
    token_diff = jnp.sum(jnp.where(hit, values, 0.0), axis=(2, 3))
    return (token_diff, jnp.sum(token_diff, axis=1))


def solution(mesh):
    return jax.shard_map(
        local,
        mesh=mesh,
        in_specs=(
            P("dp", None, "mp"),
            P("dp", None, "mp"),
            P(),
            P(),
            P(None, "mp"),
            P(None, "mp"),
            P("mp", None),
            P("mp", None),
            P(),
            P(),
            P("dp", "mp"),
            P("dp", "mp"),
            P(),
            P("dp"),
            P("dp", None),
        ),
        out_specs=(P("dp", None), P("dp")),
        check_vma=False,
    )
```
